32 devices in a mesh: req: 8 (over z, y), head: 4 (over x, core).
Axes of the slice: x: 2, y: 2, z: 4, core: 2. Of those that a mesh axis runs over, the one named last changes fastest.
Arguments:
- hidden: bfloat16 [64, 2048], P('req', 'head'), may hold values from -6 to 6
- attn_gain: float32 [2048], replicated, may hold values from 0.1 to 1.9
- q_weight: bfloat16 [2048, 2048], P(None, 'head'), may hold values from -0.125 to 0.125
- gate_weight: bfloat16 [2048, 2048], P(None, 'head'), may hold values from -0.125 to 0.125
- key_value_weight: bfloat16 [2048, 2048], P(None, 'head'), may hold values from -0.125 to 0.125
- q_gain: float32 [128], replicated, may hold values from 0.5 to 1.5
- k_gain: float32 [128], replicated, may hold values from 0.5 to 2
- out_weight: bfloat16 [2048, 2048], P('head'), may hold values from -0.5 to 0.5
- prompt_key_cache: bfloat16 [8, 4096, 8, 128], P('req', 'head'), may hold values from -3.5 to 3.5
- prompt_value_cache: bfloat16 [8, 4096, 8, 128], P('req', 'head'), may hold values from -6 to 6
- tail_key_cache: bfloat16 [8, 4, 256, 8, 128], P('req', None, 'head'), may hold values from -3.5 to 3.5
- tail_value_cache: bfloat16 [8, 4, 256, 8, 128], P('req', None, 'head'), may hold values from -6 to 6
- mlp_gain: float32 [2048], replicated, may hold values from 0.1 to 1.9
- mlp_gate: bfloat16 [2048, 6144], P('req', 'head'), may hold values from -0.125 to 0.125
- mlp_up: bfloat16 [2048, 6144], P('req', 'head'), may hold values from -0.125 to 0.125
- mlp_down: bfloat16 [6144, 2048], P('head'), may hold values from -0.109375 to 0.109375
- final_gain: float32 [2048], P('head'), may hold values from 0.1 to 1.9
- score_weight: float32 [2048], P('head'), may hold values from -0.125 to 0.125
- prompt_lengths: int32 [8], replicated, may hold values from 1 to 4096, 16384 in all
- tail_lengths: int32 [8, 4], replicated, may hold values from 1 to 256, 512 in all within a row
- group_prompt: int32 [8], replicated, may hold values from 0 to 7, each once
Outputs:
- new_hidden: bfloat16 [64, 2048], P('req', 'head')
- score: float32 [64], P('req')
The draws below stay inside these ranges and needn't reach their ends.
Inputs may be any that keep to these rules, and one draw needn't show every extreme that they name: `group_prompt`: every prompt is held by exactly one group. `prompt_lengths`: one prompt has exactly 4096 prefix tokens. `tail_lengths`: in every prompt one continuation has exactly 256 tail tokens.
All inputs are finite; a program needn't handle non-finite values.
Results may differ from the reference program's by a relative error of at most 0.023.
Values may be sent and summed in bfloat16 or wider, within the bound.
No kernel may reach another device: no remote copies, remote signals or barrier semaphores. Data moves between devices by JAX's collectives and lax.ppermute only.
A program may use at most 64 MiB of HBM per device.

```python
import math
import jax
import jax.numpy as jnp
import numpy as np
from jax import lax

MODEL_DIMENSION = 2048
QUERY_HEADS = 16
KEY_VALUE_HEADS = 8
HEAD_SIZE = 128
FF = 6144
PREFIX_SLOTS = 4096
TAIL_SLOTS = 256
CONTINUATION_COUNT = 4
NEW_TOKENS = 2
PROMPT_COUNT = 8
TOKENS = 64


def raised(values, key, source, target, blocks, factor):
    def block_of(axis_at):
        return (jnp.arange(values.shape[axis_at]) // (values.shape[axis_at] // blocks)).reshape((-1,) + (1,) * (values.ndim - 1 - axis_at))

    near = jax.random.permutation(key, blocks)[block_of(target)]
    second = (block_of(target) + blocks // 2) % blocks
    return jnp.where((block_of(source) == near) | (block_of(source) == second), factor * values, values)


def block_levels(rng, shape, split, smallest, largest):
    factor_of, own = 1.0, jax.random.fold_in(rng, 6)
    for dim, blocks in split:
        draws = jnp.exp(jax.random.uniform(jax.random.fold_in(own, dim), (blocks,), jnp.float32, smallest / len(split), largest / len(split)))
        factor_of = factor_of * jnp.repeat(draws, shape[dim] // blocks).reshape([-1 if axis == dim else 1 for axis in range(len(shape))])
    return factor_of


def profile(amount, total, most, skew):
    loads = [(1 << 20) // math.isqrt(rank ** skew) + 1 for rank in range(2, amount + 1)]
    surplus, holding = total - most - (amount - 1), [1] * (amount - 1)
    while surplus > 0:
        movable = [i for i in range(amount - 1) if holding[i] < most]
        pool, budget = sum([loads[i] for i in movable]), surplus
        for i in movable:
            more = min(most - holding[i], max(1, budget * loads[i] // pool), surplus)
            holding[i] = holding[i] + more
            surplus = surplus - more
    return np.array([most] + holding)


def ragged_sizes(rng, number_of, total, limit, skew):
    if number_of == 2:
        one = jax.random.randint(rng, (), max(1, total - limit), min(limit, total - 1) + 1)
        return jnp.stack([one, total - one])
    lengths = jnp.asarray(profile(number_of, total, limit, skew), jnp.int32)
    couples = (number_of - 1) // 2
    giver, sink = lengths[1:1 + 2 * couples:2], lengths[2:2 + 2 * couples:2]
    margin = jnp.minimum(giver - 1, limit - sink)
    moved = jax.random.randint(jax.random.fold_in(rng, 1), (couples,), 0, 1 << 20) % (margin + 1)
    lengths = lengths.at[1:1 + 2 * couples:2].set(giver - moved).at[2:2 + 2 * couples:2].set(sink + moved)
    return lengths[jax.random.permutation(jax.random.fold_in(rng, 2), number_of)]


def scatter_about(own_key, dims, width, limit, cuts=(), kind=jnp.bfloat16):
    array = width * jax.random.normal(own_key, dims, jnp.float32)
    if cuts:
        array = array * block_levels(own_key, dims, cuts, -0.22, 0.18)
    return jnp.clip(array, -limit, limit).astype(kind)


def noise_with(rng, extent, width, limit, shards, heavy, kind=jnp.bfloat16):
    values = width * jax.random.normal(rng, extent, jnp.float32)
    if shards:
        values = values * block_levels(rng, extent, shards, -0.22, 0.18)
    return jnp.clip(raised(values, jax.random.fold_in(rng, 3), *heavy), -limit, limit).astype(kind)


def setup_inputs(seed: int = 0) -> dict:
    key_of = jax.random.split(jax.random.key(seed), 22)
    return {
        "hidden": scatter_about(key_of[0], (TOKENS, MODEL_DIMENSION), 1.0, 6.0, ((0, 8), (1, 4))),
        "attn_gain": jnp.clip(1.0 + 0.18 * jax.random.normal(key_of[1], (MODEL_DIMENSION,), jnp.float32), 0.1, 1.9),
        "q_weight": scatter_about(key_of[2], (MODEL_DIMENSION, QUERY_HEADS * HEAD_SIZE), MODEL_DIMENSION ** -0.5, 0.125, ((1, 4),)),
        "gate_weight": scatter_about(key_of[3], (MODEL_DIMENSION, QUERY_HEADS * HEAD_SIZE), MODEL_DIMENSION ** -0.5, 0.125, ((1, 4),)),
        "key_value_weight": scatter_about(key_of[4], (MODEL_DIMENSION, 2 * KEY_VALUE_HEADS * HEAD_SIZE), MODEL_DIMENSION ** -0.5, 0.125, ((1, 4),)),
        "q_gain": jnp.clip(1.0 + 0.1 * jax.random.normal(key_of[5], (HEAD_SIZE,), jnp.float32), 0.5, 1.5),
        "k_gain": jnp.clip(jnp.exp(jax.random.uniform(key_of[6], (HEAD_SIZE,), jnp.float32, math.log(0.5), math.log(2.0))), 0.5, 2.0),
        "out_weight": scatter_about(key_of[7], (QUERY_HEADS * HEAD_SIZE, MODEL_DIMENSION), HEAD_SIZE ** -0.5, 0.5, ((0, 4),)),
        "prompt_key_cache": jnp.clip(jax.random.uniform(key_of[8], (PROMPT_COUNT, PREFIX_SLOTS, KEY_VALUE_HEADS, HEAD_SIZE), jnp.float32, -3.5, 3.5) * block_levels(key_of[8], (PROMPT_COUNT, PREFIX_SLOTS, KEY_VALUE_HEADS, HEAD_SIZE), ((0, 8), (1, 4)), -0.4, 0.0), -3.5, 3.5).astype(jnp.bfloat16),
        "prompt_value_cache": scatter_about(key_of[9], (PROMPT_COUNT, PREFIX_SLOTS, KEY_VALUE_HEADS, HEAD_SIZE), 1.0, 6.0, ((0, 8), (1, 4))),
        "tail_key_cache": jnp.clip(jax.random.uniform(key_of[10], (PROMPT_COUNT, CONTINUATION_COUNT, TAIL_SLOTS, KEY_VALUE_HEADS, HEAD_SIZE), jnp.float32, -3.5, 3.5) * block_levels(key_of[10], (PROMPT_COUNT, CONTINUATION_COUNT, TAIL_SLOTS, KEY_VALUE_HEADS, HEAD_SIZE), ((0, 8), (2, 4)), -0.4, 0.0), -3.5, 3.5).astype(jnp.bfloat16),
        "tail_value_cache": scatter_about(key_of[11], (PROMPT_COUNT, CONTINUATION_COUNT, TAIL_SLOTS, KEY_VALUE_HEADS, HEAD_SIZE), 1.0, 6.0, ((0, 8), (2, 4))),
        "mlp_gain": jnp.clip(1.0 + 0.18 * jax.random.normal(key_of[12], (MODEL_DIMENSION,), jnp.float32), 0.1, 1.9),
        "mlp_gate": scatter_about(key_of[13], (MODEL_DIMENSION, FF), MODEL_DIMENSION ** -0.5, 0.125, ((0, 8), (1, 4))),
        "mlp_up": scatter_about(key_of[14], (MODEL_DIMENSION, FF), MODEL_DIMENSION ** -0.5, 0.125, ((0, 8), (1, 4))),
        "mlp_down": noise_with(key_of[15], (FF, MODEL_DIMENSION), FF ** -0.5, 0.109375, ((0, 4),), (0, 1, 4, 2.0)),
        "final_gain": jnp.clip(1.0 + 0.18 * jax.random.normal(key_of[16], (MODEL_DIMENSION,), jnp.float32), 0.1, 1.9),
        "score_weight": scatter_about(key_of[17], (MODEL_DIMENSION,), MODEL_DIMENSION ** -0.5, 0.125, ((0, 4),), jnp.float32),
        "prompt_lengths": ragged_sizes(key_of[18], PROMPT_COUNT, PROMPT_COUNT * PREFIX_SLOTS // 2, PREFIX_SLOTS, 2).astype(jnp.int32),
        "tail_lengths": jax.vmap(lambda own: ragged_sizes(own, CONTINUATION_COUNT, CONTINUATION_COUNT * TAIL_SLOTS // 2, TAIL_SLOTS, 1))(jax.random.split(key_of[19], PROMPT_COUNT)).reshape((PROMPT_COUNT, CONTINUATION_COUNT)).astype(jnp.int32),
        "group_prompt": jax.random.permutation(key_of[20], PROMPT_COUNT).astype(jnp.int32),
    }


EPS = 1e-06
THETA = 1000000.0

def rms_scale(value, gain):
    return value * lax.rsqrt(lax.optimization_barrier(jnp.mean(value * value, axis=-1, keepdims=True)) + EPS) * gain

def rotate(value, position):
    head_width = value.shape[-1]
    half_width = head_width // 2
    frequency = jnp.exp(-math.log(THETA) * 2.0 * jnp.arange(half_width, dtype=jnp.float32) / head_width)
    angles = position.astype(jnp.float32)[:, None] * frequency[None, :]
    cosine = jnp.cos(angles)[:, None, :]
    sine_part = jnp.sin(angles)[:, None, :]
    first_half = value[..., :half_width]
    second_half = value[..., half_width:]
    return jnp.concatenate([first_half * cosine - second_half * sine_part, second_half * cosine + first_half * sine_part], axis=-1)

def rounded_values(value):
    return lax.optimization_barrier(value.astype(jnp.bfloat16)).astype(jnp.float32)

def reference(hidden, attn_gain, q_weight, gate_weight, key_value_weight, q_gain, k_gain, out_weight, prompt_key_cache, prompt_value_cache, tail_key_cache, tail_value_cache, mlp_gain, mlp_gate, mlp_up, mlp_down, final_gain, score_weight, prompt_lengths, tail_lengths, group_prompt):
    count_of_rows = CONTINUATION_COUNT * NEW_TOKENS
    sharing_count = QUERY_HEADS // KEY_VALUE_HEADS
    score_scale = 1.0 / math.sqrt(HEAD_SIZE)

    def one_group(group_id):
        prompt_id = group_prompt[group_id]
        prompt_len = prompt_lengths[prompt_id]
        tail_row = tail_lengths[prompt_id]
        position = (prompt_len + tail_row[:, None] + jnp.arange(NEW_TOKENS, dtype=jnp.int32)[None, :]).reshape(count_of_rows)
        block_rows = lax.dynamic_slice_in_dim(hidden, group_id * count_of_rows, count_of_rows, 0).astype(jnp.float32)
        normalized_hidden = rms_scale(block_rows, attn_gain).astype(jnp.bfloat16)
        gate_pre = jnp.dot(normalized_hidden, gate_weight, preferred_element_type=jnp.float32)
        query_rows = jnp.dot(normalized_hidden, q_weight, preferred_element_type=jnp.float32).reshape(count_of_rows, QUERY_HEADS, HEAD_SIZE)
        query_rows = rotate(rms_scale(query_rows, q_gain), position).astype(jnp.bfloat16)
        projected_rows = jnp.dot(normalized_hidden, key_value_weight, preferred_element_type=jnp.float32).reshape(count_of_rows, KEY_VALUE_HEADS, 2, HEAD_SIZE)
        incoming_keys = rotate(rms_scale(projected_rows[:, :, 0], k_gain), position).astype(jnp.bfloat16)
        incoming_values = projected_rows[:, :, 1].astype(jnp.bfloat16)
        query_groups = query_rows.astype(jnp.float32).reshape(count_of_rows, KEY_VALUE_HEADS, sharing_count, HEAD_SIZE)
        cache_keys = prompt_key_cache[group_id].astype(jnp.float32)
        cache_values = prompt_value_cache[group_id].astype(jnp.float32)
        scores = jnp.einsum('rkgd,tkd->rkgt', query_groups, cache_keys) * score_scale
        slot_live = jnp.arange(PREFIX_SLOTS, dtype=jnp.int32)[None, None, None, :] < prompt_len
        attention_weights = jnp.where(slot_live, jnp.exp(scores), 0.0)
        denominator = lax.optimization_barrier(jnp.sum(attention_weights, axis=-1))
        numerator = jnp.einsum('rkgt,tkd->rkgd', rounded_values(attention_weights), cache_values)
        continuation_rows = query_groups.reshape(CONTINUATION_COUNT, NEW_TOKENS, KEY_VALUE_HEADS, sharing_count, HEAD_SIZE)
        tkeys = tail_key_cache[group_id].astype(jnp.float32)
        tail_value_rows = tail_value_cache[group_id].astype(jnp.float32)
        scores = jnp.einsum('cjkgd,ctkd->cjkgt', continuation_rows, tkeys) * score_scale
        tail_live = jnp.arange(TAIL_SLOTS, dtype=jnp.int32)[None, :] < tail_row[:, None]
        attention_weights = jnp.where(tail_live[:, None, None, None, :], jnp.exp(scores), 0.0)
        denominator = denominator + lax.optimization_barrier(jnp.sum(attention_weights, axis=-1)).reshape(count_of_rows, KEY_VALUE_HEADS, sharing_count)
        numerator = numerator + jnp.einsum('ihbyw,iwbs->ihbys', rounded_values(attention_weights), tail_value_rows).reshape(count_of_rows, KEY_VALUE_HEADS, sharing_count, HEAD_SIZE)
        recent_key_rows = incoming_keys.astype(jnp.float32).reshape(CONTINUATION_COUNT, NEW_TOKENS, KEY_VALUE_HEADS, HEAD_SIZE)
        recent_value_rows = incoming_values.astype(jnp.float32).reshape(CONTINUATION_COUNT, NEW_TOKENS, KEY_VALUE_HEADS, HEAD_SIZE)
        scores = jnp.einsum('cjkgd,cukd->cjkgu', continuation_rows, recent_key_rows) * score_scale
        causal = jnp.arange(NEW_TOKENS, dtype=jnp.int32)[None, :] <= jnp.arange(NEW_TOKENS, dtype=jnp.int32)[:, None]
        attention_weights = jnp.where(causal[None, :, None, None, :], jnp.exp(scores), 0.0)
        denominator = denominator + lax.optimization_barrier(jnp.sum(attention_weights, axis=-1)).reshape(count_of_rows, KEY_VALUE_HEADS, sharing_count)
        numerator = numerator + jnp.einsum('bfmne,beml->bfmnl', rounded_values(attention_weights), recent_value_rows).reshape(count_of_rows, KEY_VALUE_HEADS, sharing_count, HEAD_SIZE)
        attention = (numerator / denominator[..., None]).reshape(count_of_rows, QUERY_HEADS * HEAD_SIZE)
        gated = (attention * jax.nn.sigmoid(gate_pre)).astype(jnp.bfloat16)
        return (block_rows + jnp.dot(gated, out_weight, preferred_element_type=jnp.float32)).astype(jnp.bfloat16)
    attended = lax.map(one_group, jnp.arange(PROMPT_COUNT, dtype=jnp.int32)).reshape(PROMPT_COUNT * count_of_rows, MODEL_DIMENSION)
    wide_rows = attended.astype(jnp.float32)
    mlp_in = rms_scale(wide_rows, mlp_gain).astype(jnp.bfloat16)
    gate_part = jnp.dot(mlp_in, mlp_gate, preferred_element_type=jnp.float32)
    up_part = jnp.dot(mlp_in, mlp_up, preferred_element_type=jnp.float32)
    act_rows = (jax.nn.silu(gate_part) * up_part).astype(jnp.bfloat16)
    result = (wide_rows + jnp.dot(act_rows, mlp_down, preferred_element_type=jnp.float32)).astype(jnp.bfloat16)
    owner_group = jnp.argsort(group_prompt).astype(jnp.int32)
    new_hidden = result.reshape(PROMPT_COUNT, count_of_rows, MODEL_DIMENSION)[owner_group].reshape(PROMPT_COUNT * count_of_rows, MODEL_DIMENSION)
    final_rows = new_hidden.astype(jnp.float32)
    score = lax.optimization_barrier(jnp.sum(final_rows * final_gain * score_weight, axis=-1)) * lax.rsqrt(lax.optimization_barrier(jnp.mean(final_rows * final_rows, axis=-1)) + EPS)
    return (new_hidden, score)
```

```python
import functools
import math

import jax
import jax.numpy as jnp
from jax import lax
from jax.experimental import pallas as pl
from jax.experimental.pallas import tpu as pltpu
from jax.sharding import PartitionSpec as P

EPS = 1e-06
THETA = 1000000.0
LANES = 128
BF16 = jnp.bfloat16
F32 = jnp.float32


def in_vmem(x):
    return pltpu.with_memory_space_constraint(x, pltpu.VMEM)


def whole(memory_space=pltpu.VMEM):
    return pl.BlockSpec(memory_space=memory_space)


def call(body, outs, specs, limit_mib, name, flops=0, read=0, outs_vmem=True):
    shapes = [
        pltpu.VMEM(shape, dtype) if outs_vmem else jax.ShapeDtypeStruct(shape, dtype)
        for shape, dtype in outs
    ]
    return pl.pallas_call(
        body,
        out_shape=shapes,
        in_specs=specs,
        out_specs=[whole()] * len(outs),
        compiler_params=pltpu.CompilerParams(vmem_limit_bytes=limit_mib << 20),
        cost_estimate=pl.CostEstimate(flops=flops, bytes_accessed=read, transcendentals=0),
        name=name,
    )


def group_facts(prompts_ref, tails_ref, owners_ref):
    group = lax.axis_index("req")
    prompt = owners_ref[group]
    return prompts_ref[prompt], prompt


def project_body(
    cont_count,
    rows_ref,
    gain_ref,
    q_ref,
    kv_ref,
    gate_ref,
    q_gain_ref,
    k_gain_ref,
    prompts_ref,
    tails_ref,
    owners_ref,
    sent_ref,
    gate_out_ref,
):
    count = rows_ref.shape[0]
    head_width = q_gain_ref.shape[1]
    new_count = count // cont_count
    prompt_len, prompt = group_facts(prompts_ref, tails_ref, owners_ref)
    row_of = lax.broadcasted_iota(jnp.int32, (count, head_width), 0)
    lane_of = lax.broadcasted_iota(jnp.int32, (count, head_width), 1)
    position = jnp.zeros((count, head_width), jnp.int32)
    for cont in range(cont_count):
        start = prompt_len + tails_ref[cont, prompt]
        position = jnp.where(row_of // new_count == cont, start + row_of % new_count, position)
    half = head_width // 2
    frequency = jnp.exp((-math.log(THETA) * 2.0 / head_width) * (lane_of % half).astype(F32))
    angles = position.astype(F32) * frequency
    cosine = jnp.cos(angles)
    sine = jnp.where(lane_of < half, -1.0, 1.0) * jnp.sin(angles)

    rows = rows_ref[...].astype(F32)
    scale = lax.rsqrt(jnp.mean(rows * rows, axis=-1, keepdims=True) + EPS)
    normed = (rows * scale * gain_ref[...]).astype(BF16)

    def keyed(block, gain):
        inverse = lax.rsqrt(jnp.mean(block * block, axis=-1, keepdims=True) + EPS)
        block = block * inverse * gain
        return block * cosine + pltpu.roll(block, half, 1) * sine

    queries = jnp.dot(normed, q_ref[...], preferred_element_type=F32)
    fresh = jnp.dot(normed, kv_ref[...], preferred_element_type=F32)
    block_count = kv_ref.shape[1] // head_width
    first_block = lax.axis_index("head") * block_count
    top, bottom = [], []
    for block in range(q_ref.shape[1] // head_width):
        top.append(
            keyed(queries[:, block * head_width : (block + 1) * head_width], q_gain_ref[...])
        )
    for block in range(block_count):
        plain = fresh[:, block * head_width : (block + 1) * head_width]
        is_key = (first_block + block) % 2 == 0
        bottom.append(jnp.where(is_key, keyed(plain, k_gain_ref[...]), plain))
    sent = jnp.concatenate(
        [jnp.concatenate(top, axis=1), jnp.concatenate(bottom, axis=1)], axis=0
    )
    sent_ref[...] = sent.astype(BF16)
    gate_out_ref[...] = jnp.dot(normed, gate_ref[...], preferred_element_type=F32)


def split_parts(value):
    high = value.astype(BF16).astype(F32)
    middle = (value - high).astype(BF16).astype(F32)
    low = value - high - middle
    return [high, middle, low]


def attend_body(
    cont_count,
    kv_heads,
    own_heads,
    got_ref,
    keys_ref,
    values_ref,
    tail_keys_ref,
    tail_values_ref,
    final_gain_ref,
    score_weight_ref,
    prompts_ref,
    tails_ref,
    owners_ref,
    out_ref,
):
    count = got_ref.shape[0] // 2
    width = keys_ref.shape[1]
    all_heads = got_ref.shape[1] // width
    sharing = all_heads // kv_heads
    new_count = count // cont_count
    head_place = lax.axis_index("head")
    prompt_len, prompt = group_facts(prompts_ref, tails_ref, owners_ref)
    got = got_ref[...].astype(F32)
    blocks = [got[:, i * width : (i + 1) * width] for i in range(all_heads)]
    queries = jnp.concatenate([b[:count] for b in blocks], axis=0).astype(BF16)
    fresh_keys = jnp.concatenate([blocks[2 * k][count:] for k in range(kv_heads)], axis=0)
    fresh_values = jnp.concatenate([blocks[2 * k + 1][count:] for k in range(kv_heads)], axis=0)
    many = all_heads * count
    score_scale = 1.0 / math.sqrt(width)
    ones = functools.partial(jnp.ones, dtype=BF16)

    def part(keys, values, live):
        scores = lax.dot_general(
            queries, keys, (((1,), (1,)), ((), ())), preferred_element_type=F32
        )
        weights = jnp.where(live, jnp.exp(scores * score_scale), 0.0).astype(BF16)
        with_ones = jnp.concatenate([values, ones(values.shape)], axis=1)
        return jnp.dot(weights, with_ones, preferred_element_type=F32)

    def places(span):
        row = lax.broadcasted_iota(jnp.int32, (many, span), 0)
        lane = lax.broadcasted_iota(jnp.int32, (many, span), 1)
        return row, lane

    total_rows = keys_ref.shape[0]
    step = min(1024, total_rows)
    row, lane = places(step)
    matching = lane % kv_heads == row // (count * sharing)
    left = (prompt_len - head_place * (total_rows // kv_heads)) * kv_heads
    numer = jnp.zeros((many, 2 * width), F32)
    for start in range(0, total_rows, step):
        live = matching & (lane < left - start)
        numer += part(keys_ref[start : start + step, :], values_ref[start : start + step, :], live)

    tail_rows = tail_keys_ref.shape[0] // cont_count
    row, lane = places(tail_rows)
    matching = lane % kv_heads == row // (count * sharing)
    for cont in range(cont_count):
        left = (tails_ref[cont, prompt] - head_place * (tail_rows // kv_heads)) * kv_heads
        live = matching & (lane < left) & ((row % count) // new_count == cont)
        start = cont * tail_rows
        numer += part(
            tail_keys_ref[start : start + tail_rows, :],
            tail_values_ref[start : start + tail_rows, :],
            live,
        )

    row, lane = places(count * kv_heads)
    live = (
        (lane // count == row // (count * sharing))
        & ((lane % count) // new_count == (row % count) // new_count)
        & (lane % new_count <= row % new_count)
        & (head_place == 0)
    )
    numer += part(fresh_keys.astype(BF16), fresh_values.astype(BF16), live)

    product = final_gain_ref[...] * score_weight_ref[...]
    pieces = [
        p[:, i * LANES : (i + 1) * LANES]
        for p in split_parts(product)
        for i in range(product.shape[1] // LANES)
    ]
    own_rows = own_heads * count
    filler = jnp.zeros((own_rows - len(pieces), LANES), F32)
    extra = jnp.concatenate(pieces + [filler], axis=0)
    for place in range(all_heads // own_heads):
        mine = numer[place * own_rows : (place + 1) * own_rows, :]
        out_ref[place] = jnp.concatenate([mine, extra], axis=1).astype(BF16)


def mix_body(got_ref, gate_ref, rows_ref, weight_ref, out_ref):
    sources, own_rows, _ = got_ref.shape
    count = rows_ref.shape[0]
    width = LANES
    summed = got_ref[0, :, : 2 * width].astype(F32)
    for source in range(1, sources):
        summed += got_ref[source, :, : 2 * width].astype(F32)
    attention = summed[:, :width] / summed[:, width:]
    side_by_side = jnp.concatenate(
        [attention[i : i + count] for i in range(0, own_rows, count)], axis=1
    )
    gated = (side_by_side * jax.nn.sigmoid(gate_ref[...])).astype(BF16)
    mixed = jnp.dot(gated, weight_ref[...], preferred_element_type=F32)
    mixed += rows_ref[...].astype(F32) * (1.0 / sources)
    mixed = mixed.astype(BF16)
    places, copies, _, block = out_ref.shape
    for place in range(places):
        piece = mixed[:, place * block : (place + 1) * block]
        for copy in range(copies):
            out_ref[place, copy] = piece


def expand_body(got_ref, gain_ref, gate_ref, up_ref, owners_ref, out_ref):
    groups, sources, count, block = got_ref.shape
    summed = got_ref[:, 0].astype(F32)
    for source in range(1, sources):
        summed += got_ref[:, source].astype(F32)
    attended = summed.reshape(groups * count, block).astype(BF16).astype(F32)
    scaled = (attended * gain_ref[lax.axis_index("req")]).astype(BF16)
    gate = jnp.dot(scaled, gate_ref[...], preferred_element_type=F32)
    up = jnp.dot(scaled, up_ref[...], preferred_element_type=F32)
    sent = jnp.concatenate([gate, up, attended], axis=1).astype(BF16)
    sent = sent.reshape(groups, count, sent.shape[1])
    for group in range(groups):
        out_ref[owners_ref[group]] = sent[group]


def reduce_body(sources, got_ref, weight_ref, out_ref):
    blocks, count, width = got_ref.shape
    hidden_units = weight_ref.shape[0]
    total = got_ref[0, :, : 2 * hidden_units].astype(F32)
    for block in range(1, blocks):
        total += got_ref[block, :, : 2 * hidden_units].astype(F32)
    attended = jnp.concatenate(
        [got_ref[block, :, 2 * hidden_units :].astype(F32) for block in range(blocks)], axis=1
    )
    scale = lax.rsqrt(jnp.mean(attended * attended, axis=-1, keepdims=True) + EPS)
    gate = total[:, :hidden_units] * scale
    up = total[:, hidden_units:] * scale
    act = (gate * jax.nn.sigmoid(gate) * up).astype(BF16)
    down = jnp.dot(act, weight_ref[...], preferred_element_type=F32)
    out_ref[...] = (down + attended * (1.0 / sources)).astype(BF16)


def finish_body(got_ref, parts_ref, new_ref, score_ref):
    sources, count, features = got_ref.shape
    own = new_ref.shape[1]
    pieces = own // LANES
    total = got_ref[0].astype(F32)
    for source in range(1, sources):
        total += got_ref[source].astype(F32)
    total = total.astype(BF16).astype(F32)
    mine = jnp.zeros((count, own), F32)
    for place in range(sources):
        mine = jnp.where(
            lax.axis_index("head") == place, total[:, place * own : (place + 1) * own], mine
        )
    new_ref[...] = mine.astype(BF16)
    weights = []
    for place in range(sources):
        extra = parts_ref[place, :, 2 * LANES :].astype(F32)
        for i in range(pieces):
            weights.append(
                extra[i : i + 1]
                + extra[pieces + i : pieces + i + 1]
                + extra[2 * pieces + i : 2 * pieces + i + 1]
            )
    weight = jnp.concatenate(weights, axis=1)
    product = jnp.sum(total * weight, axis=-1, keepdims=True)
    squares = jnp.sum(total * total, axis=-1, keepdims=True)
    score = product * lax.rsqrt(squares / features + EPS)
    row = lax.broadcasted_iota(jnp.int32, (count, LANES), 0)
    lane = lax.broadcasted_iota(jnp.int32, (count, LANES), 1)
    flat = jnp.sum(jnp.where(row == lane, score, 0.0), axis=0, keepdims=True)
    score_ref[...] = flat[:, :count]


def shards(
    hidden,
    attn_gain,
    q_weight,
    gate_weight,
    key_value_weight,
    q_gain,
    k_gain,
    out_weight,
    prompt_key_cache,
    prompt_value_cache,
    tail_key_cache,
    tail_value_cache,
    mlp_gain,
    mlp_gate,
    mlp_up,
    mlp_down,
    final_gain,
    score_weight,
    prompt_lengths,
    tail_lengths,
    group_prompt,
):
    head_count = lax.axis_size("head")
    group_count = lax.axis_size("req")
    count = hidden.shape[0]
    features = attn_gain.shape[0]
    width = q_gain.shape[0]
    own_cols = q_weight.shape[1]
    own_heads = own_cols // width
    kv_heads = prompt_key_cache.shape[2]
    cont_count = tail_lengths.shape[1]
    block = features // group_count
    hidden_units = mlp_gate.shape[1]
    smem = whole(pltpu.SMEM)
    facts = (prompt_lengths, tail_lengths.T, group_prompt)

    rows = lax.all_gather(hidden, "head", axis=1, tiled=True)
    sent, gate = call(
        functools.partial(project_body, cont_count),
        [((2 * count, own_cols), BF16), ((count, own_cols), F32)],
        [whole()] * 7 + [smem] * 3,
        4,
        "project",
        flops=2 * count * features * own_cols * 3,
        read=6 * features * own_cols,
    )(
        rows,
        attn_gain.reshape(1, features),
        in_vmem(q_weight),
        in_vmem(key_value_weight),
        in_vmem(gate_weight),
        q_gain.reshape(1, width),
        k_gain.reshape(1, width),
        *facts,
    )
    got = lax.all_gather(sent, "head", axis=1, tiled=True)
    (parts,) = call(
        functools.partial(attend_body, cont_count, kv_heads, own_heads),
        [((head_count, own_heads * count, 2 * width + LANES), BF16)],
        [whole()] * 7 + [smem] * 3,
        8,
        "attend",
        flops=1 << 29,
        read=4 * prompt_key_cache.size,
    )(
        got,
        in_vmem(prompt_key_cache.reshape(-1, width)),
        in_vmem(prompt_value_cache.reshape(-1, width)),
        in_vmem(tail_key_cache.reshape(-1, width)),
        in_vmem(tail_value_cache.reshape(-1, width)),
        final_gain.reshape(1, -1),
        score_weight.reshape(1, -1),
        *facts,
    )
    parts = lax.all_to_all(parts, "head", split_axis=0, concat_axis=0, tiled=True)
    (mixed,) = call(
        mix_body,
        [((group_count, head_count, count, block), BF16)],
        [whole()] * 4,
        4,
        "mix",
        flops=2 * count * features * own_cols,
        read=2 * features * own_cols,
    )(parts, gate, rows, in_vmem(out_weight))
    mixed = mixed.reshape(group_count * head_count, count, block)
    mixed = lax.all_to_all(mixed, ("req", "head"), split_axis=0, concat_axis=0, tiled=True)
    mixed = mixed.reshape(group_count, head_count, count, block)
    (wide,) = call(
        expand_body,
        [((group_count, count, 2 * hidden_units + block), BF16)],
        [whole()] * 4 + [smem],
        8,
        "expand",
        flops=4 * count * group_count * block * hidden_units,
        read=4 * block * hidden_units,
    )(
        mixed,
        mlp_gain.reshape(group_count, 1, block),
        in_vmem(mlp_gate),
        in_vmem(mlp_up),
        group_prompt,
    )
    wide = lax.all_to_all(wide, "req", split_axis=0, concat_axis=0, tiled=True)
    (down,) = call(
        functools.partial(reduce_body, head_count),
        [((count, features), BF16)],
        [whole()] * 2,
        4,
        "reduce",
        flops=2 * count * features * hidden_units,
        read=2 * features * hidden_units,
    )(wide, in_vmem(mlp_down))
    everyone = lax.all_gather(down, "head", axis=0, tiled=False)
    new_hidden, score = call(
        finish_body,
        [((count, features // head_count), BF16), ((1, count), F32)],
        [whole()] * 2,
        4,
        "finish",
        outs_vmem=False,
    )(everyone, parts)
    return (new_hidden, score.reshape(count))


def solution(mesh):
    return jax.shard_map(
        shards,
        mesh=mesh,
        in_specs=(
            P("req", "head"),
            P(),
            P(None, "head"),
            P(None, "head"),
            P(None, "head"),
            P(),
            P(),
            P("head", None),
            P("req", "head", None, None),
            P("req", "head", None, None),
            P("req", None, "head", None, None),
            P("req", None, "head", None, None),
            P(),
            P("req", "head"),
            P("req", "head"),
            P("head", None),
            P("head"),
            P("head"),
            P(),
            P(),
            P(),
        ),
        out_specs=(P("req", "head"), P("req")),
        check_vma=False,
    )
```

```python
import functools
import math

import jax
import jax.numpy as jnp
from jax import lax
from jax.experimental import pallas as pl
from jax.experimental.pallas import tpu as pltpu
from jax.sharding import PartitionSpec as P

EPS = 1e-06
THETA = 1000000.0
LANES = 128
BF16 = jnp.bfloat16
F32 = jnp.float32


def in_vmem(x):
    return pltpu.with_memory_space_constraint(x, pltpu.VMEM)


def whole(memory_space=pltpu.VMEM):
    return pl.BlockSpec(memory_space=memory_space)


def in_hbm(x):
    return pltpu.with_memory_space_constraint(x, pltpu.HBM)


def shifted(x, shift):
    size = lax.axis_size("head")
    return lax.ppermute(x, "head", [(i, (i + shift) % size) for i in range(size)])


def source_of(slot, size):
    return lax.rem(lax.axis_index("head") - slot + size, size)


def call(body, outs, specs, limit_mib, name, flops=0, read=0, outs_vmem=True, scratch=()):
    shapes = [
        pltpu.VMEM(shape, dtype) if outs_vmem else jax.ShapeDtypeStruct(shape, dtype)
        for shape, dtype in outs
    ]
    return pl.pallas_call(
        body,
        out_shape=shapes,
        in_specs=specs,
        out_specs=[whole()] * len(outs),
        scratch_shapes=list(scratch),
        compiler_params=pltpu.CompilerParams(vmem_limit_bytes=limit_mib << 20),
        cost_estimate=pl.CostEstimate(flops=flops, bytes_accessed=read, transcendentals=0),
        name=name,
    )


def prepare_body(cont_count, count, copies, *refs):
    sources, refs = refs[:copies], refs[copies:]
    (prompts_hbm, tails_hbm, owners_hbm), refs = refs[:3], refs[3:]
    targets, refs = refs[:copies], refs[copies:]
    turn_ref, prompts_ref, tails_ref, owners_ref, fact_sems, sems = refs
    facts = [
        pltpu.make_async_copy(prompts_hbm, prompts_ref, fact_sems.at[0]),
        pltpu.make_async_copy(tails_hbm, tails_ref, fact_sems.at[1]),
        pltpu.make_async_copy(owners_hbm, owners_ref, fact_sems.at[2]),
    ]
    for fact in facts:
        fact.start()
    moves = [pltpu.make_async_copy(sources[i], targets[i], sems.at[i]) for i in range(copies)]
    for move in moves:
        move.start()
    for fact in facts:
        fact.wait()
    head_width = turn_ref.shape[2]
    new_count = count // cont_count
    prompt = owners_ref[lax.axis_index("req")]
    prompt_len = prompts_ref[prompt]
    row_of = lax.broadcasted_iota(jnp.int32, (count, head_width), 0)
    lane_of = lax.broadcasted_iota(jnp.int32, (count, head_width), 1)
    position = jnp.zeros((count, head_width), jnp.int32)
    for cont in range(cont_count):
        start = prompt_len + tails_ref[cont, prompt]
        position = jnp.where(row_of // new_count == cont, start + row_of % new_count, position)
    half = head_width // 2
    frequency = jnp.exp((-math.log(THETA) * 2.0 / head_width) * (lane_of % half).astype(F32))
    angles = position.astype(F32) * frequency
    turn_ref[0] = jnp.cos(angles)
    turn_ref[1] = jnp.where(lane_of < half, -1.0, 1.0) * jnp.sin(angles)
    for move in moves:
        move.wait()


def project_body(slots, *refs):
    slot_refs, refs = refs[:slots], refs[slots:]
    gain_ref, q_ref, kv_ref, gate_ref, q_gain_ref, k_gain_ref, turn_ref = refs[:7]
    sent_ref, gate_out_ref, rows_out_ref, rows_ref = refs[7:]
    count, own = slot_refs[0].shape
    head_width = q_gain_ref.shape[1]
    half = head_width // 2
    for slot in range(slots):
        start = pl.multiple_of(source_of(slot, slots) * own, LANES)
        rows_ref[:, pl.ds(start, own)] = slot_refs[slot][...].astype(F32)
    cosine, sine = turn_ref[0], turn_ref[1]
    rows = rows_ref[...]
    rows_out_ref[...] = rows * (1.0 / slots)
    scale = lax.rsqrt(jnp.mean(rows * rows, axis=-1, keepdims=True) + EPS)
    normed = (rows * scale * gain_ref[...]).astype(BF16)

    def keyed(block, gain):
        inverse = lax.rsqrt(jnp.mean(block * block, axis=-1, keepdims=True) + EPS)
        block = block * inverse * gain
        return block * cosine + pltpu.roll(block, half, 1) * sine

    queries = jnp.dot(normed, q_ref[...], preferred_element_type=F32)
    fresh = jnp.dot(normed, kv_ref[...], preferred_element_type=F32)
    block_count = kv_ref.shape[1] // head_width
    first_block = lax.axis_index("head") * block_count
    top, bottom = [], []
    for block in range(q_ref.shape[1] // head_width):
        top.append(
            keyed(queries[:, block * head_width : (block + 1) * head_width], q_gain_ref[...])
        )
    for block in range(block_count):
        plain = fresh[:, block * head_width : (block + 1) * head_width]
        is_key = (first_block + block) % 2 == 0
        bottom.append(jnp.where(is_key, keyed(plain, k_gain_ref[...]), plain))
    sent = jnp.concatenate(
        [jnp.concatenate(top, axis=1), jnp.concatenate(bottom, axis=1)], axis=0
    )
    sent_ref[...] = sent.astype(BF16)
    gate_out_ref[...] = jnp.dot(normed, gate_ref[...], preferred_element_type=F32)


def split_parts(value):
    high = value.astype(BF16).astype(F32)
    middle = (value - high).astype(BF16).astype(F32)
    low = value - high - middle
    return [high, middle, low]


def attend_body(cont_count, kv_heads, slots, *refs):
    slot_refs, refs = refs[:slots], refs[slots:]
    (
        keys_ref,
        values_ref,
        tail_keys_ref,
        tail_values_ref,
        final_gain_ref,
        score_weight_ref,
        prompts_ref,
        tails_ref,
        owners_ref,
    ) = refs[:9]
    out_refs, fresh_ref = refs[9 : 9 + slots], refs[9 + slots]
    count = slot_refs[0].shape[0] // 2
    width = keys_ref.shape[1]
    own_heads = slot_refs[0].shape[1] // width
    own_rows = own_heads * count
    all_heads = own_heads * slots
    sharing = all_heads // kv_heads
    new_count = count // cont_count
    head_place = lax.axis_index("head")
    prompt = owners_ref[lax.axis_index("req")]
    prompt_len = prompts_ref[prompt]
    queries = []
    for slot in range(slots):
        got = slot_refs[slot][...].astype(F32)
        source = source_of(slot, slots)
        for i in range(own_heads):
            piece = got[:, i * width : (i + 1) * width]
            queries.append(piece[:count])
            fresh_ref[source * own_heads + i] = piece[count:]
    queries = jnp.concatenate(queries, axis=0).astype(BF16)
    fresh_keys = jnp.concatenate([fresh_ref[2 * k] for k in range(kv_heads)], axis=0)
    fresh_values = jnp.concatenate([fresh_ref[2 * k + 1] for k in range(kv_heads)], axis=0)
    many = all_heads * count
    score_scale = 1.0 / math.sqrt(width)

    def part(keys, values, live):
        scores = lax.dot_general(
            queries, keys, (((1,), (1,)), ((), ())), preferred_element_type=F32
        )
        weights = jnp.where(live, jnp.exp(scores * score_scale), 0.0).astype(BF16)
        with_ones = jnp.concatenate([values, jnp.ones(values.shape, BF16)], axis=1)
        return jnp.dot(weights, with_ones, preferred_element_type=F32)

    def places(span):
        row = lax.broadcasted_iota(jnp.int32, (many, span), 0)
        lane = lax.broadcasted_iota(jnp.int32, (many, span), 1)
        place = head_place - row // own_rows
        place = jnp.where(place < 0, place + slots, place)
        head = place * own_heads + (row % own_rows) // count
        return row, lane, head // sharing

    total_rows = keys_ref.shape[0]
    step = min(1024, total_rows)
    row, lane, kv_of = places(step)
    matching = lane % kv_heads == kv_of
    left = (prompt_len - head_place * (total_rows // kv_heads)) * kv_heads
    numer = jnp.zeros((many, 2 * width), F32)
    for start in range(0, total_rows, step):
        live = matching & (lane < left - start)
        numer += part(keys_ref[start : start + step, :], values_ref[start : start + step, :], live)

    tail_rows = tail_keys_ref.shape[0] // cont_count
    row, lane, kv_of = places(tail_rows)
    matching = lane % kv_heads == kv_of
    for cont in range(cont_count):
        left = (tails_ref[cont, prompt] - head_place * (tail_rows // kv_heads)) * kv_heads
        live = matching & (lane < left) & ((row % count) // new_count == cont)
        start = cont * tail_rows
        numer += part(
            tail_keys_ref[start : start + tail_rows, :],
            tail_values_ref[start : start + tail_rows, :],
            live,
        )

    row, lane, kv_of = places(count * kv_heads)
    live = (
        (lane // count == kv_of)
        & ((lane % count) // new_count == (row % count) // new_count)
        & (lane % new_count <= row % new_count)
        & (head_place == 0)
    )
    numer += part(fresh_keys.astype(BF16), fresh_values.astype(BF16), live)

    product = final_gain_ref[...] * score_weight_ref[...]
    pieces = [
        p[:, i * LANES : (i + 1) * LANES]
        for p in split_parts(product)
        for i in range(product.shape[1] // LANES)
    ]
    filler = jnp.zeros((own_rows - len(pieces), LANES), F32)
    extra = jnp.concatenate(pieces + [filler], axis=0)
    for slot in range(slots):
        mine = numer[slot * own_rows : (slot + 1) * own_rows, :]
        out_refs[slot][...] = jnp.concatenate([mine, extra], axis=1).astype(BF16)


def mix_body(slots, *refs):
    got_refs = refs[:slots]
    gate_ref, rows_ref, weight_ref, out_ref = refs[slots:]
    own_rows = got_refs[0].shape[0]
    count = rows_ref.shape[0]
    width = LANES
    summed = got_refs[0][:, : 2 * width].astype(F32)
    for slot in range(1, slots):
        summed += got_refs[slot][:, : 2 * width].astype(F32)
    attention = summed[:, :width] / summed[:, width:]
    side_by_side = jnp.concatenate(
        [attention[i : i + count] for i in range(0, own_rows, count)], axis=1
    )
    gated = (side_by_side * jax.nn.sigmoid(gate_ref[...])).astype(BF16)
    mixed = jnp.dot(gated, weight_ref[...], preferred_element_type=F32)
    mixed += rows_ref[...]
    mixed = mixed.astype(BF16)
    places, copies, _, block = out_ref.shape
    for place in range(places):
        piece = mixed[:, place * block : (place + 1) * block]
        for copy in range(copies):
            out_ref[place, copy] = piece


def expand_body(got_ref, gain_ref, gate_ref, up_ref, owners_ref, out_ref):
    groups, sources, count, block = got_ref.shape
    summed = got_ref[:, 0].astype(F32)
    for source in range(1, sources):
        summed += got_ref[:, source].astype(F32)
    attended = summed.reshape(groups * count, block).astype(BF16).astype(F32)
    scaled = (attended * gain_ref[lax.axis_index("req")]).astype(BF16)
    gate = jnp.dot(scaled, gate_ref[...], preferred_element_type=F32)
    up = jnp.dot(scaled, up_ref[...], preferred_element_type=F32)
    sent = jnp.concatenate([gate, up, attended], axis=1).astype(BF16)
    sent = sent.reshape(groups, count, sent.shape[1])
    for group in range(groups):
        out_ref[owners_ref[group]] = sent[group]


def reduce_body(sources, got_ref, weight_ref, out_ref):
    blocks, count, width = got_ref.shape
    hidden_units = weight_ref.shape[0]
    total = got_ref[0, :, : 2 * hidden_units].astype(F32)
    for block in range(1, blocks):
        total += got_ref[block, :, : 2 * hidden_units].astype(F32)
    attended = jnp.concatenate(
        [got_ref[block, :, 2 * hidden_units :].astype(F32) for block in range(blocks)], axis=1
    )
    scale = lax.rsqrt(jnp.mean(attended * attended, axis=-1, keepdims=True) + EPS)
    gate = total[:, :hidden_units] * scale
    up = total[:, hidden_units:] * scale
    act = (gate * jax.nn.sigmoid(gate) * up).astype(BF16)
    down = jnp.dot(act, weight_ref[...], preferred_element_type=F32)
    out_ref[...] = (down + attended * (1.0 / sources)).astype(BF16)


def finish_body(slots, *refs):
    got_refs, part_refs = refs[:slots], refs[slots : 2 * slots]
    new_ref, score_ref, total_ref, whole_ref, weight_ref = refs[2 * slots :]
    count, features = got_refs[0].shape
    own = new_ref.shape[1]
    pieces = own // LANES
    for slot in range(slots):
        total_ref[source_of(slot, slots)] = got_refs[slot][...].astype(F32)
        source = lax.rem(lax.axis_index("head") + slot, slots)
        extra = part_refs[slot][:, 2 * LANES :].astype(F32)
        for i in range(pieces):
            start = pl.multiple_of(source * own + i * LANES, LANES)
            weight_ref[:, pl.ds(start, LANES)] = (
                extra[i : i + 1]
                + extra[pieces + i : pieces + i + 1]
                + extra[2 * pieces + i : 2 * pieces + i + 1]
            )
    total = total_ref[0]
    for source in range(1, slots):
        total += total_ref[source]
    total = total.astype(BF16).astype(F32)
    whole_ref[...] = total
    start = pl.multiple_of(lax.axis_index("head") * own, LANES)
    new_ref[...] = whole_ref[:, pl.ds(start, own)].astype(BF16)
    weight = weight_ref[...]
    product = jnp.sum(total * weight, axis=-1, keepdims=True)
    squares = jnp.sum(total * total, axis=-1, keepdims=True)
    score = product * lax.rsqrt(squares / features + EPS)
    row = lax.broadcasted_iota(jnp.int32, (count, LANES), 0)
    lane = lax.broadcasted_iota(jnp.int32, (count, LANES), 1)
    flat = jnp.sum(jnp.where(row == lane, score, 0.0), axis=0, keepdims=True)
    score_ref[...] = flat[:, :count]


def shards(
    hidden,
    attn_gain,
    q_weight,
    gate_weight,
    key_value_weight,
    q_gain,
    k_gain,
    out_weight,
    prompt_key_cache,
    prompt_value_cache,
    tail_key_cache,
    tail_value_cache,
    mlp_gain,
    mlp_gate,
    mlp_up,
    mlp_down,
    final_gain,
    score_weight,
    prompt_lengths,
    tail_lengths,
    group_prompt,
):
    head_count = lax.axis_size("head")
    group_count = lax.axis_size("req")
    count = hidden.shape[0]
    features = attn_gain.shape[0]
    width = q_gain.shape[0]
    own_cols = q_weight.shape[1]
    own_heads = own_cols // width
    kv_heads = prompt_key_cache.shape[2]
    cont_count = tail_lengths.shape[1]
    block = features // group_count
    hidden_units = mlp_gate.shape[1]
    smem = whole(pltpu.SMEM)
    facts = (prompt_lengths, tail_lengths.T, group_prompt)

    shifts = range(1, head_count)

    def around(x):
        return [x] + [shifted(x, shift) for shift in shifts]

    rows = around(hidden)
    moved = (
        q_weight,
        key_value_weight,
        gate_weight,
        prompt_key_cache.reshape(-1, width),
        prompt_value_cache.reshape(-1, width),
        tail_key_cache.reshape(-1, width),
        tail_value_cache.reshape(-1, width),
    )
    prepared = call(
        functools.partial(prepare_body, cont_count, count, len(moved)),
        [(x.shape, x.dtype) for x in moved] + [((2, count, width), F32)],
        [whole(pl.ANY)] * (len(moved) + 3),
        4,
        "prepare",
        read=2 * sum(x.size for x in moved),
        scratch=[
            pltpu.SMEM(facts[0].shape, jnp.int32),
            pltpu.SMEM(facts[1].shape, jnp.int32),
            pltpu.SMEM(facts[2].shape, jnp.int32),
            pltpu.SemaphoreType.DMA((3,)),
            pltpu.SemaphoreType.DMA((len(moved),)),
        ],
    )(*[in_hbm(x) for x in moved + facts])
    near_weights, near_caches, turn = prepared[:3], prepared[3:7], prepared[7]
    sent, gate, rows_share = call(
        functools.partial(project_body, head_count),
        [((2 * count, own_cols), BF16), ((count, own_cols), F32), ((count, features), F32)],
        [whole()] * (head_count + 7),
        4,
        "project",
        flops=2 * count * features * own_cols * 3,
        read=6 * features * own_cols,
        scratch=[pltpu.VMEM((count, features), F32)],
    )(
        *rows,
        attn_gain.reshape(1, features),
        *near_weights,
        q_gain.reshape(1, width),
        k_gain.reshape(1, width),
        turn,
    )
    parts = call(
        functools.partial(attend_body, cont_count, kv_heads, head_count),
        [((own_heads * count, 2 * width + LANES), BF16)] * head_count,
        [whole()] * (head_count + 6) + [smem] * 3,
        8,
        "attend",
        flops=1 << 29,
        read=4 * prompt_key_cache.size,
        scratch=[pltpu.VMEM((2 * kv_heads, count, width), F32)],
    )(
        *around(sent),
        *near_caches,
        final_gain.reshape(1, -1),
        score_weight.reshape(1, -1),
        *facts,
    )
    parts = [parts[0]] + [shifted(parts[shift], -shift) for shift in shifts]
    (mixed,) = call(
        functools.partial(mix_body, head_count),
        [((group_count, head_count, count, block), BF16)],
        [whole()] * (head_count + 3),
        4,
        "mix",
        flops=2 * count * features * own_cols,
        read=2 * features * own_cols,
    )(*parts, gate, rows_share, in_vmem(out_weight))
    mixed = mixed.reshape(group_count * head_count, count, block)
    mixed = lax.all_to_all(mixed, ("req", "head"), split_axis=0, concat_axis=0, tiled=True)
    mixed = mixed.reshape(group_count, head_count, count, block)
    (wide,) = call(
        expand_body,
        [((group_count, count, 2 * hidden_units + block), BF16)],
        [whole()] * 4 + [smem],
        8,
        "expand",
        flops=4 * count * group_count * block * hidden_units,
        read=4 * block * hidden_units,
    )(
        mixed,
        mlp_gain.reshape(group_count, 1, block),
        in_vmem(mlp_gate),
        in_vmem(mlp_up),
        group_prompt,
    )
    wide = lax.all_to_all(wide, "req", split_axis=0, concat_axis=0, tiled=True)
    (down,) = call(
        functools.partial(reduce_body, head_count),
        [((count, features), BF16)],
        [whole()] * 2,
        4,
        "reduce",
        flops=2 * count * features * hidden_units,
        read=2 * features * hidden_units,
    )(wide, in_vmem(mlp_down))
    own = features // head_count
    new_hidden, score = call(
        functools.partial(finish_body, head_count),
        [((count, own), BF16), ((1, count), F32)],
        [whole()] * (2 * head_count),
        4,
        "finish",
        outs_vmem=False,
        scratch=[
            pltpu.VMEM((head_count, count, features), F32),
            pltpu.VMEM((count, features), F32),
            pltpu.VMEM((1, features), F32),
        ],
    )(*around(down), *parts)
    return (new_hidden, score.reshape(count))


def solution(mesh):
    return jax.shard_map(
        shards,
        mesh=mesh,
        in_specs=(
            P("req", "head"),
            P(),
            P(None, "head"),
            P(None, "head"),
            P(None, "head"),
            P(),
            P(),
            P("head", None),
            P("req", "head", None, None),
            P("req", "head", None, None),
            P("req", None, "head", None, None),
            P("req", None, "head", None, None),
            P(),
            P("req", "head"),
            P("req", "head"),
            P("head", None),
            P("head"),
            P("head"),
            P(),
            P(),
            P(),
        ),
        out_specs=(P("req", "head"), P("req")),
        check_vma=False,
    )
```

```python
import functools
import math

import jax
import jax.numpy as jnp
from jax import lax
from jax.experimental import pallas as pl
from jax.experimental.pallas import tpu as pltpu
from jax.sharding import PartitionSpec as P

EPS = 1e-06
THETA = 1000000.0
LANES = 128
BF16 = jnp.bfloat16
F32 = jnp.float32


def in_vmem(x):
    return pltpu.with_memory_space_constraint(x, pltpu.VMEM)


def whole(memory_space=pltpu.VMEM):
    return pl.BlockSpec(memory_space=memory_space)


def in_hbm(x):
    return pltpu.with_memory_space_constraint(x, pltpu.HBM)


def swapped(x, axis, flip):
    return lax.ppermute(x, axis, [(i, i ^ flip) for i in range(lax.axis_size(axis))])


def far_first(count):
    return [0] + list(reversed(range(1, count)))


def reversed_tail(pieces):
    return [pieces[0]] + list(reversed(pieces[1:]))


def around(pieces, axis):
    got = [
        swapped(piece, axis, flip) if flip else piece
        for flip, piece in zip(far_first(len(pieces)), pieces)
    ]
    return reversed_tail(got)


def partner(axis, slot):
    return lax.axis_index(axis) ^ slot


def call(body, outs, specs, limit_mib, name, flops=0, read=0, outs_vmem=True, scratch=()):
    shapes = [
        pltpu.VMEM(shape, dtype) if outs_vmem else jax.ShapeDtypeStruct(shape, dtype)
        for shape, dtype in outs
    ]
    return pl.pallas_call(
        body,
        out_shape=shapes,
        in_specs=specs,
        out_specs=[whole()] * len(outs),
        scratch_shapes=list(scratch),
        compiler_params=pltpu.CompilerParams(vmem_limit_bytes=limit_mib << 20),
        cost_estimate=pl.CostEstimate(flops=flops, bytes_accessed=read, transcendentals=0),
        name=name,
    )


def start_copies(sources, targets, sems):
    moves = [
        pltpu.make_async_copy(source, target, sems.at[i])
        for i, (source, target) in enumerate(zip(sources, targets))
    ]
    for move in moves:
        move.start()
    return moves


def prepare_body(cont_count, count, copies, *refs):
    sources, refs = refs[:copies], refs[copies:]
    facts_hbm, refs = refs[:3], refs[3:]
    targets, refs = refs[:copies], refs[copies:]
    turn_ref, prompts_ref, tails_ref, owners_ref, fact_sems, sems = refs
    facts = start_copies(facts_hbm, (prompts_ref, tails_ref, owners_ref), fact_sems)
    moves = start_copies(sources, targets, sems)
    for fact in facts:
        fact.wait()
    head_width = turn_ref.shape[2]
    new_count = count // cont_count
    prompt = owners_ref[lax.axis_index("req")]
    prompt_len = prompts_ref[prompt]
    row_of = lax.broadcasted_iota(jnp.int32, (count, head_width), 0)
    lane_of = lax.broadcasted_iota(jnp.int32, (count, head_width), 1)
    position = jnp.zeros((count, head_width), jnp.int32)
    for cont in range(cont_count):
        start = prompt_len + tails_ref[cont, prompt]
        position = jnp.where(row_of // new_count == cont, start + row_of % new_count, position)
    half = head_width // 2
    frequency = jnp.exp((-math.log(THETA) * 2.0 / head_width) * (lane_of % half).astype(F32))
    angles = position.astype(F32) * frequency
    turn_ref[0] = jnp.cos(angles)
    turn_ref[1] = jnp.where(lane_of < half, -1.0, 1.0) * jnp.sin(angles)
    for move in moves:
        move.wait()


def project_body(slots, *refs):
    slot_refs, refs = refs[:slots], refs[slots:]
    gain_ref, q_ref, kv_ref, q_gain_ref, k_gain_ref, turn_ref = refs[:6]
    sent_ref, normed_ref, rows_out_ref, rows_ref = refs[6:]
    count, own = slot_refs[0].shape
    head_width = q_gain_ref.shape[1]
    half = head_width // 2
    for slot in range(slots):
        start = pl.multiple_of(partner("head", slot) * own, LANES)
        rows_ref[:, pl.ds(start, own)] = slot_refs[slot][...].astype(F32)
    cosine, sine = turn_ref[0], turn_ref[1]
    rows = rows_ref[...]
    rows_out_ref[...] = rows * (1.0 / slots)
    scale = lax.rsqrt(jnp.mean(rows * rows, axis=-1, keepdims=True) + EPS)
    normed = (rows * scale * gain_ref[...]).astype(BF16)
    normed_ref[...] = normed

    def keyed(block, gain):
        inverse = lax.rsqrt(jnp.mean(block * block, axis=-1, keepdims=True) + EPS)
        block = block * inverse * gain
        return block * cosine + pltpu.roll(block, half, 1) * sine

    queries = jnp.dot(normed, q_ref[...], preferred_element_type=F32)
    fresh = jnp.dot(normed, kv_ref[...], preferred_element_type=F32)
    block_count = kv_ref.shape[1] // head_width
    first_block = lax.axis_index("head") * block_count
    top, bottom = [], []
    for block in range(q_ref.shape[1] // head_width):
        top.append(
            keyed(queries[:, block * head_width : (block + 1) * head_width], q_gain_ref[...])
        )
    for block in range(block_count):
        plain = fresh[:, block * head_width : (block + 1) * head_width]
        is_key = (first_block + block) % 2 == 0
        bottom.append(jnp.where(is_key, keyed(plain, k_gain_ref[...]), plain))
    sent = jnp.concatenate(
        [jnp.concatenate(top, axis=1), jnp.concatenate(bottom, axis=1)], axis=0
    )
    sent_ref[...] = sent.astype(BF16)


def gate_body(copies, normed_ref, weight_hbm, *refs):
    sources, targets = refs[:copies], refs[copies : 2 * copies]
    gate_ref, weight_ref, weight_sem, sems = refs[2 * copies :]
    first = pltpu.make_async_copy(weight_hbm, weight_ref, weight_sem)
    first.start()
    moves = start_copies(sources, targets, sems)
    first.wait()
    gate_ref[...] = jnp.dot(normed_ref[...], weight_ref[...], preferred_element_type=F32)
    for move in moves:
        move.wait()


def split_parts(value):
    high = value.astype(BF16).astype(F32)
    middle = (value - high).astype(BF16).astype(F32)
    low = value - high - middle
    return [high, middle, low]


def attend_body(cont_count, kv_heads, slots, *refs):
    slot_refs, refs = refs[:slots], refs[slots:]
    (
        keys_ref,
        values_ref,
        tail_keys_ref,
        tail_values_ref,
        final_gain_ref,
        score_weight_ref,
        prompts_ref,
        tails_ref,
        owners_ref,
    ) = refs[:9]
    out_refs, fresh_ref = refs[9 : 9 + slots], refs[9 + slots]
    count = slot_refs[0].shape[0] // 2
    width = keys_ref.shape[1]
    own_heads = slot_refs[0].shape[1] // width
    own_rows = own_heads * count
    all_heads = own_heads * slots
    sharing = all_heads // kv_heads
    new_count = count // cont_count
    head_place = lax.axis_index("head")
    prompt = owners_ref[lax.axis_index("req")]
    prompt_len = prompts_ref[prompt]
    queries = []
    for slot in range(slots):
        got = slot_refs[slot][...].astype(F32)
        source = partner("head", slot)
        for i in range(own_heads):
            piece = got[:, i * width : (i + 1) * width]
            queries.append(piece[:count])
            fresh_ref[source * own_heads + i] = piece[count:]
    queries = jnp.concatenate(queries, axis=0).astype(BF16)
    fresh_keys = jnp.concatenate([fresh_ref[2 * k] for k in range(kv_heads)], axis=0)
    fresh_values = jnp.concatenate([fresh_ref[2 * k + 1] for k in range(kv_heads)], axis=0)
    many = all_heads * count
    score_scale = 1.0 / math.sqrt(width)

    def part(keys, values, live):
        scores = lax.dot_general(
            queries, keys, (((1,), (1,)), ((), ())), preferred_element_type=F32
        )
        weights = jnp.where(live, jnp.exp(scores * score_scale), 0.0).astype(BF16)
        with_ones = jnp.concatenate([values, jnp.ones(values.shape, BF16)], axis=1)
        return jnp.dot(weights, with_ones, preferred_element_type=F32)

    def places(span):
        row = lax.broadcasted_iota(jnp.int32, (many, span), 0)
        lane = lax.broadcasted_iota(jnp.int32, (many, span), 1)
        place = head_place ^ (row // own_rows)
        head = place * own_heads + (row % own_rows) // count
        return row, lane, head // sharing

    total_rows = keys_ref.shape[0]
    step = min(1024, total_rows)
    row, lane, kv_of = places(step)
    matching = lane % kv_heads == kv_of
    left = (prompt_len - head_place * (total_rows // kv_heads)) * kv_heads
    numer = jnp.zeros((many, 2 * width), F32)
    for start in range(0, total_rows, step):
        live = matching & (lane < left - start)
        numer += part(keys_ref[start : start + step, :], values_ref[start : start + step, :], live)

    tail_rows = tail_keys_ref.shape[0] // cont_count
    row, lane, kv_of = places(tail_rows)
    matching = lane % kv_heads == kv_of
    for cont in range(cont_count):
        left = (tails_ref[cont, prompt] - head_place * (tail_rows // kv_heads)) * kv_heads
        live = matching & (lane < left) & ((row % count) // new_count == cont)
        start = cont * tail_rows
        numer += part(
            tail_keys_ref[start : start + tail_rows, :],
            tail_values_ref[start : start + tail_rows, :],
            live,
        )

    row, lane, kv_of = places(count * kv_heads)
    live = (
        (lane // count == kv_of)
        & ((lane % count) // new_count == (row % count) // new_count)
        & (lane % new_count <= row % new_count)
        & (head_place == 0)
    )
    numer += part(fresh_keys.astype(BF16), fresh_values.astype(BF16), live)

    product = final_gain_ref[...] * score_weight_ref[...]
    pieces = [
        p[:, i * LANES : (i + 1) * LANES]
        for p in split_parts(product)
        for i in range(product.shape[1] // LANES)
    ]
    filler = jnp.zeros((own_rows - len(pieces), LANES), F32)
    extra = jnp.concatenate(pieces + [filler], axis=0)
    for slot, out_ref in zip(far_first(slots), out_refs):
        mine = numer[slot * own_rows : (slot + 1) * own_rows, :]
        out_ref[...] = jnp.concatenate([mine, extra], axis=1).astype(BF16)


def mix_body(slots, *refs):
    got_refs = refs[:slots]
    gate_ref, rows_ref, weight_ref, out_ref = refs[slots:]
    own_rows = got_refs[0].shape[0]
    count = rows_ref.shape[0]
    width = LANES
    summed = got_refs[0][:, : 2 * width].astype(F32)
    for slot in range(1, slots):
        summed += got_refs[slot][:, : 2 * width].astype(F32)
    attention = summed[:, :width] / summed[:, width:]
    side_by_side = jnp.concatenate(
        [attention[i : i + count] for i in range(0, own_rows, count)], axis=1
    )
    gated = (side_by_side * jax.nn.sigmoid(gate_ref[...])).astype(BF16)
    mixed = jnp.dot(gated, weight_ref[...], preferred_element_type=F32)
    mixed += rows_ref[...]
    mixed = mixed.astype(BF16)
    places, copies, _, block = out_ref.shape
    for place in range(places):
        piece = mixed[:, place * block : (place + 1) * block]
        for copy in range(copies):
            out_ref[place, copy] = piece


def expand_body(got_ref, gain_ref, gate_ref, up_ref, owners_ref, *out_refs):
    groups, sources, count, block = got_ref.shape
    pieces = []
    for slot in range(groups):
        group = jnp.int32(0)
        for i in range(groups):
            group = jnp.where(owners_ref[i] == partner("req", slot), i, group)
        got = got_ref[group]
        summed = got[0].astype(F32)
        for source in range(1, sources):
            summed += got[source].astype(F32)
        pieces.append(summed)
    attended = jnp.concatenate(pieces, axis=0).astype(BF16).astype(F32)
    scaled = (attended * gain_ref[lax.axis_index("req")]).astype(BF16)
    gate = jnp.dot(scaled, gate_ref[...], preferred_element_type=F32)
    up = jnp.dot(scaled, up_ref[...], preferred_element_type=F32)
    for slot, out_ref in zip(far_first(groups), out_refs):
        rows = slice(slot * count, (slot + 1) * count)
        sent = jnp.concatenate([gate[rows], up[rows], attended[rows]], axis=1)
        out_ref[...] = sent.astype(BF16)


def reduce_body(slots, sources, *refs):
    got_refs = refs[:slots]
    weight_ref, out_ref, attended_ref = refs[slots:]
    hidden_units = weight_ref.shape[0]
    total = got_refs[0][:, : 2 * hidden_units].astype(F32)
    for slot in range(1, slots):
        total += got_refs[slot][:, : 2 * hidden_units].astype(F32)
    for slot, got_ref in zip(far_first(slots), got_refs):
        attended_ref[partner("req", slot)] = got_ref[:, 2 * hidden_units :].astype(F32)
    attended = jnp.concatenate([attended_ref[i] for i in range(slots)], axis=1)
    scale = lax.rsqrt(jnp.mean(attended * attended, axis=-1, keepdims=True) + EPS)
    gate = total[:, :hidden_units] * scale
    up = total[:, hidden_units:] * scale
    act = (gate * jax.nn.sigmoid(gate) * up).astype(BF16)
    down = jnp.dot(act, weight_ref[...], preferred_element_type=F32)
    out_ref[...] = (down + attended * (1.0 / sources)).astype(BF16)


def finish_body(slots, *refs):
    got_refs, part_refs = refs[:slots], refs[slots : 2 * slots]
    new_ref, score_ref, total_ref, whole_ref, weight_ref = refs[2 * slots :]
    count, features = got_refs[0].shape
    own = new_ref.shape[1]
    pieces = own // LANES
    for slot in range(slots):
        source = partner("head", slot)
        total_ref[source] = got_refs[slot][...].astype(F32)
        extra = part_refs[slot][:, 2 * LANES :].astype(F32)
        for i in range(pieces):
            start = pl.multiple_of(source * own + i * LANES, LANES)
            weight_ref[:, pl.ds(start, LANES)] = (
                extra[i : i + 1]
                + extra[pieces + i : pieces + i + 1]
                + extra[2 * pieces + i : 2 * pieces + i + 1]
            )
    total = total_ref[0]
    for source in range(1, slots):
        total += total_ref[source]
    total = total.astype(BF16).astype(F32)
    whole_ref[...] = total
    start = pl.multiple_of(lax.axis_index("head") * own, LANES)
    new_ref[...] = whole_ref[:, pl.ds(start, own)].astype(BF16)
    weight = weight_ref[...]
    product = jnp.sum(total * weight, axis=-1, keepdims=True)
    squares = jnp.sum(total * total, axis=-1, keepdims=True)
    score = product * lax.rsqrt(squares / features + EPS)
    row = lax.broadcasted_iota(jnp.int32, (count, LANES), 0)
    lane = lax.broadcasted_iota(jnp.int32, (count, LANES), 1)
    flat = jnp.sum(jnp.where(row == lane, score, 0.0), axis=0, keepdims=True)
    score_ref[...] = flat[:, :count]


def shards(
    hidden,
    attn_gain,
    q_weight,
    gate_weight,
    key_value_weight,
    q_gain,
    k_gain,
    out_weight,
    prompt_key_cache,
    prompt_value_cache,
    tail_key_cache,
    tail_value_cache,
    mlp_gain,
    mlp_gate,
    mlp_up,
    mlp_down,
    final_gain,
    score_weight,
    prompt_lengths,
    tail_lengths,
    group_prompt,
):
    head_count = lax.axis_size("head")
    group_count = lax.axis_size("req")
    count = hidden.shape[0]
    features = attn_gain.shape[0]
    width = q_gain.shape[0]
    own_cols = q_weight.shape[1]
    own_heads = own_cols // width
    kv_heads = prompt_key_cache.shape[2]
    cont_count = tail_lengths.shape[1]
    block = features // group_count
    hidden_units = mlp_gate.shape[1]
    smem = whole(pltpu.SMEM)
    facts = (prompt_lengths, tail_lengths.T, group_prompt)

    rows = around([hidden] * head_count, "head")
    moved = (q_weight, key_value_weight)
    near_q, near_kv, turn = call(
        functools.partial(prepare_body, cont_count, count, len(moved)),
        [(x.shape, x.dtype) for x in moved] + [((2, count, width), F32)],
        [whole(pl.ANY)] * (len(moved) + 3),
        4,
        "prepare",
        read=2 * sum(x.size for x in moved),
        scratch=[
            pltpu.SMEM(facts[0].shape, jnp.int32),
            pltpu.SMEM(facts[1].shape, jnp.int32),
            pltpu.SMEM(facts[2].shape, jnp.int32),
            pltpu.SemaphoreType.DMA((3,)),
            pltpu.SemaphoreType.DMA((len(moved),)),
        ],
    )(*[in_hbm(x) for x in moved + facts])
    sent, normed, rows_share = call(
        functools.partial(project_body, head_count),
        [((2 * count, own_cols), BF16), ((count, features), BF16), ((count, features), F32)],
        [whole()] * (head_count + 6),
        4,
        "project",
        flops=2 * count * features * own_cols * 2,
        read=4 * features * own_cols,
        scratch=[pltpu.VMEM((count, features), F32)],
    )(
        *rows,
        attn_gain.reshape(1, features),
        near_q,
        near_kv,
        q_gain.reshape(1, width),
        k_gain.reshape(1, width),
        turn,
    )
    got = around([sent] * head_count, "head")
    caches = [
        x.reshape(-1, width)
        for x in (prompt_key_cache, prompt_value_cache, tail_key_cache, tail_value_cache)
    ]
    *near_caches, gate = call(
        functools.partial(gate_body, len(caches)),
        [(x.shape, x.dtype) for x in caches] + [((count, own_cols), F32)],
        [whole()] + [whole(pl.ANY)] * (1 + len(caches)),
        8,
        "gate",
        flops=2 * count * features * own_cols,
        read=2 * features * own_cols + 2 * sum(x.size for x in caches),
        scratch=[
            pltpu.VMEM(gate_weight.shape, BF16),
            pltpu.SemaphoreType.DMA,
            pltpu.SemaphoreType.DMA((len(caches),)),
        ],
    )(normed, in_hbm(gate_weight), *[in_hbm(x) for x in caches])
    parts = call(
        functools.partial(attend_body, cont_count, kv_heads, head_count),
        [((own_heads * count, 2 * width + LANES), BF16)] * head_count,
        [whole()] * (head_count + 6) + [smem] * 3,
        8,
        "attend",
        flops=1 << 29,
        read=4 * prompt_key_cache.size,
        scratch=[pltpu.VMEM((2 * kv_heads, count, width), F32)],
    )(
        *got,
        *near_caches,
        final_gain.reshape(1, -1),
        score_weight.reshape(1, -1),
        *facts,
    )
    parts = around(parts, "head")
    (mixed,) = call(
        functools.partial(mix_body, head_count),
        [((group_count, head_count, count, block), BF16)],
        [whole()] * (head_count + 3),
        4,
        "mix",
        flops=2 * count * features * own_cols,
        read=2 * features * own_cols,
    )(*reversed_tail(parts), gate, rows_share, in_vmem(out_weight))
    mixed = mixed.reshape(group_count * head_count, count, block)
    mixed = lax.all_to_all(mixed, ("req", "head"), split_axis=0, concat_axis=0, tiled=True)
    mixed = mixed.reshape(group_count, head_count, count, block)
    wide = call(
        expand_body,
        [((count, 2 * hidden_units + block), BF16)] * group_count,
        [whole()] * 4 + [smem],
        8,
        "expand",
        flops=4 * count * group_count * block * hidden_units,
        read=4 * block * hidden_units,
    )(
        mixed,
        mlp_gain.reshape(group_count, 1, block),
        in_vmem(mlp_gate),
        in_vmem(mlp_up),
        group_prompt,
    )
    (down,) = call(
        functools.partial(reduce_body, group_count, head_count),
        [((count, features), BF16)],
        [whole()] * (group_count + 1),
        4,
        "reduce",
        flops=2 * count * features * hidden_units,
        read=2 * features * hidden_units,
        scratch=[pltpu.VMEM((group_count, count, block), F32)],
    )(*reversed_tail(around(wide, "req")), in_vmem(mlp_down))
    own = features // head_count
    new_hidden, score = call(
        functools.partial(finish_body, head_count),
        [((count, own), BF16), ((1, count), F32)],
        [whole()] * (2 * head_count),
        4,
        "finish",
        outs_vmem=False,
        scratch=[
            pltpu.VMEM((head_count, count, features), F32),
            pltpu.VMEM((count, features), F32),
            pltpu.VMEM((1, features), F32),
        ],
    )(*around([down] * head_count, "head"), *parts)
    return (new_hidden, score.reshape(count))


def solution(mesh):
    return jax.shard_map(
        shards,
        mesh=mesh,
        in_specs=(
            P("req", "head"),
            P(),
            P(None, "head"),
            P(None, "head"),
            P(None, "head"),
            P(),
            P(),
            P("head", None),
            P("req", "head", None, None),
            P("req", "head", None, None),
            P("req", None, "head", None, None),
            P("req", None, "head", None, None),
            P(),
            P("req", "head"),
            P("req", "head"),
            P("head", None),
            P("head"),
            P("head"),
            P(),
            P(),
            P(),
        ),
        out_specs=(P("req", "head"), P("req")),
        check_vma=False,
    )
```

```python
import functools
import math

import jax
import jax.numpy as jnp
from jax import lax
from jax.experimental import pallas as pl
from jax.experimental.pallas import tpu as pltpu
from jax.sharding import PartitionSpec as P

EPS = 1e-06
THETA = 1000000.0
LANES = 128
BF16 = jnp.bfloat16
F32 = jnp.float32


def in_vmem(x):
    return pltpu.with_memory_space_constraint(x, pltpu.VMEM)


def whole(memory_space=pltpu.VMEM):
    return pl.BlockSpec(memory_space=memory_space)


def in_hbm(x):
    return pltpu.with_memory_space_constraint(x, pltpu.HBM)


def swapped(x, axis, flip):
    return lax.ppermute(x, axis, [(i, i ^ flip) for i in range(lax.axis_size(axis))])


def far_first(count):
    return [0] + list(reversed(range(1, count)))


def reversed_tail(pieces):
    return [pieces[0]] + list(reversed(pieces[1:]))


def around(pieces, axis):
    got = [
        swapped(piece, axis, flip) if flip else piece
        for flip, piece in zip(far_first(len(pieces)), pieces)
    ]
    return reversed_tail(got)


def partner(axis, slot):
    return lax.axis_index(axis) ^ slot


def call(body, outs, specs, limit_mib, name, flops=0, read=0, outs_vmem=True, scratch=()):
    shapes = [
        pltpu.VMEM(shape, dtype) if outs_vmem else jax.ShapeDtypeStruct(shape, dtype)
        for shape, dtype in outs
    ]
    return pl.pallas_call(
        body,
        out_shape=shapes,
        in_specs=specs,
        out_specs=[whole()] * len(outs),
        scratch_shapes=list(scratch),
        compiler_params=pltpu.CompilerParams(vmem_limit_bytes=limit_mib << 20),
        cost_estimate=pl.CostEstimate(flops=flops, bytes_accessed=read, transcendentals=0),
        name=name,
    )


def start_copies(sources, targets, sems):
    moves = [
        pltpu.make_async_copy(source, target, sems.at[i])
        for i, (source, target) in enumerate(zip(sources, targets))
    ]
    for move in moves:
        move.start()
    return moves


def prepare_body(cont_count, count, copies, *refs):
    sources, refs = refs[:copies], refs[copies:]
    facts_hbm, refs = refs[:3], refs[3:]
    targets, refs = refs[:copies], refs[copies:]
    turn_ref, prompts_ref, tails_ref, owners_ref, fact_sems, sems = refs
    facts = start_copies(facts_hbm, (prompts_ref, tails_ref, owners_ref), fact_sems)
    moves = start_copies(sources, targets, sems)
    for fact in facts:
        fact.wait()
    head_width = turn_ref.shape[2]
    new_count = count // cont_count
    prompt = owners_ref[lax.axis_index("req")]
    prompt_len = prompts_ref[prompt]
    row_of = lax.broadcasted_iota(jnp.int32, (count, head_width), 0)
    lane_of = lax.broadcasted_iota(jnp.int32, (count, head_width), 1)
    position = jnp.zeros((count, head_width), jnp.int32)
    for cont in range(cont_count):
        start = prompt_len + tails_ref[cont, prompt]
        position = jnp.where(row_of // new_count == cont, start + row_of % new_count, position)
    half = head_width // 2
    frequency = jnp.exp((-math.log(THETA) * 2.0 / head_width) * (lane_of % half).astype(F32))
    angles = position.astype(F32) * frequency
    turn_ref[0] = jnp.cos(angles)
    turn_ref[1] = jnp.where(lane_of < half, -1.0, 1.0) * jnp.sin(angles)
    for move in moves:
        move.wait()


def project_body(slots, *refs):
    slot_refs, refs = refs[:slots], refs[slots:]
    gain_ref, q_ref, kv_ref, q_gain_ref, k_gain_ref, turn_ref = refs[:6]
    sent_ref, normed_ref, rows_out_ref, rows_ref = refs[6:]
    count, own = slot_refs[0].shape
    head_width = q_gain_ref.shape[1]
    half = head_width // 2
    for slot in range(slots):
        start = pl.multiple_of(partner("head", slot) * own, LANES)
        rows_ref[:, pl.ds(start, own)] = slot_refs[slot][...].astype(F32)
    cosine, sine = turn_ref[0], turn_ref[1]
    rows = rows_ref[...]
    rows_out_ref[...] = rows * (1.0 / slots)
    scale = lax.rsqrt(jnp.mean(rows * rows, axis=-1, keepdims=True) + EPS)
    normed = (rows * scale * gain_ref[...]).astype(BF16)
    normed_ref[...] = normed

    def keyed(block, gain):
        inverse = lax.rsqrt(jnp.mean(block * block, axis=-1, keepdims=True) + EPS)
        block = block * inverse * gain
        return block * cosine + pltpu.roll(block, half, 1) * sine

    queries = jnp.dot(normed, q_ref[...], preferred_element_type=F32)
    fresh = jnp.dot(normed, kv_ref[...], preferred_element_type=F32)
    block_count = kv_ref.shape[1] // head_width
    first_block = lax.axis_index("head") * block_count
    top, bottom = [], []
    for block in range(q_ref.shape[1] // head_width):
        top.append(
            keyed(queries[:, block * head_width : (block + 1) * head_width], q_gain_ref[...])
        )
    for block in range(block_count):
        plain = fresh[:, block * head_width : (block + 1) * head_width]
        is_key = (first_block + block) % 2 == 0
        bottom.append(jnp.where(is_key, keyed(plain, k_gain_ref[...]), plain))
    sent = jnp.concatenate(
        [jnp.concatenate(top, axis=1), jnp.concatenate(bottom, axis=1)], axis=0
    )
    sent_ref[...] = sent.astype(BF16)


def gate_body(normed_ref, weight_hbm, gate_ref, weight_ref, sem):
    move = pltpu.make_async_copy(weight_hbm, weight_ref, sem)
    move.start()
    move.wait()
    gate_ref[...] = jnp.dot(normed_ref[...], weight_ref[...], preferred_element_type=F32)


def split_parts(value):
    high = value.astype(BF16).astype(F32)
    middle = (value - high).astype(BF16).astype(F32)
    low = value - high - middle
    return [high, middle, low]


def attend_body(cont_count, kv_heads, steps, slots, *refs):
    slot_refs, refs = refs[:slots], refs[slots:]
    final_gain_ref, score_weight_ref, prompts_ref, tails_ref, owners_ref = refs[:5]
    caches_hbm, refs = refs[5:9], refs[9:]
    out_refs, fresh_ref, caches, sems, step_sems = (
        refs[:slots],
        refs[slots],
        refs[slots + 1 : slots + 5],
        refs[slots + 5],
        refs[slots + 6],
    )
    tail_keys_ref, tail_values_ref, keys_ref, values_ref = caches
    tail_moves = start_copies(caches_hbm[:2], caches[:2], sems)
    step = keys_ref.shape[0] // steps
    moves = []
    for i in range(steps):
        rows = pl.ds(i * step, step)
        moves.append(
            [
                pltpu.make_async_copy(
                    caches_hbm[2 + j].at[rows], caches[2 + j].at[rows], step_sems.at[j, i]
                )
                for j in range(2)
            ]
        )
        for move in moves[-1]:
            move.start()
    count = slot_refs[0].shape[0] // 2
    width = keys_ref.shape[1]
    own_heads = slot_refs[0].shape[1] // width
    own_rows = own_heads * count
    all_heads = own_heads * slots
    sharing = all_heads // kv_heads
    new_count = count // cont_count
    head_place = lax.axis_index("head")
    prompt = owners_ref[lax.axis_index("req")]
    prompt_len = prompts_ref[prompt]
    queries = []
    for slot in range(slots):
        got = slot_refs[slot][...].astype(F32)
        source = partner("head", slot)
        for i in range(own_heads):
            piece = got[:, i * width : (i + 1) * width]
            queries.append(piece[:count])
            fresh_ref[source * own_heads + i] = piece[count:]
    queries = jnp.concatenate(queries, axis=0).astype(BF16)
    fresh_keys = jnp.concatenate([fresh_ref[2 * k] for k in range(kv_heads)], axis=0)
    fresh_values = jnp.concatenate([fresh_ref[2 * k + 1] for k in range(kv_heads)], axis=0)
    many = all_heads * count
    score_scale = 1.0 / math.sqrt(width)

    def part(keys, values, live):
        scores = lax.dot_general(
            queries, keys, (((1,), (1,)), ((), ())), preferred_element_type=F32
        )
        weights = jnp.where(live, jnp.exp(scores * score_scale), 0.0).astype(BF16)
        with_ones = jnp.concatenate([values, jnp.ones(values.shape, BF16)], axis=1)
        return jnp.dot(weights, with_ones, preferred_element_type=F32)

    def places(span):
        row = lax.broadcasted_iota(jnp.int32, (many, span), 0)
        lane = lax.broadcasted_iota(jnp.int32, (many, span), 1)
        place = head_place ^ (row // own_rows)
        head = place * own_heads + (row % own_rows) // count
        return row, lane, head // sharing

    row, lane, kv_of = places(count * kv_heads)
    live = (
        (lane // count == kv_of)
        & ((lane % count) // new_count == (row % count) // new_count)
        & (lane % new_count <= row % new_count)
        & (head_place == 0)
    )
    numer = part(fresh_keys.astype(BF16), fresh_values.astype(BF16), live)

    tail_rows = tail_keys_ref.shape[0] // cont_count
    row, lane, kv_of = places(tail_rows)
    matching = lane % kv_heads == kv_of
    for move in tail_moves:
        move.wait()
    for cont in range(cont_count):
        left = (tails_ref[cont, prompt] - head_place * (tail_rows // kv_heads)) * kv_heads
        live = matching & (lane < left) & ((row % count) // new_count == cont)
        start = cont * tail_rows
        numer += part(
            tail_keys_ref[start : start + tail_rows, :],
            tail_values_ref[start : start + tail_rows, :],
            live,
        )

    row, lane, kv_of = places(step)
    matching = lane % kv_heads == kv_of
    left = (prompt_len - head_place * (keys_ref.shape[0] // kv_heads)) * kv_heads
    for i in range(steps):
        for move in moves[i]:
            move.wait()
        start = i * step
        live = matching & (lane < left - start)
        numer += part(keys_ref[start : start + step, :], values_ref[start : start + step, :], live)

    product = final_gain_ref[...] * score_weight_ref[...]
    pieces = [
        p[:, i * LANES : (i + 1) * LANES]
        for p in split_parts(product)
        for i in range(product.shape[1] // LANES)
    ]
    filler = jnp.zeros((own_rows - len(pieces), LANES), F32)
    extra = jnp.concatenate(pieces + [filler], axis=0)
    for slot, out_ref in zip(far_first(slots), out_refs):
        mine = numer[slot * own_rows : (slot + 1) * own_rows, :]
        out_ref[...] = jnp.concatenate([mine, extra], axis=1).astype(BF16)


def mix_body(slots, *refs):
    got_refs = refs[:slots]
    gate_ref, rows_ref, weight_ref, out_ref = refs[slots:]
    own_rows = got_refs[0].shape[0]
    count = rows_ref.shape[0]
    width = LANES
    summed = got_refs[0][:, : 2 * width].astype(F32)
    for slot in range(1, slots):
        summed += got_refs[slot][:, : 2 * width].astype(F32)
    attention = summed[:, :width] / summed[:, width:]
    side_by_side = jnp.concatenate(
        [attention[i : i + count] for i in range(0, own_rows, count)], axis=1
    )
    gated = (side_by_side * jax.nn.sigmoid(gate_ref[...])).astype(BF16)
    mixed = jnp.dot(gated, weight_ref[...], preferred_element_type=F32)
    mixed += rows_ref[...]
    mixed = mixed.astype(BF16)
    places, copies, _, block = out_ref.shape
    for place in range(places):
        piece = mixed[:, place * block : (place + 1) * block]
        for copy in range(copies):
            out_ref[place, copy] = piece


def halves(places):
    middle = max(places // 2, 1)
    return list(range(middle, places, 2)), list(range(0, middle, 2))


def expand_body(got_ref, gain_ref, gate_ref, up_ref, owners_ref, *out_refs):
    groups, sources, count, block = got_ref.shape
    flips = [half for half in halves(groups)]
    order = [flip ^ bit for half in flips for bit in (1, 0) for flip in half]
    pieces = []
    for slot in order:
        group = jnp.int32(0)
        for i in range(groups):
            group = jnp.where(owners_ref[i] == partner("req", slot), i, group)
        got = got_ref[group]
        summed = got[0].astype(F32)
        for source in range(1, sources):
            summed += got[source].astype(F32)
        pieces.append(summed)
    attended = jnp.concatenate(pieces, axis=0).astype(BF16).astype(F32)
    scaled = (attended * gain_ref[lax.axis_index("req")]).astype(BF16)
    gate = jnp.dot(scaled, gate_ref[...], preferred_element_type=F32)
    up = jnp.dot(scaled, up_ref[...], preferred_element_type=F32)
    wide = jnp.concatenate([gate, up, attended], axis=1)
    start = 0
    for out_ref in out_refs:
        for i in range(out_ref.shape[0]):
            out_ref[i] = wide[start : start + count].astype(out_ref.dtype)
            start += count


def pair_body(sums, got_ref, kept_ref, *out_refs):
    odd = lax.axis_index("req") % 2 == 1
    for i, out_ref in enumerate(out_refs):
        got = got_ref[i].astype(F32)
        kept = kept_ref[i]
        first = jnp.where(odd, got[:, sums:], kept[:, sums:])
        second = jnp.where(odd, kept[:, sums:], got[:, sums:])
        both = [got[:, :sums] + kept[:, :sums], first, second]
        out_ref[...] = jnp.concatenate(both, axis=1).astype(out_ref.dtype)


def reduce_body(flips, sources, *refs):
    got_refs = refs[: len(flips)]
    weight_ref, out_ref, attended_ref = refs[len(flips) :]
    hidden_units = weight_ref.shape[0]
    total = got_refs[0][:, : 2 * hidden_units].astype(F32)
    for got_ref in got_refs[1:]:
        total += got_ref[:, : 2 * hidden_units].astype(F32)
    for flip, got_ref in zip(flips, got_refs):
        attended_ref[partner("req", flip) // 2] = got_ref[:, 2 * hidden_units :].astype(F32)
    attended = jnp.concatenate([attended_ref[i] for i in range(len(flips))], axis=1)
    scale = lax.rsqrt(jnp.mean(attended * attended, axis=-1, keepdims=True) + EPS)
    gate = total[:, :hidden_units] * scale
    up = total[:, hidden_units:] * scale
    act = (gate * jax.nn.sigmoid(gate) * up).astype(BF16)
    down = jnp.dot(act, weight_ref[...], preferred_element_type=F32)
    out_ref[...] = (down + attended * (1.0 / sources)).astype(BF16)


def finish_body(slots, *refs):
    got_refs, part_refs = refs[:slots], refs[slots : 2 * slots]
    new_ref, score_ref, total_ref, whole_ref, weight_ref = refs[2 * slots :]
    count, features = got_refs[0].shape
    own = new_ref.shape[1]
    pieces = own // LANES
    for slot in range(slots):
        source = partner("head", slot)
        total_ref[source] = got_refs[slot][...].astype(F32)
        extra = part_refs[slot][:, 2 * LANES :].astype(F32)
        for i in range(pieces):
            start = pl.multiple_of(source * own + i * LANES, LANES)
            weight_ref[:, pl.ds(start, LANES)] = (
                extra[i : i + 1]
                + extra[pieces + i : pieces + i + 1]
                + extra[2 * pieces + i : 2 * pieces + i + 1]
            )
    total = total_ref[0]
    for source in range(1, slots):
        total += total_ref[source]
    total = total.astype(BF16).astype(F32)
    whole_ref[...] = total
    start = pl.multiple_of(lax.axis_index("head") * own, LANES)
    new_ref[...] = whole_ref[:, pl.ds(start, own)].astype(BF16)
    weight = weight_ref[...]
    product = jnp.sum(total * weight, axis=-1, keepdims=True)
    squares = jnp.sum(total * total, axis=-1, keepdims=True)
    score = product * lax.rsqrt(squares / features + EPS)
    row = lax.broadcasted_iota(jnp.int32, (count, LANES), 0)
    lane = lax.broadcasted_iota(jnp.int32, (count, LANES), 1)
    flat = jnp.sum(jnp.where(row == lane, score, 0.0), axis=0, keepdims=True)
    score_ref[...] = flat[:, :count]


def shards(
    hidden,
    attn_gain,
    q_weight,
    gate_weight,
    key_value_weight,
    q_gain,
    k_gain,
    out_weight,
    prompt_key_cache,
    prompt_value_cache,
    tail_key_cache,
    tail_value_cache,
    mlp_gain,
    mlp_gate,
    mlp_up,
    mlp_down,
    final_gain,
    score_weight,
    prompt_lengths,
    tail_lengths,
    group_prompt,
):
    head_count = lax.axis_size("head")
    group_count = lax.axis_size("req")
    count = hidden.shape[0]
    features = attn_gain.shape[0]
    width = q_gain.shape[0]
    own_cols = q_weight.shape[1]
    own_heads = own_cols // width
    kv_heads = prompt_key_cache.shape[2]
    cont_count = tail_lengths.shape[1]
    block = features // group_count
    hidden_units = mlp_gate.shape[1]
    smem = whole(pltpu.SMEM)
    facts = (prompt_lengths, tail_lengths.T, group_prompt)

    rows = around([hidden] * head_count, "head")
    moved = (q_weight, key_value_weight)
    near_q, near_kv, turn = call(
        functools.partial(prepare_body, cont_count, count, len(moved)),
        [(x.shape, x.dtype) for x in moved] + [((2, count, width), F32)],
        [whole(pl.ANY)] * (len(moved) + 3),
        4,
        "prepare",
        read=2 * sum(x.size for x in moved),
        scratch=[
            pltpu.SMEM(facts[0].shape, jnp.int32),
            pltpu.SMEM(facts[1].shape, jnp.int32),
            pltpu.SMEM(facts[2].shape, jnp.int32),
            pltpu.SemaphoreType.DMA((3,)),
            pltpu.SemaphoreType.DMA((len(moved),)),
        ],
    )(*[in_hbm(x) for x in moved + facts])
    sent, normed, rows_share = call(
        functools.partial(project_body, head_count),
        [((2 * count, own_cols), BF16), ((count, features), BF16), ((count, features), F32)],
        [whole()] * (head_count + 6),
        4,
        "project",
        flops=2 * count * features * own_cols * 2,
        read=4 * features * own_cols,
        scratch=[pltpu.VMEM((count, features), F32)],
    )(
        *rows,
        attn_gain.reshape(1, features),
        near_q,
        near_kv,
        q_gain.reshape(1, width),
        k_gain.reshape(1, width),
        turn,
    )
    got = around([sent] * head_count, "head")
    (gate,) = call(
        gate_body,
        [((count, own_cols), F32)],
        [whole(), whole(pl.ANY)],
        4,
        "gate",
        flops=2 * count * features * own_cols,
        read=2 * features * own_cols,
        scratch=[pltpu.VMEM(gate_weight.shape, BF16), pltpu.SemaphoreType.DMA],
    )(normed, in_hbm(gate_weight))
    caches = [
        x.reshape(-1, width)
        for x in (tail_key_cache, tail_value_cache, prompt_key_cache, prompt_value_cache)
    ]
    steps = pl.cdiv(caches[2].shape[0], 1024)
    parts = call(
        functools.partial(attend_body, cont_count, kv_heads, steps, head_count),
        [((own_heads * count, 2 * width + LANES), BF16)] * head_count,
        [whole()] * (head_count + 2) + [smem] * 3 + [whole(pl.ANY)] * len(caches),
        12,
        "attend",
        flops=1 << 29,
        read=2 * sum(x.size for x in caches),
        scratch=[pltpu.VMEM((2 * kv_heads, count, width), F32)]
        + [pltpu.VMEM(x.shape, BF16) for x in caches]
        + [pltpu.SemaphoreType.DMA((2,)), pltpu.SemaphoreType.DMA((2, steps))],
    )(
        *got,
        final_gain.reshape(1, -1),
        score_weight.reshape(1, -1),
        *facts,
        *[in_hbm(x) for x in caches],
    )
    parts = around(parts, "head")
    (mixed,) = call(
        functools.partial(mix_body, head_count),
        [((group_count, head_count, count, block), BF16)],
        [whole()] * (head_count + 3),
        4,
        "mix",
        flops=2 * count * features * own_cols,
        read=2 * features * own_cols,
    )(*reversed_tail(parts), gate, rows_share, in_vmem(out_weight))
    mixed = mixed.reshape(group_count * head_count, count, block)
    mixed = lax.all_to_all(mixed, ("req", "head"), split_axis=0, concat_axis=0, tiled=True)
    mixed = mixed.reshape(group_count, head_count, count, block)
    sums = 2 * hidden_units
    far, near = halves(group_count)
    pieces = call(
        expand_body,
        [
            ((len(half), count, sums + block), dtype)
            for half in (far, near)
            for dtype in (BF16, F32)
        ],
        [whole()] * 4 + [smem],
        8,
        "expand",
        flops=4 * count * group_count * block * hidden_units,
        read=4 * block * hidden_units,
    )(
        mixed,
        mlp_gain.reshape(group_count, 1, block),
        in_vmem(mlp_gate),
        in_vmem(mlp_up),
        group_prompt,
    )
    summed = []
    for half, sent, kept in ((far, *pieces[:2]), (near, *pieces[2:])):
        pairs = call(
            functools.partial(pair_body, sums),
            [((count, sums + 2 * block), BF16)] * len(half),
            [whole()] * 2,
            4,
            "pair",
            read=4 * sent.size,
        )(swapped(sent, "req", 1), kept)
        for flip, pair in zip(half, pairs):
            summed.append(swapped(pair, "req", flip) if flip else pair)
    (down,) = call(
        functools.partial(reduce_body, far + near, head_count),
        [((count, features), BF16)],
        [whole()] * (len(summed) + 1),
        4,
        "reduce",
        flops=2 * count * features * hidden_units,
        read=2 * features * hidden_units,
        scratch=[pltpu.VMEM((len(summed), count, 2 * block), F32)],
    )(*summed, in_vmem(mlp_down))
    own = features // head_count
    new_hidden, score = call(
        functools.partial(finish_body, head_count),
        [((count, own), BF16), ((1, count), F32)],
        [whole()] * (2 * head_count),
        4,
        "finish",
        outs_vmem=False,
        scratch=[
            pltpu.VMEM((head_count, count, features), F32),
            pltpu.VMEM((count, features), F32),
            pltpu.VMEM((1, features), F32),
        ],
    )(*around([down] * head_count, "head"), *parts)
    return (new_hidden, score.reshape(count))


def solution(mesh):
    return jax.shard_map(
        shards,
        mesh=mesh,
        in_specs=(
            P("req", "head"),
            P(),
            P(None, "head"),
            P(None, "head"),
            P(None, "head"),
            P(),
            P(),
            P("head", None),
            P("req", "head", None, None),
            P("req", "head", None, None),
            P("req", None, "head", None, None),
            P("req", None, "head", None, None),
            P(),
            P("req", "head"),
            P("req", "head"),
            P("head", None),
            P("head"),
            P("head"),
            P(),
            P(),
            P(),
        ),
        out_specs=(P("req", "head"), P("req")),
        check_vma=False,
    )
```

```python
import functools
import math

import jax
import jax.numpy as jnp
from jax import lax
from jax.experimental import pallas as pl
from jax.experimental.pallas import tpu as pltpu
from jax.sharding import PartitionSpec as P

EPS = 1e-06
THETA = 1000000.0
LANES = 128
BF16 = jnp.bfloat16
F32 = jnp.float32


def in_vmem(x):
    return pltpu.with_memory_space_constraint(x, pltpu.VMEM)


def whole(memory_space=pltpu.VMEM):
    return pl.BlockSpec(memory_space=memory_space)


def in_hbm(x):
    return pltpu.with_memory_space_constraint(x, pltpu.HBM)


def swapped(x, axis, flip):
    return lax.ppermute(x, axis, [(i, i ^ flip) for i in range(lax.axis_size(axis))])


def partner(axis, slot):
    return lax.axis_index(axis) ^ slot


def call(body, outs, specs, limit_mib, name, flops=0, read=0, outs_vmem=True, scratch=()):
    shapes = [
        pltpu.VMEM(shape, dtype) if outs_vmem else jax.ShapeDtypeStruct(shape, dtype)
        for shape, dtype in outs
    ]
    return pl.pallas_call(
        body,
        out_shape=shapes,
        in_specs=specs,
        out_specs=[whole()] * len(outs),
        scratch_shapes=list(scratch),
        compiler_params=pltpu.CompilerParams(vmem_limit_bytes=limit_mib << 20),
        cost_estimate=pl.CostEstimate(flops=flops, bytes_accessed=read, transcendentals=0),
        name=name,
    )


def start_copies(sources, targets, sems):
    moves = [
        pltpu.make_async_copy(source, target, sems.at[i])
        for i, (source, target) in enumerate(zip(sources, targets))
    ]
    for move in moves:
        move.start()
    return moves


def prepare_body(cont_count, count, copies, *refs):
    sources, refs = refs[:copies], refs[copies:]
    facts_hbm, refs = refs[:3], refs[3:]
    targets, refs = refs[:copies], refs[copies:]
    turn_ref, prompts_ref, tails_ref, owners_ref, fact_sems, sems = refs
    facts = start_copies(facts_hbm, (prompts_ref, tails_ref, owners_ref), fact_sems)
    moves = start_copies(sources, targets, sems)
    for fact in facts:
        fact.wait()
    head_width = turn_ref.shape[2]
    new_count = count // cont_count
    prompt = owners_ref[lax.axis_index("req")]
    prompt_len = prompts_ref[prompt]
    row_of = lax.broadcasted_iota(jnp.int32, (count, head_width), 0)
    lane_of = lax.broadcasted_iota(jnp.int32, (count, head_width), 1)
    position = jnp.zeros((count, head_width), jnp.int32)
    for cont in range(cont_count):
        start = prompt_len + tails_ref[cont, prompt]
        position = jnp.where(row_of // new_count == cont, start + row_of % new_count, position)
    half = head_width // 2
    frequency = jnp.exp((-math.log(THETA) * 2.0 / head_width) * (lane_of % half).astype(F32))
    angles = position.astype(F32) * frequency
    turn_ref[0] = jnp.cos(angles)
    turn_ref[1] = jnp.where(lane_of < half, -1.0, 1.0) * jnp.sin(angles)
    for move in moves:
        move.wait()


def project_body(slots, *refs):
    slot_refs, refs = refs[:slots], refs[slots:]
    gain_ref, q_ref, kv_ref, q_gain_ref, k_gain_ref, turn_ref = refs[:6]
    final_gain_ref, score_weight_ref = refs[6:8]
    sent_ref, normed_ref, rows_out_ref, rows_ref = refs[8:]
    count, own = slot_refs[0].shape
    head_width = q_gain_ref.shape[1]
    half = head_width // 2
    for slot in range(slots):
        start = pl.multiple_of(partner("head", slot) * own, LANES)
        rows_ref[:, pl.ds(start, own)] = slot_refs[slot][...].astype(F32)
    cosine, sine = turn_ref[0], turn_ref[1]
    rows = rows_ref[...]
    rows_out_ref[...] = rows * (1.0 / slots)
    scale = lax.rsqrt(jnp.mean(rows * rows, axis=-1, keepdims=True) + EPS)
    normed = (rows * scale * gain_ref[...]).astype(BF16)
    normed_ref[...] = normed

    def keyed(block, gain):
        inverse = lax.rsqrt(jnp.mean(block * block, axis=-1, keepdims=True) + EPS)
        block = block * inverse * gain
        return block * cosine + pltpu.roll(block, half, 1) * sine

    queries = jnp.dot(normed, q_ref[...], preferred_element_type=F32)
    fresh = jnp.dot(normed, kv_ref[...], preferred_element_type=F32)
    block_count = kv_ref.shape[1] // head_width
    first_block = lax.axis_index("head") * block_count
    top, bottom = [], []
    for block in range(q_ref.shape[1] // head_width):
        top.append(
            keyed(queries[:, block * head_width : (block + 1) * head_width], q_gain_ref[...])
        )
    for block in range(block_count):
        plain = fresh[:, block * head_width : (block + 1) * head_width]
        is_key = (first_block + block) % 2 == 0
        bottom.append(jnp.where(is_key, keyed(plain, k_gain_ref[...]), plain))
    score_parts = split_parts(final_gain_ref[...] * score_weight_ref[...])
    filler = jnp.zeros((count - len(score_parts), own), F32)
    sent = jnp.concatenate(
        [jnp.concatenate(top, axis=1), jnp.concatenate(bottom, axis=1), *score_parts, filler],
        axis=0,
    )
    sent_ref[0] = sent.astype(BF16)


def gate_body(normed_ref, weight_hbm, gate_ref, weight_ref, sem):
    move = pltpu.make_async_copy(weight_hbm, weight_ref, sem)
    move.start()
    move.wait()
    gate_ref[...] = jnp.dot(normed_ref[...], weight_ref[...], preferred_element_type=F32)


def fetch_body(copies, after_ref, *refs):
    sources, targets, sems = refs[:copies], refs[copies : 2 * copies], refs[2 * copies]
    first = [s.at[pl.ds(0, t.shape[0])] for s, t in zip(sources, targets)]
    for move in start_copies(first, targets, sems):
        move.wait()


def join_body(first_ref, second_ref, out_ref):
    size = first_ref.shape[0]
    out_ref[:size] = first_ref[...]
    out_ref[size:] = second_ref[...]


def add_body(first_ref, second_ref, out_ref):
    total = first_ref[...].astype(F32) + second_ref[...].astype(F32)
    out_ref[...] = total.astype(out_ref.dtype)


def fold_body(kept_ref, got_ref, sent_ref, still_kept_ref):
    for i in range(sent_ref.shape[0]):
        still_kept_ref[i] = kept_ref[2 * i] + got_ref[2 * i].astype(F32)
        sent_ref[i] = (kept_ref[2 * i + 1] + got_ref[2 * i + 1].astype(F32)).astype(BF16)


def split_parts(value):
    high = value.astype(BF16).astype(F32)
    middle = (value - high).astype(BF16).astype(F32)
    low = value - high - middle
    return [high, middle, low]


def attend_body(cont_count, kv_heads, *refs):
    near_ref, far_ref, prompts_ref, tails_ref, owners_ref = refs[:5]
    tail_keys_ref, tail_values_ref, early_keys_ref, early_values_ref = refs[5:9]
    late_hbm, refs = refs[9:11], refs[11:]
    sent_ref, kept_ref, fresh_ref, late_keys_ref, late_values_ref, sems = refs
    early = early_keys_ref.shape[0]
    late = late_keys_ref.shape[0]
    moves = start_copies(
        [hbm.at[pl.ds(early, late)] for hbm in late_hbm], [late_keys_ref, late_values_ref], sems
    )
    half = near_ref.shape[0]
    slots = 2 * half
    count = near_ref.shape[1] // 3
    width = early_keys_ref.shape[1]
    own_heads = near_ref.shape[2] // width
    own_rows = own_heads * count
    all_heads = own_heads * slots
    sharing = all_heads // kv_heads
    new_count = count // cont_count
    head_place = lax.axis_index("head")
    prompt = owners_ref[lax.axis_index("req")]
    prompt_len = prompts_ref[prompt]
    queries = []
    for slot in range(slots):
        got = (near_ref, far_ref)[slot // half][slot % half].astype(F32)
        source = partner("head", slot)
        for i in range(own_heads):
            piece = got[:, i * width : (i + 1) * width]
            queries.append(piece[:count])
            fresh_ref[source * own_heads + i] = piece[count : 2 * count]
    queries = jnp.concatenate(queries, axis=0).astype(BF16)
    fresh_keys = jnp.concatenate([fresh_ref[2 * k] for k in range(kv_heads)], axis=0)
    fresh_values = jnp.concatenate([fresh_ref[2 * k + 1] for k in range(kv_heads)], axis=0)
    many = all_heads * count
    score_scale = 1.0 / math.sqrt(width)

    def part(keys, values, live):
        scores = lax.dot_general(
            queries, keys, (((1,), (1,)), ((), ())), preferred_element_type=F32
        )
        weights = jnp.where(live, jnp.exp(scores * score_scale), 0.0).astype(BF16)
        with_ones = jnp.concatenate([values, jnp.ones(values.shape, BF16)], axis=1)
        return jnp.dot(weights, with_ones, preferred_element_type=F32)

    def places(span):
        row = lax.broadcasted_iota(jnp.int32, (many, span), 0)
        lane = lax.broadcasted_iota(jnp.int32, (many, span), 1)
        place = head_place ^ (row // own_rows)
        head = place * own_heads + (row % own_rows) // count
        return row, lane, head // sharing

    row, lane, kv_of = places(count * kv_heads)
    live = (
        (lane // count == kv_of)
        & ((lane % count) // new_count == (row % count) // new_count)
        & (lane % new_count <= row % new_count)
        & (head_place == 0)
    )
    numer = part(fresh_keys.astype(BF16), fresh_values.astype(BF16), live)

    tail_rows = tail_keys_ref.shape[0] // cont_count
    row, lane, kv_of = places(tail_rows)
    matching = lane % kv_heads == kv_of
    for cont in range(cont_count):
        left = (tails_ref[cont, prompt] - head_place * (tail_rows // kv_heads)) * kv_heads
        live = matching & (lane < left) & ((row % count) // new_count == cont)
        start = cont * tail_rows
        numer += part(
            tail_keys_ref[start : start + tail_rows, :],
            tail_values_ref[start : start + tail_rows, :],
            live,
        )

    step = min(1024, early)
    row, lane, kv_of = places(step)
    matching = lane % kv_heads == kv_of
    left = (prompt_len - head_place * ((early + late) // kv_heads)) * kv_heads
    for keys_ref, values_ref, base in (
        (early_keys_ref, early_values_ref, 0),
        (late_keys_ref, late_values_ref, early),
    ):
        if base:
            for move in moves:
                move.wait()
        for start in range(0, keys_ref.shape[0], step):
            live = matching & (lane < left - base - start)
            numer += part(
                keys_ref[start : start + step, :], values_ref[start : start + step, :], live
            )

    for i in range(half):
        kept_ref[i] = numer[2 * i * own_rows : (2 * i + 1) * own_rows, :]
        sent = numer[(2 * i + 1) * own_rows : (2 * i + 2) * own_rows, :]
        sent_ref[i] = sent.astype(BF16)


def mix_body(kept_ref, got_ref, gate_ref, rows_ref, weight_ref, out_ref):
    summed = kept_ref[0] + got_ref[0].astype(F32)
    count = rows_ref.shape[0]
    width = LANES
    attention = summed[:, :width] / summed[:, width:]
    side_by_side = jnp.concatenate(
        [attention[i : i + count] for i in range(0, summed.shape[0], count)], axis=1
    )
    gated = (side_by_side * jax.nn.sigmoid(gate_ref[...])).astype(BF16)
    mixed = jnp.dot(gated, weight_ref[...], preferred_element_type=F32)
    mixed = mixed + rows_ref[...]
    places, _, block = out_ref.shape
    for place in range(places):
        out_ref[place] = mixed[:, place * block : (place + 1) * block].astype(BF16)


def deal_body(first_ref, second_ref, kept_ref, sent_ref, whole_ref):
    total = first_ref[...].astype(F32) + second_ref[...].astype(F32)
    whole_ref[...] = total
    for i in range(kept_ref.shape[0]):
        kept_ref[i, 0] = whole_ref[partner("req", 2 * i)].astype(BF16)
        sent_ref[i, 0] = whole_ref[partner("req", 2 * i + 1)].astype(BF16)


def pass_body(held_ref, got_ref, kept_ref, sent_ref):
    rows = held_ref.shape[1]
    for i in range(kept_ref.shape[0]):
        for source, target in ((2 * i, kept_ref), (2 * i + 1, sent_ref)):
            target[i, :rows] = held_ref[source]
            target[i, rows:] = got_ref[source]


def halves(places):
    middle = max(places // 2, 1)
    return list(range(middle, places, 2)), list(range(0, middle, 2))


def expand_body(held_ref, got_ref, gain_ref, gate_ref, up_ref, owners_ref, *refs):
    out_refs, rows_ref = refs[:-1], refs[-1]
    half, count, block = held_ref.shape[1:]
    groups = 2 * half
    rows_ref[:half] = held_ref[0].astype(F32)
    rows_ref[half:] = got_ref[0].astype(F32)
    order = [flip ^ bit for part in halves(groups) for bit in (1, 0) for flip in part]
    pieces = []
    for slot in order:
        group = jnp.int32(0)
        for i in range(groups):
            group = jnp.where(owners_ref[i] == partner("req", slot), i, group)
        pieces.append(rows_ref[partner("req", group)])
    attended = jnp.concatenate(pieces, axis=0)
    scaled = (attended * gain_ref[lax.axis_index("req")]).astype(BF16)
    gate = jnp.dot(scaled, gate_ref[...], preferred_element_type=F32)
    up = jnp.dot(scaled, up_ref[...], preferred_element_type=F32)
    wide = jnp.concatenate([gate, up, attended], axis=1)
    start = 0
    for out_ref in out_refs:
        for i in range(out_ref.shape[0]):
            out_ref[i] = wide[start : start + count].astype(out_ref.dtype)
            start += count


def pair_body(sums, later, got_ref, kept_ref, *refs):
    out_refs = refs
    if later:
        later_ref, later_out_ref = refs[0], refs[1]
        later_out_ref[...] = later_ref[...]
        out_refs = refs[2:]
    odd = lax.axis_index("req") % 2 == 1
    for i, out_ref in enumerate(out_refs):
        got = got_ref[i].astype(F32)
        kept = kept_ref[i]
        first = jnp.where(odd, got[:, sums:], kept[:, sums:])
        second = jnp.where(odd, kept[:, sums:], got[:, sums:])
        both = [got[:, :sums] + kept[:, :sums], first, second]
        out_ref[...] = jnp.concatenate(both, axis=1).astype(out_ref.dtype)


def reduce_body(flips, sources, *refs):
    got_refs = refs[: len(flips)]
    weight_ref, out_ref, attended_ref = refs[len(flips) :]
    hidden_units = weight_ref.shape[0]
    total = got_refs[0][:, : 2 * hidden_units].astype(F32)
    for got_ref in got_refs[1:]:
        total += got_ref[:, : 2 * hidden_units].astype(F32)
    for flip, got_ref in zip(flips, got_refs):
        attended_ref[partner("req", flip) // 2] = got_ref[:, 2 * hidden_units :].astype(F32)
    attended = jnp.concatenate([attended_ref[i] for i in range(len(flips))], axis=1)
    scale = lax.rsqrt(jnp.mean(attended * attended, axis=-1, keepdims=True) + EPS)
    gate = total[:, :hidden_units] * scale
    up = total[:, hidden_units:] * scale
    act = (gate * jax.nn.sigmoid(gate) * up).astype(BF16)
    down = jnp.dot(act, weight_ref[...], preferred_element_type=F32)
    down = down + attended * (1.0 / sources)
    block = out_ref.shape[2]
    for i in range(out_ref.shape[0]):
        out_ref[i] = down[:, i * block : (i + 1) * block].astype(BF16)


def finish_body(kept_ref, got_ref, near_ref, far_ref, new_ref, score_ref, whole_ref, weight_ref):
    places, count, block = kept_ref.shape
    features = places * block
    own = new_ref.shape[1]
    half = near_ref.shape[0]
    total = kept_ref[...].astype(F32) + got_ref[...].astype(F32)
    total = jnp.concatenate([total[i] for i in range(places)], axis=1)
    total = total.astype(BF16).astype(F32)
    whole_ref[...] = total
    start = pl.multiple_of(lax.axis_index("head") * own, LANES)
    new_ref[...] = whole_ref[:, pl.ds(start, own)].astype(BF16)
    for slot in range(2 * half):
        parts = (near_ref, far_ref)[slot // half][slot % half].astype(F32)[2 * count :]
        start = pl.multiple_of(partner("head", slot) * own, LANES)
        weight_ref[:, pl.ds(start, own)] = parts[0:1] + parts[1:2] + parts[2:3]
    weight = weight_ref[...]
    product = jnp.sum(total * weight, axis=-1, keepdims=True)
    squares = jnp.sum(total * total, axis=-1, keepdims=True)
    score = product * lax.rsqrt(squares / features + EPS)
    row = lax.broadcasted_iota(jnp.int32, (count, LANES), 0)
    lane = lax.broadcasted_iota(jnp.int32, (count, LANES), 1)
    flat = jnp.sum(jnp.where(row == lane, score, 0.0), axis=0, keepdims=True)
    score_ref[...] = flat[:, :count]


def shards(
    hidden,
    attn_gain,
    q_weight,
    gate_weight,
    key_value_weight,
    q_gain,
    k_gain,
    out_weight,
    prompt_key_cache,
    prompt_value_cache,
    tail_key_cache,
    tail_value_cache,
    mlp_gain,
    mlp_gate,
    mlp_up,
    mlp_down,
    final_gain,
    score_weight,
    prompt_lengths,
    tail_lengths,
    group_prompt,
):
    head_count = lax.axis_size("head")
    group_count = lax.axis_size("req")
    count = hidden.shape[0]
    features = attn_gain.shape[0]
    width = q_gain.shape[0]
    own_cols = q_weight.shape[1]
    own_heads = own_cols // width
    kv_heads = prompt_key_cache.shape[2]
    cont_count = tail_lengths.shape[1]
    block = features // group_count
    hidden_units = mlp_gate.shape[1]
    smem = whole(pltpu.SMEM)
    facts = (prompt_lengths, tail_lengths.T, group_prompt)

    bits = [1 << i for i in range(head_count.bit_length() - 1)]
    req_bits = [1 << i for i in range(group_count.bit_length() - 1)]

    def like(x, *shape, dtype=BF16):
        return (tuple(shape) + x.shape[len(shape) :], dtype)

    rows = [hidden] + [swapped(hidden, "head", flip) for flip in range(1, head_count)]
    moved = (q_weight, key_value_weight)
    near_q, near_kv, turn = call(
        functools.partial(prepare_body, cont_count, count, len(moved)),
        [(x.shape, x.dtype) for x in moved] + [((2, count, width), F32)],
        [whole(pl.ANY)] * (len(moved) + 3),
        4,
        "prepare",
        read=2 * sum(x.size for x in moved),
        scratch=[
            pltpu.SMEM(facts[0].shape, jnp.int32),
            pltpu.SMEM(facts[1].shape, jnp.int32),
            pltpu.SMEM(facts[2].shape, jnp.int32),
            pltpu.SemaphoreType.DMA((3,)),
            pltpu.SemaphoreType.DMA((len(moved),)),
        ],
    )(*[in_hbm(x) for x in moved + facts])
    sent, normed, rows_share = call(
        functools.partial(project_body, head_count),
        [((1, 3 * count, own_cols), BF16), ((count, features), BF16), ((count, features), F32)],
        [whole()] * (head_count + 8),
        4,
        "project",
        flops=2 * count * features * own_cols * 2,
        read=4 * features * own_cols,
        scratch=[pltpu.VMEM((count, features), F32)],
    )(
        *rows,
        attn_gain.reshape(1, features),
        near_q,
        near_kv,
        q_gain.reshape(1, width),
        k_gain.reshape(1, width),
        turn,
        final_gain.reshape(1, -1),
        score_weight.reshape(1, -1),
    )
    near = sent
    for bit in bits[:-1]:
        joined = [like(near, 2 * near.shape[0])]
        (near,) = call(join_body, joined, [whole()] * 2, 4, "join")(
            near, swapped(near, "head", bit)
        )
    far = swapped(near, "head", bits[-1])
    (gate,) = call(
        gate_body,
        [((count, own_cols), F32)],
        [whole(), whole(pl.ANY)],
        4,
        "gate",
        flops=2 * count * features * own_cols,
        read=2 * features * own_cols,
        scratch=[pltpu.VMEM(gate_weight.shape, BF16), pltpu.SemaphoreType.DMA],
    )(normed, in_hbm(gate_weight))
    caches = [
        x.reshape(-1, width)
        for x in (tail_key_cache, tail_value_cache, prompt_key_cache, prompt_value_cache)
    ]
    early = caches[2].shape[0] // 2
    fetched = call(
        functools.partial(fetch_body, len(caches)),
        [(x.shape, BF16) for x in caches[:2]] + [((early, width), BF16)] * 2,
        [whole(pl.ANY)] * (1 + len(caches)),
        4,
        "fetch",
        read=2 * sum(x.size for x in caches) * 2 // 3,
        scratch=[pltpu.SemaphoreType.DMA((len(caches),))],
    )(near, *[in_hbm(x) for x in caches])
    pieces = head_count // 2
    sent, kept = call(
        functools.partial(attend_body, cont_count, kv_heads),
        [((pieces, own_heads * count, 2 * width), dtype) for dtype in (BF16, F32)],
        [whole()] * 2 + [smem] * 3 + [whole()] * 4 + [whole(pl.ANY)] * 2,
        12,
        "attend",
        flops=1 << 29,
        read=2 * caches[2].size,
        scratch=[pltpu.VMEM((2 * kv_heads, count, width), F32)]
        + [pltpu.VMEM((caches[2].shape[0] - early, width), BF16)] * 2
        + [pltpu.SemaphoreType.DMA((2,))],
    )(near, far, *facts, *fetched, *[in_hbm(x) for x in caches[2:]])
    for bit in bits[:-1]:
        pieces //= 2
        sent, kept = call(
            fold_body,
            [like(kept, pieces), like(kept, pieces, dtype=F32)],
            [whole()] * 2,
            4,
            "fold",
        )(kept, swapped(sent, "head", bit))
    (mixed,) = call(
        mix_body,
        [((group_count, count, block), BF16)],
        [whole()] * 5,
        4,
        "mix",
        flops=2 * count * features * own_cols,
        read=2 * features * own_cols,
    )(kept, swapped(sent, "head", bits[-1]), gate, rows_share, in_vmem(out_weight))

    def all_but_last_sum(x):
        for bit in bits[:-1]:
            (x,) = call(add_body, [like(x)], [whole()] * 2, 4, "add")(x, swapped(x, "head", bit))
        return x, swapped(x, "head", bits[-1])

    pieces, groups = group_count // 2, 1
    held, sent = call(
        deal_body,
        [((pieces, 1, count, block), BF16)] * 2,
        [whole()] * 2,
        4,
        "deal",
        scratch=[pltpu.VMEM((group_count, count, block), F32)],
    )(*all_but_last_sum(mixed))
    for bit in req_bits[:-1]:
        pieces, groups = pieces // 2, groups * 2
        held, sent = call(
            pass_body, [((pieces, groups, count, block), BF16)] * 2, [whole()] * 2, 4, "pass"
        )(held, swapped(sent, "req", bit))
    got = swapped(sent, "req", req_bits[-1])
    sums = 2 * hidden_units
    halved = halves(group_count)
    pieces = call(
        expand_body,
        [
            ((len(half), count, sums + block), dtype)
            for half in halved
            for dtype in (BF16, F32)
        ],
        [whole()] * 5 + [smem],
        8,
        "expand",
        flops=4 * count * group_count * block * hidden_units,
        read=4 * block * hidden_units,
        scratch=[pltpu.VMEM((group_count, count, block), F32)],
    )(
        held,
        got,
        mlp_gain.reshape(group_count, 1, block),
        in_vmem(mlp_gate),
        in_vmem(mlp_up),
        group_prompt,
    )
    sent_far, kept_far, sent_near, kept_near = pieces
    pair = ((count, sums + 2 * block), BF16)
    sent_near, *far_sums = call(
        functools.partial(pair_body, sums, True),
        [like(sent_near)] + [pair] * len(halved[0]),
        [whole()] * 3,
        4,
        "pair_far",
        read=4 * sent_far.size,
    )(swapped(sent_far, "req", 1), kept_far, sent_near)
    near_sums = call(
        functools.partial(pair_body, sums, False),
        [pair] * len(halved[1]),
        [whole()] * 2,
        4,
        "pair_near",
        read=4 * sent_near.size,
    )(swapped(sent_near, "req", 1), kept_near)
    flips = halved[0] + halved[1]
    summed = [
        swapped(x, "req", flip) if flip else x for flip, x in zip(flips, [*far_sums, *near_sums])
    ]
    (down,) = call(
        functools.partial(reduce_body, flips, head_count),
        [((group_count, count, block), BF16)],
        [whole()] * (len(summed) + 1),
        4,
        "reduce",
        flops=2 * count * features * hidden_units,
        read=2 * features * hidden_units,
        scratch=[pltpu.VMEM((len(summed), count, 2 * block), F32)],
    )(*summed, in_vmem(mlp_down))
    own = features // head_count
    new_hidden, score = call(
        finish_body,
        [((count, own), BF16), ((1, count), F32)],
        [whole()] * 4,
        4,
        "finish",
        outs_vmem=False,
        scratch=[pltpu.VMEM((count, features), F32), pltpu.VMEM((1, features), F32)],
    )(*all_but_last_sum(down), near, far)
    return (new_hidden, score.reshape(count))


def solution(mesh):
    return jax.shard_map(
        shards,
        mesh=mesh,
        in_specs=(
            P("req", "head"),
            P(),
            P(None, "head"),
            P(None, "head"),
            P(None, "head"),
            P(),
            P(),
            P("head", None),
            P("req", "head", None, None),
            P("req", "head", None, None),
            P("req", None, "head", None, None),
            P("req", None, "head", None, None),
            P(),
            P("req", "head"),
            P("req", "head"),
            P("head", None),
            P("head"),
            P("head"),
            P(),
            P(),
            P(),
        ),
        out_specs=(P("req", "head"), P("req")),
        check_vma=False,
    )
```

```python
import functools
import math

import jax
import jax.numpy as jnp
from jax import lax
from jax.experimental import pallas as pl
from jax.experimental.pallas import tpu as pltpu
from jax.sharding import PartitionSpec as P

EPS = 1e-06
THETA = 1000000.0
LANES = 128
BF16 = jnp.bfloat16
F32 = jnp.float32


def in_vmem(x):
    return pltpu.with_memory_space_constraint(x, pltpu.VMEM)


def whole(memory_space=pltpu.VMEM):
    return pl.BlockSpec(memory_space=memory_space)


def in_hbm(x):
    return pltpu.with_memory_space_constraint(x, pltpu.HBM)


def swapped(x, axis, flip):
    return lax.ppermute(x, axis, [(i, i ^ flip) for i in range(lax.axis_size(axis))])


def far_first(count):
    return [0] + list(reversed(range(1, count)))


def reversed_tail(pieces):
    return [pieces[0]] + list(reversed(pieces[1:]))


def around(pieces, axis):
    got = [
        swapped(piece, axis, flip) if flip else piece
        for flip, piece in zip(far_first(len(pieces)), pieces)
    ]
    return reversed_tail(got)


def partner(axis, slot):
    return lax.axis_index(axis) ^ slot


def call(body, outs, specs, limit_mib, name, flops=0, read=0, outs_vmem=True, scratch=()):
    shapes = [
        pltpu.VMEM(shape, dtype) if outs_vmem else jax.ShapeDtypeStruct(shape, dtype)
        for shape, dtype in outs
    ]
    return pl.pallas_call(
        body,
        out_shape=shapes,
        in_specs=specs,
        out_specs=[whole()] * len(outs),
        scratch_shapes=list(scratch),
        compiler_params=pltpu.CompilerParams(vmem_limit_bytes=limit_mib << 20),
        cost_estimate=pl.CostEstimate(flops=flops, bytes_accessed=read, transcendentals=0),
        name=name,
    )


def start_copies(sources, targets, sems):
    moves = [
        pltpu.make_async_copy(source, target, sems.at[i])
        for i, (source, target) in enumerate(zip(sources, targets))
    ]
    for move in moves:
        move.start()
    return moves


def prepare_body(cont_count, count, copies, *refs):
    sources, refs = refs[:copies], refs[copies:]
    facts_hbm, refs = refs[:3], refs[3:]
    targets, refs = refs[:copies], refs[copies:]
    turn_ref, limits_ref, prompts_ref, tails_ref, owners_ref, fact_sems, sems = refs
    facts = start_copies(facts_hbm, (prompts_ref, tails_ref, owners_ref), fact_sems)
    moves = start_copies(sources, targets, sems)
    for fact in facts:
        fact.wait()
    head_width = turn_ref.shape[2]
    new_count = count // cont_count
    prompt = owners_ref[lax.axis_index("req")]
    prompt_len = prompts_ref[prompt]
    row_of = lax.broadcasted_iota(jnp.int32, (count, head_width), 0)
    lane_of = lax.broadcasted_iota(jnp.int32, (count, head_width), 1)
    position = jnp.zeros((count, head_width), jnp.int32)
    limits_ref[0] = jnp.full((count, head_width), prompt_len, jnp.int32)
    for cont in range(cont_count):
        start = prompt_len + tails_ref[cont, prompt]
        limits_ref[1 + cont] = jnp.full((count, head_width), tails_ref[cont, prompt], jnp.int32)
        position = jnp.where(row_of // new_count == cont, start + row_of % new_count, position)
    half = head_width // 2
    frequency = jnp.exp((-math.log(THETA) * 2.0 / head_width) * (lane_of % half).astype(F32))
    angles = position.astype(F32) * frequency
    turn_ref[0] = jnp.cos(angles)
    turn_ref[1] = jnp.where(lane_of < half, -1.0, 1.0) * jnp.sin(angles)
    for move in moves:
        move.wait()


def project_body(slots, *refs):
    slot_refs, refs = refs[:slots], refs[slots:]
    gain_ref, q_ref, kv_ref, q_gain_ref, k_gain_ref, turn_ref = refs[:6]
    sent_ref, normed_ref, rows_out_ref, rows_ref = refs[6:]
    count, own = slot_refs[0].shape
    head_width = q_gain_ref.shape[1]
    half = head_width // 2
    for slot in range(slots):
        start = pl.multiple_of(partner("head", slot) * own, LANES)
        rows_ref[:, pl.ds(start, own)] = slot_refs[slot][...].astype(F32)
    cosine, sine = turn_ref[0], turn_ref[1]
    rows = rows_ref[...]
    rows_out_ref[...] = rows * (1.0 / slots)
    scale = lax.rsqrt(jnp.mean(rows * rows, axis=-1, keepdims=True) + EPS)
    normed = (rows * scale * gain_ref[...]).astype(BF16)
    normed_ref[...] = normed

    def keyed(block, gain):
        inverse = lax.rsqrt(jnp.mean(block * block, axis=-1, keepdims=True) + EPS)
        block = block * inverse * gain
        return block * cosine + pltpu.roll(block, half, 1) * sine

    queries = jnp.dot(normed, q_ref[...], preferred_element_type=F32)
    fresh = jnp.dot(normed, kv_ref[...], preferred_element_type=F32)
    block_count = kv_ref.shape[1] // head_width
    first_block = lax.axis_index("head") * block_count
    top, bottom = [], []
    for block in range(q_ref.shape[1] // head_width):
        top.append(
            keyed(queries[:, block * head_width : (block + 1) * head_width], q_gain_ref[...])
        )
    for block in range(block_count):
        plain = fresh[:, block * head_width : (block + 1) * head_width]
        is_key = (first_block + block) % 2 == 0
        bottom.append(jnp.where(is_key, keyed(plain, k_gain_ref[...]), plain))
    sent = jnp.concatenate(
        [jnp.concatenate(top, axis=1), jnp.concatenate(bottom, axis=1)], axis=0
    )
    sent_ref[...] = sent.astype(BF16)


def gate_body(normed_ref, weight_hbm, gate_ref, weight_ref, sem):
    move = pltpu.make_async_copy(weight_hbm, weight_ref, sem)
    move.start()
    move.wait()
    gate_ref[...] = jnp.dot(normed_ref[...], weight_ref[...], preferred_element_type=F32)


def split_parts(value):
    high = value.astype(BF16).astype(F32)
    middle = (value - high).astype(BF16).astype(F32)
    low = value - high - middle
    return [high, middle, low]


def attend_body(cont_count, kv_heads, slots, *refs):
    slot_refs, refs = refs[:slots], refs[slots:]
    (
        keys_ref,
        values_ref,
        tail_keys_ref,
        tail_values_ref,
        final_gain_ref,
        score_weight_ref,
        limits_ref,
    ) = refs[:7]
    out_refs, fresh_ref = refs[7 : 7 + slots], refs[7 + slots]
    count = slot_refs[0].shape[0] // 2
    width = keys_ref.shape[1]
    own_heads = slot_refs[0].shape[1] // width
    own_rows = own_heads * count
    all_heads = own_heads * slots
    sharing = all_heads // kv_heads
    new_count = count // cont_count
    head_place = lax.axis_index("head")
    queries = []
    for slot in range(slots):
        got = slot_refs[slot][...].astype(F32)
        source = partner("head", slot)
        for i in range(own_heads):
            piece = got[:, i * width : (i + 1) * width]
            queries.append(piece[:count])
            fresh_ref[source * own_heads + i] = piece[count:]
    queries = jnp.concatenate(queries, axis=0).astype(BF16)
    fresh_keys = jnp.concatenate([fresh_ref[2 * k] for k in range(kv_heads)], axis=0)
    fresh_values = jnp.concatenate([fresh_ref[2 * k + 1] for k in range(kv_heads)], axis=0)
    many = all_heads * count
    score_scale = 1.0 / math.sqrt(width)

    def part(keys, values, live):
        scores = lax.dot_general(
            queries, keys, (((1,), (1,)), ((), ())), preferred_element_type=F32
        )
        weights = jnp.where(live, jnp.exp(scores * score_scale), 0.0).astype(BF16)
        with_ones = jnp.concatenate([values, jnp.ones(values.shape, BF16)], axis=1)
        return jnp.dot(weights, with_ones, preferred_element_type=F32)

    def places(span):
        row = lax.broadcasted_iota(jnp.int32, (many, span), 0)
        lane = lax.broadcasted_iota(jnp.int32, (many, span), 1)
        place = head_place ^ (row // own_rows)
        head = place * own_heads + (row % own_rows) // count
        return row, lane, head // sharing

    total_rows = keys_ref.shape[0]
    step = min(1024, total_rows)
    row, lane, kv_of = places(step)
    matching = lane % kv_heads == kv_of
    left = (limits_ref[0][:1, :1] - head_place * (total_rows // kv_heads)) * kv_heads
    numer = jnp.zeros((many, 2 * width), F32)
    for start in range(0, total_rows, step):
        live = matching & (lane < left - start)
        numer += part(keys_ref[start : start + step, :], values_ref[start : start + step, :], live)

    tail_rows = tail_keys_ref.shape[0] // cont_count
    row, lane, kv_of = places(tail_rows)
    matching = lane % kv_heads == kv_of
    for cont in range(cont_count):
        left = (limits_ref[1 + cont][:1, :1] - head_place * (tail_rows // kv_heads)) * kv_heads
        live = matching & (lane < left) & ((row % count) // new_count == cont)
        start = cont * tail_rows
        numer += part(
            tail_keys_ref[start : start + tail_rows, :],
            tail_values_ref[start : start + tail_rows, :],
            live,
        )

    row, lane, kv_of = places(count * kv_heads)
    live = (
        (lane // count == kv_of)
        & ((lane % count) // new_count == (row % count) // new_count)
        & (lane % new_count <= row % new_count)
        & (head_place == 0)
    )
    numer += part(fresh_keys.astype(BF16), fresh_values.astype(BF16), live)

    product = final_gain_ref[...] * score_weight_ref[...]
    pieces = [
        p[:, i * LANES : (i + 1) * LANES]
        for p in split_parts(product)
        for i in range(product.shape[1] // LANES)
    ]
    filler = jnp.zeros((own_rows - len(pieces), LANES), F32)
    extra = jnp.concatenate(pieces + [filler], axis=0)
    for slot, out_ref in zip(far_first(slots), out_refs):
        mine = numer[slot * own_rows : (slot + 1) * own_rows, :]
        out_ref[...] = jnp.concatenate([mine, extra], axis=1).astype(BF16)


def mix_body(slots, *refs):
    got_refs = refs[:slots]
    gate_ref, rows_ref, weight_ref, out_ref = refs[slots:]
    own_rows = got_refs[0].shape[0]
    count = rows_ref.shape[0]
    width = LANES
    summed = got_refs[0][:, : 2 * width].astype(F32)
    for slot in range(1, slots):
        summed += got_refs[slot][:, : 2 * width].astype(F32)
    attention = summed[:, :width] / summed[:, width:]
    side_by_side = jnp.concatenate(
        [attention[i : i + count] for i in range(0, own_rows, count)], axis=1
    )
    gated = (side_by_side * jax.nn.sigmoid(gate_ref[...])).astype(BF16)
    mixed = jnp.dot(gated, weight_ref[...], preferred_element_type=F32)
    mixed += rows_ref[...]
    mixed = mixed.astype(BF16)
    places, copies, _, block = out_ref.shape
    for place in range(places):
        piece = mixed[:, place * block : (place + 1) * block]
        for copy in range(copies):
            out_ref[place, copy] = piece


def halves(places):
    middle = max(places // 2, 1)
    return list(range(middle, places, 2)), list(range(middle))


def expand_body(got_ref, gain_ref, gate_ref, up_ref, owners_ref, sent_ref, kept_ref, *near_refs):
    groups, sources, count, block = got_ref.shape
    far, near = halves(groups)
    order = [flip ^ 1 for flip in far] + far + near
    pieces = []
    for slot in order:
        group = jnp.int32(0)
        for i in range(groups):
            group = jnp.where(owners_ref[i] == partner("req", slot), i, group)
        got = got_ref[group]
        summed = got[0].astype(F32)
        for source in range(1, sources):
            summed += got[source].astype(F32)
        pieces.append(summed)
    attended = jnp.concatenate(pieces, axis=0).astype(BF16).astype(F32)
    scaled = (attended * gain_ref[lax.axis_index("req")]).astype(BF16)
    gate = jnp.dot(scaled, gate_ref[...], preferred_element_type=F32)
    up = jnp.dot(scaled, up_ref[...], preferred_element_type=F32)
    wide = jnp.concatenate([gate, up, attended], axis=1)
    places = [sent_ref.at[i] for i in range(len(far))] + [kept_ref.at[i] for i in range(len(far))]
    for i, place in enumerate(places + list(near_refs)):
        place[...] = wide[i * count : (i + 1) * count].astype(place.dtype)


def pair_body(sums, got_ref, kept_ref, *out_refs):
    odd = lax.axis_index("req") % 2 == 1
    for i, out_ref in enumerate(out_refs):
        got = got_ref[i].astype(F32)
        kept = kept_ref[i]
        first = jnp.where(odd, got[:, sums:], kept[:, sums:])
        second = jnp.where(odd, kept[:, sums:], got[:, sums:])
        both = [got[:, :sums] + kept[:, :sums], first, second]
        out_ref[...] = jnp.concatenate(both, axis=1).astype(out_ref.dtype)


def near_body(sums, *refs):
    got_refs, total_ref, blocks_ref = refs[:-2], refs[-2], refs[-1]
    total = got_refs[0][:, :sums].astype(F32)
    for got_ref in got_refs[1:]:
        total += got_ref[:, :sums].astype(F32)
    total_ref[...] = total
    for i, got_ref in enumerate(got_refs):
        blocks_ref[i] = got_ref[:, sums:].astype(F32)


def reduce_body(far, near, sources, *refs):
    got_refs = refs[: len(far)]
    near_ref, blocks_ref, weight_ref, out_ref, attended_ref = refs[len(far) :]
    hidden_units = weight_ref.shape[0]
    sums = 2 * hidden_units
    total = near_ref[...]
    for got_ref in got_refs:
        total += got_ref[:, :sums].astype(F32)
    block = attended_ref.shape[2]
    for i, flip in enumerate(near):
        attended_ref[partner("req", flip)] = blocks_ref[i]
    for flip, got_ref in zip(far, got_refs):
        first = lax.shift_left(lax.shift_right_logical(partner("req", flip), 1), 1)
        attended_ref[first] = got_ref[:, sums : sums + block].astype(F32)
        attended_ref[first + 1] = got_ref[:, sums + block :].astype(F32)
    attended = jnp.concatenate([attended_ref[i] for i in range(attended_ref.shape[0])], axis=1)
    scale = lax.rsqrt(jnp.mean(attended * attended, axis=-1, keepdims=True) + EPS)
    gate = total[:, :hidden_units] * scale
    up = total[:, hidden_units:] * scale
    act = (gate * jax.nn.sigmoid(gate) * up).astype(BF16)
    down = jnp.dot(act, weight_ref[...], preferred_element_type=F32)
    out_ref[...] = (down + attended * (1.0 / sources)).astype(BF16)


def finish_body(slots, *refs):
    got_refs, part_refs = refs[:slots], refs[slots : 2 * slots]
    new_ref, score_ref, total_ref, whole_ref, weight_ref = refs[2 * slots :]
    count, features = got_refs[0].shape
    own = new_ref.shape[1]
    pieces = own // LANES
    for slot in range(slots):
        source = partner("head", slot)
        total_ref[source] = got_refs[slot][...].astype(F32)
        extra = part_refs[slot][:, 2 * LANES :].astype(F32)
        for i in range(pieces):
            start = pl.multiple_of(source * own + i * LANES, LANES)
            weight_ref[:, pl.ds(start, LANES)] = (
                extra[i : i + 1]
                + extra[pieces + i : pieces + i + 1]
                + extra[2 * pieces + i : 2 * pieces + i + 1]
            )
    total = total_ref[0]
    for source in range(1, slots):
        total += total_ref[source]
    total = total.astype(BF16).astype(F32)
    whole_ref[...] = total
    start = pl.multiple_of(lax.axis_index("head") * own, LANES)
    new_ref[...] = whole_ref[:, pl.ds(start, own)].astype(BF16)
    weight = weight_ref[...]
    product = jnp.sum(total * weight, axis=-1, keepdims=True)
    squares = jnp.sum(total * total, axis=-1, keepdims=True)
    score = product * lax.rsqrt(squares / features + EPS)
    row = lax.broadcasted_iota(jnp.int32, (count, LANES), 0)
    lane = lax.broadcasted_iota(jnp.int32, (count, LANES), 1)
    flat = jnp.sum(jnp.where(row == lane, score, 0.0), axis=0, keepdims=True)
    score_ref[...] = flat[:, :count]


def shards(
    hidden,
    attn_gain,
    q_weight,
    gate_weight,
    key_value_weight,
    q_gain,
    k_gain,
    out_weight,
    prompt_key_cache,
    prompt_value_cache,
    tail_key_cache,
    tail_value_cache,
    mlp_gain,
    mlp_gate,
    mlp_up,
    mlp_down,
    final_gain,
    score_weight,
    prompt_lengths,
    tail_lengths,
    group_prompt,
):
    head_count = lax.axis_size("head")
    group_count = lax.axis_size("req")
    count = hidden.shape[0]
    features = attn_gain.shape[0]
    width = q_gain.shape[0]
    own_cols = q_weight.shape[1]
    own_heads = own_cols // width
    kv_heads = prompt_key_cache.shape[2]
    cont_count = tail_lengths.shape[1]
    block = features // group_count
    hidden_units = mlp_gate.shape[1]
    smem = whole(pltpu.SMEM)
    facts = (prompt_lengths, tail_lengths.T, group_prompt)

    rows = around([hidden] * head_count, "head")[1:]
    moved = (
        q_weight,
        key_value_weight,
        hidden,
        attn_gain.reshape(1, features),
        q_gain.reshape(1, width),
        k_gain.reshape(1, width),
        final_gain.reshape(1, -1),
        score_weight.reshape(1, -1),
    )
    near_q, near_kv, own_rows, gain, near_q_gain, near_k_gain, last_gain, last_weight, *rest = call(
        functools.partial(prepare_body, cont_count, count, len(moved)),
        [(x.shape, x.dtype) for x in moved]
        + [((2, count, width), F32), ((1 + cont_count, count, width), jnp.int32)],
        [whole(pl.ANY)] * (len(moved) + 3),
        4,
        "prepare",
        read=2 * sum(x.size for x in moved),
        scratch=[
            pltpu.SMEM(facts[0].shape, jnp.int32),
            pltpu.SMEM(facts[1].shape, jnp.int32),
            pltpu.SMEM(facts[2].shape, jnp.int32),
            pltpu.SemaphoreType.DMA((3,)),
            pltpu.SemaphoreType.DMA((len(moved),)),
        ],
    )(*[in_hbm(x) for x in moved + facts])
    turn, limits = rest
    sent, normed, rows_share = call(
        functools.partial(project_body, head_count),
        [((2 * count, own_cols), BF16), ((count, features), BF16), ((count, features), F32)],
        [whole()] * (head_count + 6),
        4,
        "project",
        flops=2 * count * features * own_cols * 2,
        read=4 * features * own_cols,
        scratch=[pltpu.VMEM((count, features), F32)],
    )(
        own_rows,
        *rows,
        gain,
        near_q,
        near_kv,
        near_q_gain,
        near_k_gain,
        turn,
    )
    got = around([sent] * head_count, "head")
    (gate,) = call(
        gate_body,
        [((count, own_cols), F32)],
        [whole(), whole(pl.ANY)],
        4,
        "gate",
        flops=2 * count * features * own_cols,
        read=2 * features * own_cols,
        scratch=[pltpu.VMEM(gate_weight.shape, BF16), pltpu.SemaphoreType.DMA],
    )(normed, in_hbm(gate_weight))
    caches = [
        x.reshape(-1, width)
        for x in (prompt_key_cache, prompt_value_cache, tail_key_cache, tail_value_cache)
    ]
    parts = call(
        functools.partial(attend_body, cont_count, kv_heads, head_count),
        [((own_heads * count, 2 * width + LANES), BF16)] * head_count,
        [whole()] * (head_count + 7),
        8,
        "attend",
        flops=1 << 29,
        read=4 * prompt_key_cache.size,
        scratch=[pltpu.VMEM((2 * kv_heads, count, width), F32)],
    )(
        *got,
        *[in_vmem(x) for x in caches],
        last_gain,
        last_weight,
        limits,
    )
    parts = around(parts, "head")
    (mixed,) = call(
        functools.partial(mix_body, head_count),
        [((group_count, head_count, count, block), BF16)],
        [whole()] * (head_count + 3),
        4,
        "mix",
        flops=2 * count * features * own_cols,
        read=2 * features * own_cols,
    )(*reversed_tail(parts), gate, rows_share, in_vmem(out_weight))
    mixed = mixed.reshape(group_count * head_count, count, block)
    mixed = lax.all_to_all(mixed, ("req", "head"), split_axis=0, concat_axis=0, tiled=True)
    mixed = mixed.reshape(group_count, head_count, count, block)
    sums = 2 * hidden_units
    far, near = halves(group_count)
    sent, kept, *near_pieces = call(
        expand_body,
        [((len(far), count, sums + block), dtype) for dtype in (BF16, F32)]
        + [((count, sums + block), BF16)] * len(near),
        [whole()] * 4 + [smem],
        8,
        "expand",
        flops=4 * count * group_count * block * hidden_units,
        read=4 * block * hidden_units,
    )(
        mixed,
        mlp_gain.reshape(group_count, 1, block),
        in_vmem(mlp_gate),
        in_vmem(mlp_up),
        group_prompt,
    )
    pairs = call(
        functools.partial(pair_body, sums),
        [((count, sums + 2 * block), BF16)] * len(far),
        [whole()] * 2,
        4,
        "pair",
        read=4 * sent.size,
    )(swapped(sent, "req", 1), kept)
    near_sums = call(
        functools.partial(near_body, sums),
        [((count, sums), F32), ((len(near), count, block), F32)],
        [whole()] * len(near),
        4,
        "near",
        read=16 << 20,
    )(*[swapped(x, "req", flip) if flip else x for flip, x in zip(near, near_pieces)])
    (down,) = call(
        functools.partial(reduce_body, far, near, head_count),
        [((count, features), BF16)],
        [whole()] * (len(far) + 3),
        4,
        "reduce",
        flops=2 * count * features * hidden_units,
        read=2 * features * hidden_units,
        scratch=[pltpu.VMEM((group_count, count, block), F32)],
    )(*[swapped(x, "req", flip) for flip, x in zip(far, pairs)], *near_sums, in_vmem(mlp_down))
    own = features // head_count
    new_hidden, score = call(
        functools.partial(finish_body, head_count),
        [((count, own), BF16), ((1, count), F32)],
        [whole()] * (2 * head_count),
        4,
        "finish",
        outs_vmem=False,
        scratch=[
            pltpu.VMEM((head_count, count, features), F32),
            pltpu.VMEM((count, features), F32),
            pltpu.VMEM((1, features), F32),
        ],
    )(*around([down] * head_count, "head"), *parts)
    return (new_hidden, score.reshape(count))


def solution(mesh):
    return jax.shard_map(
        shards,
        mesh=mesh,
        in_specs=(
            P("req", "head"),
            P(),
            P(None, "head"),
            P(None, "head"),
            P(None, "head"),
            P(),
            P(),
            P("head", None),
            P("req", "head", None, None),
            P("req", "head", None, None),
            P("req", None, "head", None, None),
            P("req", None, "head", None, None),
            P(),
            P("req", "head"),
            P("req", "head"),
            P("head", None),
            P("head"),
            P("head"),
            P(),
            P(),
            P(),
        ),
        out_specs=(P("req", "head"), P("req")),
        check_vma=False,
    )
```

```python
import functools
import math

import jax
import jax.numpy as jnp
from jax import lax
from jax.experimental import pallas as pl
from jax.experimental.pallas import tpu as pltpu
from jax.sharding import PartitionSpec as P

EPS = 1e-06
THETA = 1000000.0
LANES = 128
BF16 = jnp.bfloat16
F32 = jnp.float32


def in_vmem(x):
    return pltpu.with_memory_space_constraint(x, pltpu.VMEM)


def whole(memory_space=pltpu.VMEM):
    return pl.BlockSpec(memory_space=memory_space)


def in_hbm(x):
    return pltpu.with_memory_space_constraint(x, pltpu.HBM)


def swapped(x, axis, flip):
    return lax.ppermute(x, axis, [(i, i ^ flip) for i in range(lax.axis_size(axis))])


def far_first(count):
    return [0] + list(reversed(range(1, count)))


def reversed_tail(pieces):
    return [pieces[0]] + list(reversed(pieces[1:]))


def around(pieces, axis):
    got = [
        swapped(piece, axis, flip) if flip else piece
        for flip, piece in zip(far_first(len(pieces)), pieces)
    ]
    return reversed_tail(got)


def partner(axis, slot):
    return lax.axis_index(axis) ^ slot


def call(body, outs, specs, limit_mib, name, flops=0, read=0, outs_vmem=True, scratch=()):
    shapes = [
        pltpu.VMEM(shape, dtype) if outs_vmem else jax.ShapeDtypeStruct(shape, dtype)
        for shape, dtype in outs
    ]
    return pl.pallas_call(
        body,
        out_shape=shapes,
        in_specs=specs,
        out_specs=[whole()] * len(outs),
        scratch_shapes=list(scratch),
        compiler_params=pltpu.CompilerParams(vmem_limit_bytes=limit_mib << 20),
        cost_estimate=pl.CostEstimate(flops=flops, bytes_accessed=read, transcendentals=0),
        name=name,
    )


def start_copies(sources, targets, sems):
    moves = [
        pltpu.make_async_copy(source, target, sems.at[i])
        for i, (source, target) in enumerate(zip(sources, targets))
    ]
    for move in moves:
        move.start()
    return moves


def prepare_body(cont_count, count, copies, *refs):
    sources, refs = refs[:copies], refs[copies:]
    facts_hbm, refs = refs[:3], refs[3:]
    targets, refs = refs[:copies], refs[copies:]
    turn_ref, limits_ref, prompts_ref, tails_ref, owners_ref, fact_sems, sems = refs
    facts = start_copies(facts_hbm, (prompts_ref, tails_ref, owners_ref), fact_sems)
    moves = start_copies(sources, targets, sems)
    for fact in facts:
        fact.wait()
    head_width = turn_ref.shape[2]
    new_count = count // cont_count
    prompt = owners_ref[lax.axis_index("req")]
    prompt_len = prompts_ref[prompt]
    row_of = lax.broadcasted_iota(jnp.int32, (count, head_width), 0)
    lane_of = lax.broadcasted_iota(jnp.int32, (count, head_width), 1)
    position = jnp.zeros((count, head_width), jnp.int32)
    limits_ref[0] = jnp.full((count, head_width), prompt_len, jnp.int32)
    for cont in range(cont_count):
        start = prompt_len + tails_ref[cont, prompt]
        limits_ref[1 + cont] = jnp.full((count, head_width), tails_ref[cont, prompt], jnp.int32)
        position = jnp.where(row_of // new_count == cont, start + row_of % new_count, position)
    half = head_width // 2
    frequency = jnp.exp((-math.log(THETA) * 2.0 / head_width) * (lane_of % half).astype(F32))
    angles = position.astype(F32) * frequency
    turn_ref[0] = jnp.cos(angles)
    turn_ref[1] = jnp.where(lane_of < half, -1.0, 1.0) * jnp.sin(angles)
    for move in moves:
        move.wait()


def project_body(slots, *refs):
    slot_refs, refs = refs[:slots], refs[slots:]
    gain_ref, q_ref, kv_ref, q_gain_ref, k_gain_ref, turn_ref = refs[:6]
    sent_ref, normed_ref, rows_out_ref, rows_ref = refs[6:]
    count, own = slot_refs[0].shape
    head_width = q_gain_ref.shape[1]
    half = head_width // 2
    for slot in range(slots):
        start = pl.multiple_of(partner("head", slot) * own, LANES)
        rows_ref[:, pl.ds(start, own)] = slot_refs[slot][...].astype(F32)
    cosine, sine = turn_ref[0], turn_ref[1]
    rows = rows_ref[...]
    rows_out_ref[...] = rows * (1.0 / slots)
    scale = lax.rsqrt(jnp.mean(rows * rows, axis=-1, keepdims=True) + EPS)
    normed = (rows * scale * gain_ref[...]).astype(BF16)
    normed_ref[...] = normed

    def keyed(block, gain):
        inverse = lax.rsqrt(jnp.mean(block * block, axis=-1, keepdims=True) + EPS)
        block = block * inverse * gain
        return block * cosine + pltpu.roll(block, half, 1) * sine

    queries = jnp.dot(normed, q_ref[...], preferred_element_type=F32)
    fresh = jnp.dot(normed, kv_ref[...], preferred_element_type=F32)
    block_count = kv_ref.shape[1] // head_width
    first_block = lax.axis_index("head") * block_count
    top, bottom = [], []
    for block in range(q_ref.shape[1] // head_width):
        top.append(
            keyed(queries[:, block * head_width : (block + 1) * head_width], q_gain_ref[...])
        )
    for block in range(block_count):
        plain = fresh[:, block * head_width : (block + 1) * head_width]
        is_key = (first_block + block) % 2 == 0
        bottom.append(jnp.where(is_key, keyed(plain, k_gain_ref[...]), plain))
    sent = jnp.concatenate(
        [jnp.concatenate(top, axis=1), jnp.concatenate(bottom, axis=1)], axis=0
    )
    sent_ref[...] = sent.astype(BF16)


def gate_body(normed_ref, weight_hbm, gate_ref, weight_ref, sem):
    move = pltpu.make_async_copy(weight_hbm, weight_ref, sem)
    move.start()
    move.wait()
    gate_ref[...] = jnp.dot(normed_ref[...], weight_ref[...], preferred_element_type=F32)


def split_parts(value):
    high = value.astype(BF16).astype(F32)
    middle = (value - high).astype(BF16).astype(F32)
    low = value - high - middle
    return [high, middle, low]


def attend_body(cont_count, kv_heads, slots, *refs):
    slot_refs, refs = refs[:slots], refs[slots:]
    (
        keys_ref,
        values_ref,
        tail_keys_ref,
        tail_values_ref,
        final_gain_ref,
        score_weight_ref,
        limits_ref,
    ) = refs[:7]
    out_refs, fresh_ref = refs[7 : 7 + slots], refs[7 + slots]
    count = slot_refs[0].shape[0] // 2
    width = keys_ref.shape[1]
    own_heads = slot_refs[0].shape[1] // width
    own_rows = own_heads * count
    all_heads = own_heads * slots
    sharing = all_heads // kv_heads
    new_count = count // cont_count
    head_place = lax.axis_index("head")
    queries = []
    for slot in range(slots):
        got = slot_refs[slot][...].astype(F32)
        source = partner("head", slot)
        for i in range(own_heads):
            piece = got[:, i * width : (i + 1) * width]
            queries.append(piece[:count])
            fresh_ref[source * own_heads + i] = piece[count:]
    queries = jnp.concatenate(queries, axis=0).astype(BF16)
    fresh_keys = jnp.concatenate([fresh_ref[2 * k] for k in range(kv_heads)], axis=0)
    fresh_values = jnp.concatenate([fresh_ref[2 * k + 1] for k in range(kv_heads)], axis=0)
    many = all_heads * count
    score_scale = 1.0 / math.sqrt(width)

    def part(keys, values, live):
        scores = lax.dot_general(
            queries, keys, (((1,), (1,)), ((), ())), preferred_element_type=F32
        )
        weights = jnp.where(live, jnp.exp(scores * score_scale), 0.0).astype(BF16)
        with_ones = jnp.concatenate([values, jnp.ones(values.shape, BF16)], axis=1)
        return jnp.dot(weights, with_ones, preferred_element_type=F32)

    def places(span):
        row = lax.broadcasted_iota(jnp.int32, (many, span), 0)
        lane = lax.broadcasted_iota(jnp.int32, (many, span), 1)
        place = head_place ^ (row // own_rows)
        head = place * own_heads + (row % own_rows) // count
        return row, lane, head // sharing

    total_rows = keys_ref.shape[0]
    step = min(1024, total_rows)
    row, lane, kv_of = places(step)
    matching = lane % kv_heads == kv_of
    left = (limits_ref[0][:1, :1] - head_place * (total_rows // kv_heads)) * kv_heads
    numer = jnp.zeros((many, 2 * width), F32)
    for start in range(0, total_rows, step):
        live = matching & (lane < left - start)
        numer += part(keys_ref[start : start + step, :], values_ref[start : start + step, :], live)

    tail_rows = tail_keys_ref.shape[0] // cont_count
    row, lane, kv_of = places(tail_rows)
    matching = lane % kv_heads == kv_of
    for cont in range(cont_count):
        left = (limits_ref[1 + cont][:1, :1] - head_place * (tail_rows // kv_heads)) * kv_heads
        live = matching & (lane < left) & ((row % count) // new_count == cont)
        start = cont * tail_rows
        numer += part(
            tail_keys_ref[start : start + tail_rows, :],
            tail_values_ref[start : start + tail_rows, :],
            live,
        )

    row, lane, kv_of = places(count * kv_heads)
    live = (
        (lane // count == kv_of)
        & ((lane % count) // new_count == (row % count) // new_count)
        & (lane % new_count <= row % new_count)
        & (head_place == 0)
    )
    numer += part(fresh_keys.astype(BF16), fresh_values.astype(BF16), live)

    product = final_gain_ref[...] * score_weight_ref[...]
    pieces = [
        p[:, i * LANES : (i + 1) * LANES]
        for p in split_parts(product)
        for i in range(product.shape[1] // LANES)
    ]
    filler = jnp.zeros((own_rows - len(pieces), LANES), F32)
    extra = jnp.concatenate(pieces + [filler], axis=0)
    for slot, out_ref in zip(far_first(slots), out_refs):
        mine = numer[slot * own_rows : (slot + 1) * own_rows, :]
        out_ref[...] = jnp.concatenate([mine, extra], axis=1).astype(BF16)


def mix_body(slots, *refs):
    got_refs = refs[:slots]
    gate_ref, rows_ref, weight_ref, out_ref = refs[slots:]
    own_rows = got_refs[0].shape[0]
    count = rows_ref.shape[0]
    width = LANES
    summed = got_refs[0][:, : 2 * width].astype(F32)
    for slot in range(1, slots):
        summed += got_refs[slot][:, : 2 * width].astype(F32)
    attention = summed[:, :width] / summed[:, width:]
    side_by_side = jnp.concatenate(
        [attention[i : i + count] for i in range(0, own_rows, count)], axis=1
    )
    gated = (side_by_side * jax.nn.sigmoid(gate_ref[...])).astype(BF16)
    mixed = jnp.dot(gated, weight_ref[...], preferred_element_type=F32)
    mixed += rows_ref[...]
    mixed = mixed.astype(BF16)
    places, copies, _, block = out_ref.shape
    for place in range(places):
        piece = mixed[:, place * block : (place + 1) * block]
        for copy in range(copies):
            out_ref[place, copy] = piece


def halves(places):
    middle = max(places // 2, 1)
    return list(range(middle, places, 2)), list(range(0, middle, 2))


def expand_body(got_ref, gain_ref, gate_ref, up_ref, owners_ref, *out_refs):
    groups, sources, count, block = got_ref.shape
    flips = [half for half in halves(groups)]
    order = [flip ^ bit for half in flips for bit in (1, 0) for flip in half]
    pieces = []
    for slot in order:
        group = jnp.int32(0)
        for i in range(groups):
            group = jnp.where(owners_ref[i] == partner("req", slot), i, group)
        got = got_ref[group]
        summed = got[0].astype(F32)
        for source in range(1, sources):
            summed += got[source].astype(F32)
        pieces.append(summed)
    attended = jnp.concatenate(pieces, axis=0).astype(BF16).astype(F32)
    scaled = (attended * gain_ref[lax.axis_index("req")]).astype(BF16)
    gate = jnp.dot(scaled, gate_ref[...], preferred_element_type=F32)
    up = jnp.dot(scaled, up_ref[...], preferred_element_type=F32)
    wide = jnp.concatenate([gate, up, attended], axis=1)
    start = 0
    for out_ref in out_refs:
        for i in range(out_ref.shape[0]):
            out_ref[i] = wide[start : start + count].astype(out_ref.dtype)
            start += count


def pair_body(sums, got_ref, kept_ref, *out_refs):
    odd = lax.axis_index("req") % 2 == 1
    for i, out_ref in enumerate(out_refs):
        got = got_ref[i].astype(F32)
        kept = kept_ref[i]
        first = jnp.where(odd, got[:, sums:], kept[:, sums:])
        second = jnp.where(odd, kept[:, sums:], got[:, sums:])
        both = [got[:, :sums] + kept[:, :sums], first, second]
        out_ref[...] = jnp.concatenate(both, axis=1).astype(out_ref.dtype)


def reduce_body(flips, sources, *refs):
    got_refs = refs[: len(flips)]
    weight_ref, out_ref, attended_ref = refs[len(flips) :]
    hidden_units = weight_ref.shape[0]
    total = got_refs[0][:, : 2 * hidden_units].astype(F32)
    for got_ref in got_refs[1:]:
        total += got_ref[:, : 2 * hidden_units].astype(F32)
    for flip, got_ref in zip(flips, got_refs):
        attended_ref[partner("req", flip) // 2] = got_ref[:, 2 * hidden_units :].astype(F32)
    attended = jnp.concatenate([attended_ref[i] for i in range(len(flips))], axis=1)
    scale = lax.rsqrt(jnp.mean(attended * attended, axis=-1, keepdims=True) + EPS)
    gate = total[:, :hidden_units] * scale
    up = total[:, hidden_units:] * scale
    act = (gate * jax.nn.sigmoid(gate) * up).astype(BF16)
    down = jnp.dot(act, weight_ref[...], preferred_element_type=F32)
    out_ref[...] = (down + attended * (1.0 / sources)).astype(BF16)


def finish_body(slots, *refs):
    got_refs, part_refs = refs[:slots], refs[slots : 2 * slots]
    new_ref, score_ref, total_ref, whole_ref, weight_ref = refs[2 * slots :]
    count, features = got_refs[0].shape
    own = new_ref.shape[1]
    pieces = own // LANES
    for slot in range(slots):
        source = partner("head", slot)
        total_ref[source] = got_refs[slot][...].astype(F32)
        extra = part_refs[slot][:, 2 * LANES :].astype(F32)
        for i in range(pieces):
            start = pl.multiple_of(source * own + i * LANES, LANES)
            weight_ref[:, pl.ds(start, LANES)] = (
                extra[i : i + 1]
                + extra[pieces + i : pieces + i + 1]
                + extra[2 * pieces + i : 2 * pieces + i + 1]
            )
    total = total_ref[0]
    for source in range(1, slots):
        total += total_ref[source]
    total = total.astype(BF16).astype(F32)
    whole_ref[...] = total
    start = pl.multiple_of(lax.axis_index("head") * own, LANES)
    new_ref[...] = whole_ref[:, pl.ds(start, own)].astype(BF16)
    weight = weight_ref[...]
    product = jnp.sum(total * weight, axis=-1, keepdims=True)
    squares = jnp.sum(total * total, axis=-1, keepdims=True)
    score = product * lax.rsqrt(squares / features + EPS)
    row = lax.broadcasted_iota(jnp.int32, (count, LANES), 0)
    lane = lax.broadcasted_iota(jnp.int32, (count, LANES), 1)
    flat = jnp.sum(jnp.where(row == lane, score, 0.0), axis=0, keepdims=True)
    score_ref[...] = flat[:, :count]


def shards(
    hidden,
    attn_gain,
    q_weight,
    gate_weight,
    key_value_weight,
    q_gain,
    k_gain,
    out_weight,
    prompt_key_cache,
    prompt_value_cache,
    tail_key_cache,
    tail_value_cache,
    mlp_gain,
    mlp_gate,
    mlp_up,
    mlp_down,
    final_gain,
    score_weight,
    prompt_lengths,
    tail_lengths,
    group_prompt,
):
    head_count = lax.axis_size("head")
    group_count = lax.axis_size("req")
    count = hidden.shape[0]
    features = attn_gain.shape[0]
    width = q_gain.shape[0]
    own_cols = q_weight.shape[1]
    own_heads = own_cols // width
    kv_heads = prompt_key_cache.shape[2]
    cont_count = tail_lengths.shape[1]
    block = features // group_count
    hidden_units = mlp_gate.shape[1]
    smem = whole(pltpu.SMEM)
    facts = (prompt_lengths, tail_lengths.T, group_prompt)

    rows = around([hidden] * head_count, "head")[1:]
    moved = (
        q_weight,
        key_value_weight,
        hidden,
        attn_gain.reshape(1, features),
        q_gain.reshape(1, width),
        k_gain.reshape(1, width),
        final_gain.reshape(1, -1),
        score_weight.reshape(1, -1),
    )
    near_q, near_kv, own_rows, gain, near_q_gain, near_k_gain, last_gain, last_weight, *rest = call(
        functools.partial(prepare_body, cont_count, count, len(moved)),
        [(x.shape, x.dtype) for x in moved]
        + [((2, count, width), F32), ((1 + cont_count, count, width), jnp.int32)],
        [whole(pl.ANY)] * (len(moved) + 3),
        4,
        "prepare",
        read=2 * sum(x.size for x in moved),
        scratch=[
            pltpu.SMEM(facts[0].shape, jnp.int32),
            pltpu.SMEM(facts[1].shape, jnp.int32),
            pltpu.SMEM(facts[2].shape, jnp.int32),
            pltpu.SemaphoreType.DMA((3,)),
            pltpu.SemaphoreType.DMA((len(moved),)),
        ],
    )(*[in_hbm(x) for x in moved + facts])
    turn, limits = rest
    sent, normed, rows_share = call(
        functools.partial(project_body, head_count),
        [((2 * count, own_cols), BF16), ((count, features), BF16), ((count, features), F32)],
        [whole()] * (head_count + 6),
        4,
        "project",
        flops=2 * count * features * own_cols * 2,
        read=4 * features * own_cols,
        scratch=[pltpu.VMEM((count, features), F32)],
    )(
        own_rows,
        *rows,
        gain,
        near_q,
        near_kv,
        near_q_gain,
        near_k_gain,
        turn,
    )
    got = around([sent] * head_count, "head")
    (gate,) = call(
        gate_body,
        [((count, own_cols), F32)],
        [whole(), whole(pl.ANY)],
        4,
        "gate",
        flops=2 * count * features * own_cols,
        read=2 * features * own_cols,
        scratch=[pltpu.VMEM(gate_weight.shape, BF16), pltpu.SemaphoreType.DMA],
    )(normed, in_hbm(gate_weight))
    caches = [
        x.reshape(-1, width)
        for x in (prompt_key_cache, prompt_value_cache, tail_key_cache, tail_value_cache)
    ]
    parts = call(
        functools.partial(attend_body, cont_count, kv_heads, head_count),
        [((own_heads * count, 2 * width + LANES), BF16)] * head_count,
        [whole()] * (head_count + 7),
        8,
        "attend",
        flops=1 << 29,
        read=4 * prompt_key_cache.size,
        scratch=[pltpu.VMEM((2 * kv_heads, count, width), F32)],
    )(
        *got,
        *[in_vmem(x) for x in caches],
        last_gain,
        last_weight,
        limits,
    )
    parts = around(parts, "head")
    (mixed,) = call(
        functools.partial(mix_body, head_count),
        [((group_count, head_count, count, block), BF16)],
        [whole()] * (head_count + 3),
        4,
        "mix",
        flops=2 * count * features * own_cols,
        read=2 * features * own_cols,
    )(*reversed_tail(parts), gate, rows_share, in_vmem(out_weight))
    mixed = mixed.reshape(group_count * head_count, count, block)
    mixed = lax.all_to_all(mixed, ("req", "head"), split_axis=0, concat_axis=0, tiled=True)
    mixed = mixed.reshape(group_count, head_count, count, block)
    sums = 2 * hidden_units
    far, near = halves(group_count)
    pieces = call(
        expand_body,
        [
            ((len(half), count, sums + block), dtype)
            for half in (far, near)
            for dtype in (BF16, F32)
        ],
        [whole()] * 4 + [smem],
        8,
        "expand",
        flops=4 * count * group_count * block * hidden_units,
        read=4 * block * hidden_units,
    )(
        mixed,
        mlp_gain.reshape(group_count, 1, block),
        in_vmem(mlp_gate),
        in_vmem(mlp_up),
        group_prompt,
    )
    summed = []
    for half, sent, kept in ((far, *pieces[:2]), (near, *pieces[2:])):
        pairs = call(
            functools.partial(pair_body, sums),
            [((count, sums + 2 * block), BF16)] * len(half),
            [whole()] * 2,
            4,
            "pair",
            read=4 * sent.size,
        )(swapped(sent, "req", 1), kept)
        for flip, pair in zip(half, pairs):
            summed.append(swapped(pair, "req", flip) if flip else pair)
    (down,) = call(
        functools.partial(reduce_body, far + near, head_count),
        [((count, features), BF16)],
        [whole()] * (len(summed) + 1),
        4,
        "reduce",
        flops=2 * count * features * hidden_units,
        read=2 * features * hidden_units,
        scratch=[pltpu.VMEM((len(summed), count, 2 * block), F32)],
    )(*summed, in_vmem(mlp_down))
    own = features // head_count
    new_hidden, score = call(
        functools.partial(finish_body, head_count),
        [((count, own), BF16), ((1, count), F32)],
        [whole()] * (2 * head_count),
        4,
        "finish",
        outs_vmem=False,
        scratch=[
            pltpu.VMEM((head_count, count, features), F32),
            pltpu.VMEM((count, features), F32),
            pltpu.VMEM((1, features), F32),
        ],
    )(*around([down] * head_count, "head"), *parts)
    return (new_hidden, score.reshape(count))


def solution(mesh):
    return jax.shard_map(
        shards,
        mesh=mesh,
        in_specs=(
            P("req", "head"),
            P(),
            P(None, "head"),
            P(None, "head"),
            P(None, "head"),
            P(),
            P(),
            P("head", None),
            P("req", "head", None, None),
            P("req", "head", None, None),
            P("req", None, "head", None, None),
            P("req", None, "head", None, None),
            P(),
            P("req", "head"),
            P("req", "head"),
            P("head", None),
            P("head"),
            P("head"),
            P(),
            P(),
            P(),
        ),
        out_specs=(P("req", "head"), P("req")),
        check_vma=False,
    )
```

```python
import functools
import math

import jax
import jax.numpy as jnp
from jax import lax
from jax.experimental import pallas as pl
from jax.experimental.pallas import tpu as pltpu
from jax.sharding import PartitionSpec as P

EPS = 1e-06
THETA = 1000000.0
LANES = 128
BF16 = jnp.bfloat16
F32 = jnp.float32


def in_vmem(x):
    return pltpu.with_memory_space_constraint(x, pltpu.VMEM)


def whole(memory_space=pltpu.VMEM):
    return pl.BlockSpec(memory_space=memory_space)


def in_hbm(x):
    return pltpu.with_memory_space_constraint(x, pltpu.HBM)


def swapped(x, axis, flip):
    return lax.ppermute(x, axis, [(i, i ^ flip) for i in range(lax.axis_size(axis))])


def far_first(count):
    return [0] + list(reversed(range(1, count)))


def reversed_tail(pieces):
    return [pieces[0]] + list(reversed(pieces[1:]))


def around(pieces, axis):
    got = [
        swapped(piece, axis, flip) if flip else piece
        for flip, piece in zip(far_first(len(pieces)), pieces)
    ]
    return reversed_tail(got)


def partner(axis, slot):
    return lax.axis_index(axis) ^ slot


def call(body, outs, specs, limit_mib, name, flops=0, read=0, outs_vmem=True, scratch=()):
    shapes = [
        pltpu.VMEM(shape, dtype) if outs_vmem else jax.ShapeDtypeStruct(shape, dtype)
        for shape, dtype in outs
    ]
    return pl.pallas_call(
        body,
        out_shape=shapes,
        in_specs=specs,
        out_specs=[whole()] * len(outs),
        scratch_shapes=list(scratch),
        compiler_params=pltpu.CompilerParams(vmem_limit_bytes=limit_mib << 20),
        cost_estimate=pl.CostEstimate(flops=flops, bytes_accessed=read, transcendentals=0),
        name=name,
    )


def start_copies(sources, targets, sems):
    moves = [
        pltpu.make_async_copy(source, target, sems.at[i])
        for i, (source, target) in enumerate(zip(sources, targets))
    ]
    for move in moves:
        move.start()
    return moves


def prepare_body(cont_count, count, copies, *refs):
    sources, refs = refs[:copies], refs[copies:]
    facts_hbm, refs = refs[:3], refs[3:]
    targets, refs = refs[:copies], refs[copies:]
    turn_ref, limits_ref, prompts_ref, tails_ref, owners_ref, fact_sems, sems = refs
    facts = start_copies(facts_hbm, (prompts_ref, tails_ref, owners_ref), fact_sems)
    moves = start_copies(sources, targets, sems)
    for fact in facts:
        fact.wait()
    head_width = turn_ref.shape[2]
    new_count = count // cont_count
    prompt = owners_ref[lax.axis_index("req")]
    prompt_len = prompts_ref[prompt]
    row_of = lax.broadcasted_iota(jnp.int32, (count, head_width), 0)
    lane_of = lax.broadcasted_iota(jnp.int32, (count, head_width), 1)
    position = jnp.zeros((count, head_width), jnp.int32)
    limits_ref[0] = jnp.full((count, head_width), prompt_len, jnp.int32)
    for cont in range(cont_count):
        start = prompt_len + tails_ref[cont, prompt]
        limits_ref[1 + cont] = jnp.full((count, head_width), tails_ref[cont, prompt], jnp.int32)
        position = jnp.where(row_of // new_count == cont, start + row_of % new_count, position)
    half = head_width // 2
    frequency = jnp.exp((-math.log(THETA) * 2.0 / head_width) * (lane_of % half).astype(F32))
    angles = position.astype(F32) * frequency
    turn_ref[0] = jnp.cos(angles)
    turn_ref[1] = jnp.where(lane_of < half, -1.0, 1.0) * jnp.sin(angles)
    for move in moves:
        move.wait()


def keyed(block, gain, turn_ref):
    inverse = lax.rsqrt(jnp.mean(block * block, axis=-1, keepdims=True) + EPS)
    block = block * inverse * gain
    return block * turn_ref[0] + pltpu.roll(block, block.shape[1] // 2, 1) * turn_ref[1]


def project_body(slots, *refs):
    slot_refs, refs = refs[:slots], refs[slots:]
    gain_ref, q_ref, q_gain_ref, turn_ref = refs[:4]
    sent_ref, normed_ref, rows_out_ref, rows_ref = refs[4:]
    own = slot_refs[0].shape[1]
    head_width = q_gain_ref.shape[1]
    for slot in range(slots):
        start = pl.multiple_of(partner("head", slot) * own, LANES)
        rows_ref[:, pl.ds(start, own)] = slot_refs[slot][...].astype(F32)
    rows = rows_ref[...]
    rows_out_ref[...] = rows * (1.0 / slots)
    scale = lax.rsqrt(jnp.mean(rows * rows, axis=-1, keepdims=True) + EPS)
    normed = (rows * scale * gain_ref[...]).astype(BF16)
    normed_ref[...] = normed
    queries = jnp.dot(normed, q_ref[...], preferred_element_type=F32)
    heads = [
        keyed(queries[:, start : start + head_width], q_gain_ref[...], turn_ref)
        for start in range(0, q_ref.shape[1], head_width)
    ]
    sent_ref[...] = jnp.concatenate(heads, axis=1).astype(BF16)


def fresh_body(normed_ref, gain_ref, turn_ref, weight_hbm, out_ref, weight_ref, sem):
    move = pltpu.make_async_copy(weight_hbm, weight_ref, sem)
    move.start()
    move.wait()
    projected = jnp.dot(normed_ref[...], weight_ref[...], preferred_element_type=F32)
    blocks, _, head_width = out_ref.shape
    first_block = lax.axis_index("head") * blocks
    for block in range(blocks):
        plain = projected[:, block * head_width : (block + 1) * head_width]
        is_key = (first_block + block) % 2 == 0
        turned = keyed(plain, gain_ref[...], turn_ref)
        out_ref[block] = jnp.where(is_key, turned, plain).astype(BF16)


def gate_body(normed_ref, weight_hbm, gate_ref, weight_ref, sem):
    move = pltpu.make_async_copy(weight_hbm, weight_ref, sem)
    move.start()
    move.wait()
    gate_ref[...] = jnp.dot(normed_ref[...], weight_ref[...], preferred_element_type=F32)


def split_parts(value):
    high = value.astype(BF16).astype(F32)
    middle = (value - high).astype(BF16).astype(F32)
    low = value - high - middle
    return [high, middle, low]


def attend_body(cont_count, kv_heads, slots, *refs):
    slot_refs, refs = refs[:slots], refs[slots:]
    (
        keys_ref,
        values_ref,
        tail_keys_ref,
        tail_values_ref,
        final_gain_ref,
        score_weight_ref,
        limits_ref,
        fresh_ref,
        other_ref,
    ) = refs[:9]
    out_refs = refs[9:]
    count = slot_refs[0].shape[0]
    width = keys_ref.shape[1]
    own_heads = slot_refs[0].shape[1] // width
    own_rows = own_heads * count
    all_heads = own_heads * slots
    sharing = all_heads // kv_heads
    new_count = count // cont_count
    head_place = lax.axis_index("head")
    queries = []
    for slot in range(slots):
        got = slot_refs[slot][...].astype(F32)
        queries += [got[:, i * width : (i + 1) * width] for i in range(own_heads)]
    queries = jnp.concatenate(queries, axis=0).astype(BF16)
    blocks = fresh_ref.shape[0]
    if blocks % 2:
        own, other = fresh_ref[0].astype(F32), other_ref[0].astype(F32)
        even = head_place % 2 == 0
        fresh_keys, fresh_values = jnp.where(even, own, other), jnp.where(even, other, own)
    else:
        pairs = range(0, blocks, 2)
        fresh_keys = jnp.concatenate([fresh_ref[i].astype(F32) for i in pairs], axis=0)
        fresh_values = jnp.concatenate([fresh_ref[i + 1].astype(F32) for i in pairs], axis=0)
    many = all_heads * count
    score_scale = 1.0 / math.sqrt(width)

    def part(keys, values, live):
        rows = queries[: live.shape[0]]
        scores = lax.dot_general(
            rows, keys, (((1,), (1,)), ((), ())), preferred_element_type=F32
        )
        weights = jnp.where(live, jnp.exp(scores * score_scale), 0.0).astype(BF16)
        with_ones = jnp.concatenate([values, jnp.ones(values.shape, BF16)], axis=1)
        return jnp.dot(weights, with_ones, preferred_element_type=F32)

    def places(span):
        row = lax.broadcasted_iota(jnp.int32, (many, span), 0)
        lane = lax.broadcasted_iota(jnp.int32, (many, span), 1)
        place = head_place ^ (row // own_rows)
        head = place * own_heads + (row % own_rows) // count
        return row, lane, head // sharing

    total_rows = keys_ref.shape[0]
    step = min(1024, total_rows)
    row, lane, kv_of = places(step)
    matching = lane % kv_heads == kv_of
    left = (limits_ref[0][:1, :1] - head_place * (total_rows // kv_heads)) * kv_heads
    numer = jnp.zeros((many, 2 * width), F32)
    for start in range(0, total_rows, step):
        live = matching & (lane < left - start)
        numer += part(keys_ref[start : start + step, :], values_ref[start : start + step, :], live)

    tail_rows = tail_keys_ref.shape[0] // cont_count
    row, lane, kv_of = places(tail_rows)
    matching = lane % kv_heads == kv_of
    for cont in range(cont_count):
        left = (limits_ref[1 + cont][:1, :1] - head_place * (tail_rows // kv_heads)) * kv_heads
        live = matching & (lane < left) & ((row % count) // new_count == cont)
        start = cont * tail_rows
        numer += part(
            tail_keys_ref[start : start + tail_rows, :],
            tail_values_ref[start : start + tail_rows, :],
            live,
        )

    shape = (own_rows, fresh_keys.shape[0])
    row = lax.broadcasted_iota(jnp.int32, shape, 0)
    lane = lax.broadcasted_iota(jnp.int32, shape, 1)
    live = (
        (lane // count == row // (count * sharing))
        & ((lane % count) // new_count == (row % count) // new_count)
        & (lane % new_count <= row % new_count)
    )
    own_numer = part(fresh_keys.astype(BF16), fresh_values.astype(BF16), live)

    product = final_gain_ref[...] * score_weight_ref[...]
    pieces = [
        p[:, i * LANES : (i + 1) * LANES]
        for p in split_parts(product)
        for i in range(product.shape[1] // LANES)
    ]
    filler = jnp.zeros((own_rows - len(pieces), LANES), F32)
    extra = jnp.concatenate(pieces + [filler], axis=0)
    for slot, out_ref in zip(far_first(slots), out_refs):
        mine = numer[slot * own_rows : (slot + 1) * own_rows, :]
        mine = mine if slot else mine + own_numer
        out_ref[...] = jnp.concatenate([mine, extra], axis=1).astype(BF16)


def mix_body(slots, *refs):
    got_refs = refs[:slots]
    gate_ref, rows_ref, weight_ref, out_ref = refs[slots:]
    own_rows = got_refs[0].shape[0]
    count = rows_ref.shape[0]
    width = LANES
    summed = got_refs[0][:, : 2 * width].astype(F32)
    for slot in range(1, slots):
        summed += got_refs[slot][:, : 2 * width].astype(F32)
    attention = summed[:, :width] / summed[:, width:]
    side_by_side = jnp.concatenate(
        [attention[i : i + count] for i in range(0, own_rows, count)], axis=1
    )
    gated = (side_by_side * jax.nn.sigmoid(gate_ref[...])).astype(BF16)
    mixed = jnp.dot(gated, weight_ref[...], preferred_element_type=F32)
    mixed += rows_ref[...]
    mixed = mixed.astype(BF16)
    places, copies, _, block = out_ref.shape
    for place in range(places):
        piece = mixed[:, place * block : (place + 1) * block]
        for copy in range(copies):
            out_ref[place, copy] = piece


def halves(places):
    middle = max(places // 2, 1)
    return list(range(middle, places, 2)), list(range(0, middle, 2))


def widths(block, sources):
    share = block // sources
    return share, pl.cdiv(share + 2, LANES) * LANES, pl.cdiv(2 * share + 2, LANES) * LANES


def two_parts(value):
    high = value.astype(BF16).astype(F32)
    return [high, value - high]


def padded(pieces, width):
    filled = sum(piece.shape[1] for piece in pieces)
    filler = jnp.zeros((pieces[0].shape[0], width - filled), F32)
    return jnp.concatenate(pieces + [filler], axis=1)


def expand_body(got_ref, gain_ref, gate_ref, up_ref, owners_ref, *refs):
    out_refs, group_of_ref = refs[:-1], refs[-1]
    groups, sources, count, block = got_ref.shape
    for i in range(groups):
        group_of_ref[owners_ref[i]] = i
    order = [flip ^ bit for half in halves(groups) for bit in (1, 0) for flip in half]
    pieces = []
    for slot in order:
        got = got_ref[group_of_ref[partner("req", slot)]]
        summed = got[0].astype(F32)
        for source in range(1, sources):
            summed += got[source].astype(F32)
        pieces.append(summed)
    attended = jnp.concatenate(pieces, axis=0).astype(BF16).astype(F32)
    scaled = (attended * gain_ref[lax.axis_index("req")]).astype(BF16)
    gate = jnp.dot(scaled, gate_ref[...], preferred_element_type=F32)
    up = jnp.dot(scaled, up_ref[...], preferred_element_type=F32)
    share, extra, _ = widths(block, sources)
    mine = jnp.zeros((attended.shape[0], share), F32)
    for i in range(sources):
        piece = attended[:, i * share : (i + 1) * share]
        mine = jnp.where(lax.axis_index("head") == i, piece, mine)
    squares = jnp.sum(attended * attended, axis=-1, keepdims=True)
    beside = padded([mine] + two_parts(squares), extra)
    wide = jnp.concatenate([gate, up, beside], axis=1)
    start = 0
    for out_ref in out_refs:
        for i in range(out_ref.shape[0]):
            out_ref[i] = wide[start : start + count].astype(out_ref.dtype)
            start += count


def pair_body(sums, share, got_ref, kept_ref, *out_refs):
    odd = lax.axis_index("req") % 2 == 1
    for i, out_ref in enumerate(out_refs):
        got = got_ref[i].astype(F32)
        kept = kept_ref[i]
        added = got + kept
        got, kept = got[:, sums : sums + share], kept[:, sums : sums + share]
        first, second = jnp.where(odd, got, kept), jnp.where(odd, kept, got)
        beside = added[:, sums:]
        squares = beside[:, share : share + 1] + beside[:, share + 1 : share + 2]
        beside = padded([first, second] + two_parts(squares), out_ref.shape[1] - sums)
        out_ref[...] = jnp.concatenate([added[:, :sums], beside], axis=1).astype(out_ref.dtype)


def reduce_body(flips, sources, share, *refs):
    got_refs = refs[: len(flips)]
    weight_ref, out_ref, shares_ref = refs[len(flips) :]
    hidden_units, features = weight_ref.shape
    sums = 2 * hidden_units
    total = got_refs[0][...].astype(F32)
    for got_ref in got_refs[1:]:
        total += got_ref[...].astype(F32)
    for flip, got_ref in zip(flips, got_refs):
        first = lax.shift_left(lax.shift_right_logical(partner("req", flip), 1), 1)
        beside = got_ref[:, sums:].astype(F32)
        shares_ref[first] = beside[:, :share]
        shares_ref[first + 1] = beside[:, share : 2 * share]
    at = sums + 2 * share
    squares = total[:, at : at + 1] + total[:, at + 1 : at + 2]
    scale = lax.rsqrt(squares / features + EPS)
    gate = total[:, :hidden_units] * scale
    up = total[:, hidden_units:sums] * scale
    act = (gate * jax.nn.sigmoid(gate) * up).astype(BF16)
    down = jnp.dot(act, weight_ref[...], preferred_element_type=F32)
    residual = jnp.concatenate(
        [
            jnp.where(lax.axis_index("head") == i, shares_ref[place], 0.0)
            for place in range(shares_ref.shape[0])
            for i in range(sources)
        ],
        axis=1,
    )
    out_ref[...] = (down + residual).astype(BF16)


def finish_body(slots, *refs):
    got_refs, part_refs = refs[:slots], refs[slots : 2 * slots]
    new_ref, score_ref, total_ref, whole_ref, weight_ref = refs[2 * slots :]
    count, features = got_refs[0].shape
    own = new_ref.shape[1]
    pieces = own // LANES
    for slot in range(slots):
        source = partner("head", slot)
        total_ref[source] = got_refs[slot][...].astype(F32)
        extra = part_refs[slot][:, 2 * LANES :].astype(F32)
        for i in range(pieces):
            start = pl.multiple_of(source * own + i * LANES, LANES)
            weight_ref[:, pl.ds(start, LANES)] = (
                extra[i : i + 1]
                + extra[pieces + i : pieces + i + 1]
                + extra[2 * pieces + i : 2 * pieces + i + 1]
            )
    total = total_ref[0]
    for source in range(1, slots):
        total += total_ref[source]
    total = total.astype(BF16).astype(F32)
    whole_ref[...] = total
    start = pl.multiple_of(lax.axis_index("head") * own, LANES)
    new_ref[...] = whole_ref[:, pl.ds(start, own)].astype(BF16)
    weight = weight_ref[...]
    product = jnp.sum(total * weight, axis=-1, keepdims=True)
    squares = jnp.sum(total * total, axis=-1, keepdims=True)
    score = product * lax.rsqrt(squares / features + EPS)
    row = lax.broadcasted_iota(jnp.int32, (count, LANES), 0)
    lane = lax.broadcasted_iota(jnp.int32, (count, LANES), 1)
    flat = jnp.sum(jnp.where(row == lane, score, 0.0), axis=0, keepdims=True)
    score_ref[...] = flat[:, :count]


def shards(
    hidden,
    attn_gain,
    q_weight,
    gate_weight,
    key_value_weight,
    q_gain,
    k_gain,
    out_weight,
    prompt_key_cache,
    prompt_value_cache,
    tail_key_cache,
    tail_value_cache,
    mlp_gain,
    mlp_gate,
    mlp_up,
    mlp_down,
    final_gain,
    score_weight,
    prompt_lengths,
    tail_lengths,
    group_prompt,
):
    head_count = lax.axis_size("head")
    group_count = lax.axis_size("req")
    count = hidden.shape[0]
    features = attn_gain.shape[0]
    width = q_gain.shape[0]
    own_cols = q_weight.shape[1]
    own_heads = own_cols // width
    kv_heads = prompt_key_cache.shape[2]
    cont_count = tail_lengths.shape[1]
    block = features // group_count
    hidden_units = mlp_gate.shape[1]
    smem = whole(pltpu.SMEM)
    facts = (prompt_lengths, tail_lengths.T, group_prompt)

    rows = around([hidden] * head_count, "head")[1:]
    moved = (
        q_weight,
        hidden,
        attn_gain.reshape(1, features),
        q_gain.reshape(1, width),
        k_gain.reshape(1, width),
        final_gain.reshape(1, -1),
        score_weight.reshape(1, -1),
    )
    near_q, own_rows, gain, near_q_gain, near_k_gain, last_gain, last_weight, *rest = call(
        functools.partial(prepare_body, cont_count, count, len(moved)),
        [(x.shape, x.dtype) for x in moved]
        + [((2, count, width), F32), ((1 + cont_count, count, width), jnp.int32)],
        [whole(pl.ANY)] * (len(moved) + 3),
        4,
        "prepare",
        read=2 * sum(x.size for x in moved),
        scratch=[
            pltpu.SMEM(facts[0].shape, jnp.int32),
            pltpu.SMEM(facts[1].shape, jnp.int32),
            pltpu.SMEM(facts[2].shape, jnp.int32),
            pltpu.SemaphoreType.DMA((3,)),
            pltpu.SemaphoreType.DMA((len(moved),)),
        ],
    )(*[in_hbm(x) for x in moved + facts])
    turn, limits = rest
    sent, normed, rows_share = call(
        functools.partial(project_body, head_count),
        [((count, own_cols), BF16), ((count, features), BF16), ((count, features), F32)],
        [whole()] * (head_count + 4),
        4,
        "project",
        flops=2 * count * features * own_cols,
        read=2 * features * own_cols,
        scratch=[pltpu.VMEM((count, features), F32)],
    )(
        own_rows,
        *rows,
        gain,
        near_q,
        near_q_gain,
        turn,
    )
    blocks = key_value_weight.shape[1] // width
    (fresh,) = call(
        fresh_body,
        [((blocks, count, width), BF16)],
        [whole()] * 3 + [whole(pl.ANY)],
        4,
        "fresh",
        flops=2 * count * features * own_cols,
        read=2 * features * own_cols,
        scratch=[pltpu.VMEM(key_value_weight.shape, BF16), pltpu.SemaphoreType.DMA],
    )(normed, near_k_gain, turn, in_hbm(key_value_weight))
    other = swapped(fresh, "head", 1) if blocks % 2 else fresh
    got = around([sent] * head_count, "head")
    (gate,) = call(
        gate_body,
        [((count, own_cols), F32)],
        [whole(), whole(pl.ANY)],
        4,
        "gate",
        flops=2 * count * features * own_cols,
        read=2 * features * own_cols,
        scratch=[pltpu.VMEM(gate_weight.shape, BF16), pltpu.SemaphoreType.DMA],
    )(normed, in_hbm(gate_weight))
    caches = [
        x.reshape(-1, width)
        for x in (prompt_key_cache, prompt_value_cache, tail_key_cache, tail_value_cache)
    ]
    parts = call(
        functools.partial(attend_body, cont_count, kv_heads, head_count),
        [((own_heads * count, 2 * width + LANES), BF16)] * head_count,
        [whole()] * (head_count + 9),
        8,
        "attend",
        flops=1 << 29,
        read=4 * prompt_key_cache.size,
    )(
        *got,
        *[in_vmem(x) for x in caches],
        last_gain,
        last_weight,
        limits,
        fresh,
        other,
    )
    parts = around(parts, "head")
    (mixed,) = call(
        functools.partial(mix_body, head_count),
        [((group_count, head_count, count, block), BF16)],
        [whole()] * (head_count + 3),
        4,
        "mix",
        flops=2 * count * features * own_cols,
        read=2 * features * own_cols,
    )(*reversed_tail(parts), gate, rows_share, in_vmem(out_weight))
    mixed = mixed.reshape(group_count * head_count, count, block)
    mixed = lax.all_to_all(mixed, ("req", "head"), split_axis=0, concat_axis=0, tiled=True)
    mixed = mixed.reshape(group_count, head_count, count, block)
    sums = 2 * hidden_units
    share, extra, pair_extra = widths(block, head_count)
    far, near = halves(group_count)
    pieces = call(
        expand_body,
        [
            ((len(half), count, sums + extra), dtype)
            for half in (far, near)
            for dtype in (BF16, F32)
        ],
        [whole()] * 4 + [smem],
        8,
        "expand",
        flops=4 * count * group_count * block * hidden_units,
        read=4 * block * hidden_units,
        scratch=[pltpu.SMEM((group_count,), jnp.int32)],
    )(
        mixed,
        mlp_gain.reshape(group_count, 1, block),
        in_vmem(mlp_gate),
        in_vmem(mlp_up),
        group_prompt,
    )
    summed = []
    for half, sent, kept in ((far, *pieces[:2]), (near, *pieces[2:])):
        pairs = call(
            functools.partial(pair_body, sums, share),
            [((count, sums + pair_extra), BF16)] * len(half),
            [whole()] * 2,
            4,
            "pair",
            read=4 * sent.size,
        )(swapped(sent, "req", 1), kept)
        for flip, pair in zip(half, pairs):
            summed.append(swapped(pair, "req", flip) if flip else pair)
    (down,) = call(
        functools.partial(reduce_body, far + near, head_count, share),
        [((count, features), BF16)],
        [whole()] * (len(summed) + 1),
        4,
        "reduce",
        flops=2 * count * features * hidden_units,
        read=2 * features * hidden_units,
        scratch=[pltpu.VMEM((group_count, count, share), F32)],
    )(*summed, in_vmem(mlp_down))
    own = features // head_count
    new_hidden, score = call(
        functools.partial(finish_body, head_count),
        [((count, own), BF16), ((1, count), F32)],
        [whole()] * (2 * head_count),
        4,
        "finish",
        outs_vmem=False,
        scratch=[
            pltpu.VMEM((head_count, count, features), F32),
            pltpu.VMEM((count, features), F32),
            pltpu.VMEM((1, features), F32),
        ],
    )(*around([down] * head_count, "head"), *parts)
    return (new_hidden, score.reshape(count))


def solution(mesh):
    return jax.shard_map(
        shards,
        mesh=mesh,
        in_specs=(
            P("req", "head"),
            P(),
            P(None, "head"),
            P(None, "head"),
            P(None, "head"),
            P(),
            P(),
            P("head", None),
            P("req", "head", None, None),
            P("req", "head", None, None),
            P("req", None, "head", None, None),
            P("req", None, "head", None, None),
            P(),
            P("req", "head"),
            P("req", "head"),
            P("head", None),
            P("head"),
            P("head"),
            P(),
            P(),
            P(),
        ),
        out_specs=(P("req", "head"), P("req")),
        check_vma=False,
    )
```

```python
import functools
import math

import jax
import jax.numpy as jnp
from jax import lax
from jax.experimental import pallas as pl
from jax.experimental.pallas import tpu as pltpu
from jax.sharding import PartitionSpec as P

EPS = 1e-06
THETA = 1000000.0
LANES = 128
BF16 = jnp.bfloat16
F32 = jnp.float32


def in_vmem(x):
    return pltpu.with_memory_space_constraint(x, pltpu.VMEM)


def whole(memory_space=pltpu.VMEM):
    return pl.BlockSpec(memory_space=memory_space)


def in_hbm(x):
    return pltpu.with_memory_space_constraint(x, pltpu.HBM)


def swapped(x, axis, flip):
    return lax.ppermute(x, axis, [(i, i ^ flip) for i in range(lax.axis_size(axis))])


def far_first(count):
    return [0] + list(reversed(range(1, count)))


def reversed_tail(pieces):
    return [pieces[0]] + list(reversed(pieces[1:]))


def around(pieces, axis):
    got = [
        swapped(piece, axis, flip) if flip else piece
        for flip, piece in zip(far_first(len(pieces)), pieces)
    ]
    return reversed_tail(got)


def partner(axis, slot):
    return lax.axis_index(axis) ^ slot


def turned(flip):
    return (flip & ~3) | ((flip & 1) << 1) | ((flip >> 1) & 1)


def crossed(x, flip):
    groups, places = lax.axis_size("req"), lax.axis_size("head")
    pairs = [
        (i * places + j, (i ^ (turned(flip) if j % 2 else flip)) * places + j)
        for i in range(groups)
        for j in range(places)
    ]
    return lax.ppermute(x, ("req", "head"), pairs)


def own_flip(flip):
    return jnp.where(lax.axis_index("head") % 2 == 1, turned(flip), flip)


def call(body, outs, specs, limit_mib, name, flops=0, read=0, outs_vmem=True, scratch=()):
    shapes = [
        pltpu.VMEM(shape, dtype) if outs_vmem else jax.ShapeDtypeStruct(shape, dtype)
        for shape, dtype in outs
    ]
    return pl.pallas_call(
        body,
        out_shape=shapes,
        in_specs=specs,
        out_specs=[whole()] * len(outs),
        scratch_shapes=list(scratch),
        compiler_params=pltpu.CompilerParams(vmem_limit_bytes=limit_mib << 20),
        cost_estimate=pl.CostEstimate(flops=flops, bytes_accessed=read, transcendentals=0),
        name=name,
    )


def start_copies(sources, targets, sems):
    moves = [
        pltpu.make_async_copy(source, target, sems.at[i])
        for i, (source, target) in enumerate(zip(sources, targets))
    ]
    for move in moves:
        move.start()
    return moves


def prepare_body(cont_count, count, copies, *refs):
    sources, refs = refs[:copies], refs[copies:]
    facts_hbm, refs = refs[:3], refs[3:]
    targets, refs = refs[:copies], refs[copies:]
    turn_ref, limits_ref, prompts_ref, tails_ref, owners_ref, fact_sems, sems = refs
    facts = start_copies(facts_hbm, (prompts_ref, tails_ref, owners_ref), fact_sems)
    moves = start_copies(sources, targets, sems)
    for fact in facts:
        fact.wait()
    head_width = turn_ref.shape[2]
    new_count = count // cont_count
    prompt = owners_ref[lax.axis_index("req")]
    prompt_len = prompts_ref[prompt]
    row_of = lax.broadcasted_iota(jnp.int32, (count, head_width), 0)
    lane_of = lax.broadcasted_iota(jnp.int32, (count, head_width), 1)
    position = jnp.zeros((count, head_width), jnp.int32)
    limits_ref[0] = jnp.full((count, head_width), prompt_len, jnp.int32)
    for cont in range(cont_count):
        start = prompt_len + tails_ref[cont, prompt]
        limits_ref[1 + cont] = jnp.full((count, head_width), tails_ref[cont, prompt], jnp.int32)
        position = jnp.where(row_of // new_count == cont, start + row_of % new_count, position)
    half = head_width // 2
    frequency = jnp.exp((-math.log(THETA) * 2.0 / head_width) * (lane_of % half).astype(F32))
    angles = position.astype(F32) * frequency
    turn_ref[0] = jnp.cos(angles)
    turn_ref[1] = jnp.where(lane_of < half, -1.0, 1.0) * jnp.sin(angles)
    for move in moves:
        move.wait()


def keyed(block, gain, turn_ref):
    inverse = lax.rsqrt(jnp.mean(block * block, axis=-1, keepdims=True) + EPS)
    block = block * inverse * gain
    return block * turn_ref[0] + pltpu.roll(block, block.shape[1] // 2, 1) * turn_ref[1]


def project_body(slots, *refs):
    slot_refs, refs = refs[:slots], refs[slots:]
    gain_ref, q_ref, q_gain_ref, turn_ref = refs[:4]
    sent_ref, normed_ref, rows_out_ref, rows_ref = refs[4:]
    own = slot_refs[0].shape[1]
    head_width = q_gain_ref.shape[1]
    for slot in range(slots):
        start = pl.multiple_of(partner("head", slot) * own, LANES)
        rows_ref[:, pl.ds(start, own)] = slot_refs[slot][...].astype(F32)
    rows = rows_ref[...]
    rows_out_ref[...] = rows * (1.0 / slots)
    scale = lax.rsqrt(jnp.mean(rows * rows, axis=-1, keepdims=True) + EPS)
    normed = (rows * scale * gain_ref[...]).astype(BF16)
    normed_ref[...] = normed
    queries = jnp.dot(normed, q_ref[...], preferred_element_type=F32)
    heads = [
        keyed(queries[:, start : start + head_width], q_gain_ref[...], turn_ref)
        for start in range(0, q_ref.shape[1], head_width)
    ]
    sent_ref[...] = jnp.concatenate(heads, axis=1).astype(BF16)


def fresh_body(normed_ref, gain_ref, turn_ref, weight_hbm, out_ref, weight_ref, sem):
    move = pltpu.make_async_copy(weight_hbm, weight_ref, sem)
    move.start()
    move.wait()
    projected = jnp.dot(normed_ref[...], weight_ref[...], preferred_element_type=F32)
    blocks, _, head_width = out_ref.shape
    first_block = lax.axis_index("head") * blocks
    for block in range(blocks):
        plain = projected[:, block * head_width : (block + 1) * head_width]
        is_key = (first_block + block) % 2 == 0
        turned = keyed(plain, gain_ref[...], turn_ref)
        out_ref[block] = jnp.where(is_key, turned, plain).astype(BF16)


def gate_body(normed_ref, weight_hbm, gate_ref, weight_ref, sem):
    move = pltpu.make_async_copy(weight_hbm, weight_ref, sem)
    move.start()
    move.wait()
    gate_ref[...] = jnp.dot(normed_ref[...], weight_ref[...], preferred_element_type=F32)


def split_parts(value):
    high = value.astype(BF16).astype(F32)
    middle = (value - high).astype(BF16).astype(F32)
    low = value - high - middle
    return [high, middle, low]


def attend_body(cont_count, kv_heads, slots, *refs):
    slot_refs, refs = refs[:slots], refs[slots:]
    (
        keys_ref,
        values_ref,
        tail_keys_ref,
        tail_values_ref,
        final_gain_ref,
        score_weight_ref,
        limits_ref,
        fresh_ref,
        other_ref,
    ) = refs[:9]
    out_refs = refs[9:]
    count = slot_refs[0].shape[0]
    width = keys_ref.shape[1]
    own_heads = slot_refs[0].shape[1] // width
    own_rows = own_heads * count
    all_heads = own_heads * slots
    sharing = all_heads // kv_heads
    new_count = count // cont_count
    head_place = lax.axis_index("head")
    queries = []
    for slot in range(slots):
        got = slot_refs[slot][...].astype(F32)
        queries += [got[:, i * width : (i + 1) * width] for i in range(own_heads)]
    queries = jnp.concatenate(queries, axis=0).astype(BF16)
    blocks = fresh_ref.shape[0]
    if blocks % 2:
        own, other = fresh_ref[0].astype(F32), other_ref[0].astype(F32)
        even = head_place % 2 == 0
        fresh_keys, fresh_values = jnp.where(even, own, other), jnp.where(even, other, own)
    else:
        pairs = range(0, blocks, 2)
        fresh_keys = jnp.concatenate([fresh_ref[i].astype(F32) for i in pairs], axis=0)
        fresh_values = jnp.concatenate([fresh_ref[i + 1].astype(F32) for i in pairs], axis=0)
    many = all_heads * count
    score_scale = 1.0 / math.sqrt(width)

    def part(keys, values, live):
        rows = queries[: live.shape[0]]
        scores = lax.dot_general(
            rows, keys, (((1,), (1,)), ((), ())), preferred_element_type=F32
        )
        weights = jnp.where(live, jnp.exp(scores * score_scale), 0.0).astype(BF16)
        with_ones = jnp.concatenate([values, jnp.ones(values.shape, BF16)], axis=1)
        return jnp.dot(weights, with_ones, preferred_element_type=F32)

    def places(span):
        row = lax.broadcasted_iota(jnp.int32, (many, span), 0)
        lane = lax.broadcasted_iota(jnp.int32, (many, span), 1)
        place = head_place ^ (row // own_rows)
        head = place * own_heads + (row % own_rows) // count
        return row, lane, head // sharing

    total_rows = keys_ref.shape[0]
    step = min(1024, total_rows)
    row, lane, kv_of = places(step)
    matching = lane % kv_heads == kv_of
    left = (limits_ref[0][:1, :1] - head_place * (total_rows // kv_heads)) * kv_heads
    numer = jnp.zeros((many, 2 * width), F32)
    for start in range(0, total_rows, step):
        live = matching & (lane < left - start)
        numer += part(keys_ref[start : start + step, :], values_ref[start : start + step, :], live)

    tail_rows = tail_keys_ref.shape[0] // cont_count
    row, lane, kv_of = places(tail_rows)
    matching = lane % kv_heads == kv_of
    for cont in range(cont_count):
        left = (limits_ref[1 + cont][:1, :1] - head_place * (tail_rows // kv_heads)) * kv_heads
        live = matching & (lane < left) & ((row % count) // new_count == cont)
        start = cont * tail_rows
        numer += part(
            tail_keys_ref[start : start + tail_rows, :],
            tail_values_ref[start : start + tail_rows, :],
            live,
        )

    shape = (own_rows, fresh_keys.shape[0])
    row = lax.broadcasted_iota(jnp.int32, shape, 0)
    lane = lax.broadcasted_iota(jnp.int32, shape, 1)
    live = (
        (lane // count == row // (count * sharing))
        & ((lane % count) // new_count == (row % count) // new_count)
        & (lane % new_count <= row % new_count)
    )
    own_numer = part(fresh_keys.astype(BF16), fresh_values.astype(BF16), live)

    product = final_gain_ref[...] * score_weight_ref[...]
    pieces = [
        p[:, i * LANES : (i + 1) * LANES]
        for p in split_parts(product)
        for i in range(product.shape[1] // LANES)
    ]
    filler = jnp.zeros((own_rows - len(pieces), LANES), F32)
    extra = jnp.concatenate(pieces + [filler], axis=0)
    for slot, out_ref in zip(far_first(slots), out_refs):
        mine = numer[slot * own_rows : (slot + 1) * own_rows, :]
        mine = mine if slot else mine + own_numer
        out_ref[...] = jnp.concatenate([mine, extra], axis=1).astype(BF16)


def mix_body(slots, *refs):
    got_refs = refs[:slots]
    gate_ref, rows_ref, weight_ref, out_ref = refs[slots:]
    own_rows = got_refs[0].shape[0]
    count = rows_ref.shape[0]
    width = LANES
    summed = got_refs[0][:, : 2 * width].astype(F32)
    for slot in range(1, slots):
        summed += got_refs[slot][:, : 2 * width].astype(F32)
    attention = summed[:, :width] / summed[:, width:]
    side_by_side = jnp.concatenate(
        [attention[i : i + count] for i in range(0, own_rows, count)], axis=1
    )
    gated = (side_by_side * jax.nn.sigmoid(gate_ref[...])).astype(BF16)
    mixed = jnp.dot(gated, weight_ref[...], preferred_element_type=F32)
    mixed += rows_ref[...]
    mixed = mixed.astype(BF16)
    places, copies, _, block = out_ref.shape
    for place in range(places):
        piece = mixed[:, place * block : (place + 1) * block]
        for copy in range(copies):
            out_ref[place, copy] = piece


def halves(places):
    middle = max(places // 2, 1)
    return list(range(middle, places, 2)), list(range(0, middle, 2))


def widths(block, sources):
    share = block // sources
    return share, pl.cdiv(share + 2, LANES) * LANES, pl.cdiv(2 * share + 2, LANES) * LANES


def two_parts(value):
    high = value.astype(BF16).astype(F32)
    return [high, value - high]


def padded(pieces, width):
    filled = sum(piece.shape[1] for piece in pieces)
    filler = jnp.zeros((pieces[0].shape[0], width - filled), F32)
    return jnp.concatenate(pieces + [filler], axis=1)


def expand_body(got_ref, gain_ref, gate_ref, up_ref, owners_ref, *refs):
    out_refs, group_of_ref = refs[:-1], refs[-1]
    groups, sources, count, block = got_ref.shape
    for i in range(groups):
        group_of_ref[owners_ref[i]] = i
    order = [flip ^ bit for half in halves(groups) for bit in (1, 0) for flip in half]
    pieces = []
    for slot in order:
        got = got_ref[group_of_ref[lax.axis_index("req") ^ own_flip(slot)]]
        summed = got[0].astype(F32)
        for source in range(1, sources):
            summed += got[source].astype(F32)
        pieces.append(summed)
    attended = jnp.concatenate(pieces, axis=0).astype(BF16).astype(F32)
    scaled = (attended * gain_ref[lax.axis_index("req")]).astype(BF16)
    gate = jnp.dot(scaled, gate_ref[...], preferred_element_type=F32)
    up = jnp.dot(scaled, up_ref[...], preferred_element_type=F32)
    share, extra, _ = widths(block, sources)
    mine = jnp.zeros((attended.shape[0], share), F32)
    for i in range(sources):
        piece = attended[:, i * share : (i + 1) * share]
        mine = jnp.where(lax.axis_index("head") == i, piece, mine)
    squares = jnp.sum(attended * attended, axis=-1, keepdims=True)
    beside = padded([mine] + two_parts(squares), extra)
    wide = jnp.concatenate([gate, up, beside], axis=1)
    start = 0
    for out_ref in out_refs:
        for i in range(out_ref.shape[0]):
            out_ref[i] = wide[start : start + count].astype(out_ref.dtype)
            start += count


def pair_body(sums, share, got_ref, kept_ref, *out_refs):
    odd = (lax.axis_index("req") & own_flip(1)) != 0
    for i, out_ref in enumerate(out_refs):
        got = got_ref[i].astype(F32)
        kept = kept_ref[i]
        added = got + kept
        got, kept = got[:, sums : sums + share], kept[:, sums : sums + share]
        first, second = jnp.where(odd, got, kept), jnp.where(odd, kept, got)
        beside = added[:, sums:]
        squares = beside[:, share : share + 1] + beside[:, share + 1 : share + 2]
        beside = padded([first, second] + two_parts(squares), out_ref.shape[1] - sums)
        out_ref[...] = jnp.concatenate([added[:, :sums], beside], axis=1).astype(out_ref.dtype)


def reduce_body(flips, sources, share, *refs):
    got_refs = refs[: len(flips)]
    weight_ref, out_ref, shares_ref = refs[len(flips) :]
    hidden_units, features = weight_ref.shape
    sums = 2 * hidden_units
    total = got_refs[0][...].astype(F32)
    for got_ref in got_refs[1:]:
        total += got_ref[...].astype(F32)
    for flip, got_ref in zip(flips, got_refs):
        place = lax.axis_index("req") ^ own_flip(flip)
        first = place - (place & own_flip(1))
        beside = got_ref[:, sums:].astype(F32)
        shares_ref[first] = beside[:, :share]
        shares_ref[first + own_flip(1)] = beside[:, share : 2 * share]
    at = sums + 2 * share
    squares = total[:, at : at + 1] + total[:, at + 1 : at + 2]
    scale = lax.rsqrt(squares / features + EPS)
    gate = total[:, :hidden_units] * scale
    up = total[:, hidden_units:sums] * scale
    act = (gate * jax.nn.sigmoid(gate) * up).astype(BF16)
    down = jnp.dot(act, weight_ref[...], preferred_element_type=F32)
    residual = jnp.concatenate(
        [
            jnp.where(lax.axis_index("head") == i, shares_ref[place], 0.0)
            for place in range(shares_ref.shape[0])
            for i in range(sources)
        ],
        axis=1,
    )
    out_ref[...] = (down + residual).astype(BF16)


def finish_body(slots, *refs):
    got_refs, part_refs = refs[:slots], refs[slots : 2 * slots]
    new_ref, score_ref, total_ref, whole_ref, weight_ref = refs[2 * slots :]
    count, features = got_refs[0].shape
    own = new_ref.shape[1]
    pieces = own // LANES
    for slot in range(slots):
        source = partner("head", slot)
        total_ref[source] = got_refs[slot][...].astype(F32)
        extra = part_refs[slot][:, 2 * LANES :].astype(F32)
        for i in range(pieces):
            start = pl.multiple_of(source * own + i * LANES, LANES)
            weight_ref[:, pl.ds(start, LANES)] = (
                extra[i : i + 1]
                + extra[pieces + i : pieces + i + 1]
                + extra[2 * pieces + i : 2 * pieces + i + 1]
            )
    total = total_ref[0]
    for source in range(1, slots):
        total += total_ref[source]
    total = total.astype(BF16).astype(F32)
    whole_ref[...] = total
    start = pl.multiple_of(lax.axis_index("head") * own, LANES)
    new_ref[...] = whole_ref[:, pl.ds(start, own)].astype(BF16)
    weight = weight_ref[...]
    product = jnp.sum(total * weight, axis=-1, keepdims=True)
    squares = jnp.sum(total * total, axis=-1, keepdims=True)
    score = product * lax.rsqrt(squares / features + EPS)
    row = lax.broadcasted_iota(jnp.int32, (count, LANES), 0)
    lane = lax.broadcasted_iota(jnp.int32, (count, LANES), 1)
    flat = jnp.sum(jnp.where(row == lane, score, 0.0), axis=0, keepdims=True)
    score_ref[...] = flat[:, :count]


def shards(
    hidden,
    attn_gain,
    q_weight,
    gate_weight,
    key_value_weight,
    q_gain,
    k_gain,
    out_weight,
    prompt_key_cache,
    prompt_value_cache,
    tail_key_cache,
    tail_value_cache,
    mlp_gain,
    mlp_gate,
    mlp_up,
    mlp_down,
    final_gain,
    score_weight,
    prompt_lengths,
    tail_lengths,
    group_prompt,
):
    head_count = lax.axis_size("head")
    group_count = lax.axis_size("req")
    count = hidden.shape[0]
    features = attn_gain.shape[0]
    width = q_gain.shape[0]
    own_cols = q_weight.shape[1]
    own_heads = own_cols // width
    kv_heads = prompt_key_cache.shape[2]
    cont_count = tail_lengths.shape[1]
    block = features // group_count
    hidden_units = mlp_gate.shape[1]
    smem = whole(pltpu.SMEM)
    facts = (prompt_lengths, tail_lengths.T, group_prompt)

    rows = around([hidden] * head_count, "head")[1:]
    moved = (
        q_weight,
        hidden,
        attn_gain.reshape(1, features),
        q_gain.reshape(1, width),
        k_gain.reshape(1, width),
        final_gain.reshape(1, -1),
        score_weight.reshape(1, -1),
    )
    near_q, own_rows, gain, near_q_gain, near_k_gain, last_gain, last_weight, *rest = call(
        functools.partial(prepare_body, cont_count, count, len(moved)),
        [(x.shape, x.dtype) for x in moved]
        + [((2, count, width), F32), ((1 + cont_count, count, width), jnp.int32)],
        [whole(pl.ANY)] * (len(moved) + 3),
        4,
        "prepare",
        read=2 * sum(x.size for x in moved),
        scratch=[
            pltpu.SMEM(facts[0].shape, jnp.int32),
            pltpu.SMEM(facts[1].shape, jnp.int32),
            pltpu.SMEM(facts[2].shape, jnp.int32),
            pltpu.SemaphoreType.DMA((3,)),
            pltpu.SemaphoreType.DMA((len(moved),)),
        ],
    )(*[in_hbm(x) for x in moved + facts])
    turn, limits = rest
    sent, normed, rows_share = call(
        functools.partial(project_body, head_count),
        [((count, own_cols), BF16), ((count, features), BF16), ((count, features), F32)],
        [whole()] * (head_count + 4),
        4,
        "project",
        flops=2 * count * features * own_cols,
        read=2 * features * own_cols,
        scratch=[pltpu.VMEM((count, features), F32)],
    )(
        own_rows,
        *rows,
        gain,
        near_q,
        near_q_gain,
        turn,
    )
    blocks = key_value_weight.shape[1] // width
    (fresh,) = call(
        fresh_body,
        [((blocks, count, width), BF16)],
        [whole()] * 3 + [whole(pl.ANY)],
        4,
        "fresh",
        flops=2 * count * features * own_cols,
        read=2 * features * own_cols,
        scratch=[pltpu.VMEM(key_value_weight.shape, BF16), pltpu.SemaphoreType.DMA],
    )(normed, near_k_gain, turn, in_hbm(key_value_weight))
    other = swapped(fresh, "head", 1) if blocks % 2 else fresh
    got = around([sent] * head_count, "head")
    (gate,) = call(
        gate_body,
        [((count, own_cols), F32)],
        [whole(), whole(pl.ANY)],
        4,
        "gate",
        flops=2 * count * features * own_cols,
        read=2 * features * own_cols,
        scratch=[pltpu.VMEM(gate_weight.shape, BF16), pltpu.SemaphoreType.DMA],
    )(normed, in_hbm(gate_weight))
    caches = [
        x.reshape(-1, width)
        for x in (prompt_key_cache, prompt_value_cache, tail_key_cache, tail_value_cache)
    ]
    parts = call(
        functools.partial(attend_body, cont_count, kv_heads, head_count),
        [((own_heads * count, 2 * width + LANES), BF16)] * head_count,
        [whole()] * (head_count + 9),
        8,
        "attend",
        flops=1 << 29,
        read=4 * prompt_key_cache.size,
    )(
        *got,
        *[in_vmem(x) for x in caches],
        last_gain,
        last_weight,
        limits,
        fresh,
        other,
    )
    parts = around(parts, "head")
    (mixed,) = call(
        functools.partial(mix_body, head_count),
        [((group_count, head_count, count, block), BF16)],
        [whole()] * (head_count + 3),
        4,
        "mix",
        flops=2 * count * features * own_cols,
        read=2 * features * own_cols,
    )(*reversed_tail(parts), gate, rows_share, in_vmem(out_weight))
    mixed = mixed.reshape(group_count * head_count, count, block)
    mixed = lax.all_to_all(mixed, ("req", "head"), split_axis=0, concat_axis=0, tiled=True)
    mixed = mixed.reshape(group_count, head_count, count, block)
    sums = 2 * hidden_units
    share, extra, pair_extra = widths(block, head_count)
    far, near = halves(group_count)
    pieces = call(
        expand_body,
        [
            ((len(half), count, sums + extra), dtype)
            for half in (far, near)
            for dtype in (BF16, F32)
        ],
        [whole()] * 4 + [smem],
        8,
        "expand",
        flops=4 * count * group_count * block * hidden_units,
        read=4 * block * hidden_units,
        scratch=[pltpu.SMEM((group_count,), jnp.int32)],
    )(
        mixed,
        mlp_gain.reshape(group_count, 1, block),
        in_vmem(mlp_gate),
        in_vmem(mlp_up),
        group_prompt,
    )
    summed = []
    for half, sent, kept in ((far, *pieces[:2]), (near, *pieces[2:])):
        pairs = call(
            functools.partial(pair_body, sums, share),
            [((count, sums + pair_extra), BF16)] * len(half),
            [whole()] * 2,
            4,
            "pair",
            read=4 * sent.size,
        )(crossed(sent, 1), kept)
        for flip, pair in zip(half, pairs):
            summed.append(crossed(pair, flip) if flip else pair)
    (down,) = call(
        functools.partial(reduce_body, far + near, head_count, share),
        [((count, features), BF16)],
        [whole()] * (len(summed) + 1),
        4,
        "reduce",
        flops=2 * count * features * hidden_units,
        read=2 * features * hidden_units,
        scratch=[pltpu.VMEM((group_count, count, share), F32)],
    )(*summed, in_vmem(mlp_down))
    own = features // head_count
    new_hidden, score = call(
        functools.partial(finish_body, head_count),
        [((count, own), BF16), ((1, count), F32)],
        [whole()] * (2 * head_count),
        4,
        "finish",
        outs_vmem=False,
        scratch=[
            pltpu.VMEM((head_count, count, features), F32),
            pltpu.VMEM((count, features), F32),
            pltpu.VMEM((1, features), F32),
        ],
    )(*around([down] * head_count, "head"), *parts)
    return (new_hidden, score.reshape(count))


def solution(mesh):
    return jax.shard_map(
        shards,
        mesh=mesh,
        in_specs=(
            P("req", "head"),
            P(),
            P(None, "head"),
            P(None, "head"),
            P(None, "head"),
            P(),
            P(),
            P("head", None),
            P("req", "head", None, None),
            P("req", "head", None, None),
            P("req", None, "head", None, None),
            P("req", None, "head", None, None),
            P(),
            P("req", "head"),
            P("req", "head"),
            P("head", None),
            P("head"),
            P("head"),
            P(),
            P(),
            P(),
        ),
        out_specs=(P("req", "head"), P("req")),
        check_vma=False,
    )
```

```python
import functools
import math

import jax
import jax.numpy as jnp
from jax import lax
from jax.experimental import pallas as pl
from jax.experimental.pallas import tpu as pltpu
from jax.sharding import PartitionSpec as P

EPS = 1e-06
THETA = 1000000.0
LANES = 128
BF16 = jnp.bfloat16
F32 = jnp.float32


def in_vmem(x):
    return pltpu.with_memory_space_constraint(x, pltpu.VMEM)


def whole(memory_space=pltpu.VMEM):
    return pl.BlockSpec(memory_space=memory_space)


def in_hbm(x):
    return pltpu.with_memory_space_constraint(x, pltpu.HBM)


def swapped(x, axis, flip):
    return lax.ppermute(x, axis, [(i, i ^ flip) for i in range(lax.axis_size(axis))])


def far_first(count):
    return [0] + list(reversed(range(1, count)))


def reversed_tail(pieces):
    return [pieces[0]] + list(reversed(pieces[1:]))


def around(pieces, axis):
    got = [
        swapped(piece, axis, flip) if flip else piece
        for flip, piece in zip(far_first(len(pieces)), pieces)
    ]
    return reversed_tail(got)


def partner(axis, slot):
    return lax.axis_index(axis) ^ slot


def turned(flip):
    return (flip & ~3) | ((flip & 1) << 1) | ((flip >> 1) & 1)


def crossed(x, flip):
    groups, places = lax.axis_size("req"), lax.axis_size("head")
    pairs = [
        (i * places + j, (i ^ (turned(flip) if j % 2 else flip)) * places + j)
        for i in range(groups)
        for j in range(places)
    ]
    return lax.ppermute(x, ("req", "head"), pairs)


def own_flip(flip):
    return jnp.where(lax.axis_index("head") % 2 == 1, turned(flip), flip)


def call(body, outs, specs, limit_mib, name, flops=0, read=0, outs_vmem=True, scratch=()):
    shapes = [
        pltpu.VMEM(shape, dtype) if outs_vmem else jax.ShapeDtypeStruct(shape, dtype)
        for shape, dtype in outs
    ]
    return pl.pallas_call(
        body,
        out_shape=shapes,
        in_specs=specs,
        out_specs=[whole()] * len(outs),
        scratch_shapes=list(scratch),
        compiler_params=pltpu.CompilerParams(vmem_limit_bytes=limit_mib << 20),
        cost_estimate=pl.CostEstimate(flops=flops, bytes_accessed=read, transcendentals=0),
        name=name,
    )


def start_copies(sources, targets, sems):
    moves = [
        pltpu.make_async_copy(source, target, sems.at[i])
        for i, (source, target) in enumerate(zip(sources, targets))
    ]
    for move in moves:
        move.start()
    return moves


def prepare_body(cont_count, count, copies, *refs):
    sources, refs = refs[:copies], refs[copies:]
    facts_hbm, refs = refs[:3], refs[3:]
    targets, refs = refs[:copies], refs[copies:]
    turn_ref, limits_ref, prompts_ref, tails_ref, owners_ref, fact_sems, sems = refs
    facts = start_copies(facts_hbm, (prompts_ref, tails_ref, owners_ref), fact_sems)
    moves = start_copies(sources, targets, sems)
    for fact in facts:
        fact.wait()
    head_width = turn_ref.shape[2]
    new_count = count // cont_count
    prompt = owners_ref[lax.axis_index("req")]
    prompt_len = prompts_ref[prompt]
    row_of = lax.broadcasted_iota(jnp.int32, (count, head_width), 0)
    lane_of = lax.broadcasted_iota(jnp.int32, (count, head_width), 1)
    position = jnp.zeros((count, head_width), jnp.int32)
    limits_ref[0] = jnp.full((count, head_width), prompt_len, jnp.int32)
    for cont in range(cont_count):
        start = prompt_len + tails_ref[cont, prompt]
        limits_ref[1 + cont] = jnp.full((count, head_width), tails_ref[cont, prompt], jnp.int32)
        position = jnp.where(row_of // new_count == cont, start + row_of % new_count, position)
    half = head_width // 2
    frequency = jnp.exp((-math.log(THETA) * 2.0 / head_width) * (lane_of % half).astype(F32))
    angles = position.astype(F32) * frequency
    turn_ref[0] = jnp.cos(angles)
    turn_ref[1] = jnp.where(lane_of < half, -1.0, 1.0) * jnp.sin(angles)
    for move in moves:
        move.wait()


def keyed(block, gain, turn_ref):
    inverse = lax.rsqrt(jnp.mean(block * block, axis=-1, keepdims=True) + EPS)
    block = block * inverse * gain
    return block * turn_ref[0] + pltpu.roll(block, block.shape[1] // 2, 1) * turn_ref[1]


def project_body(slots, *refs):
    slot_refs, refs = refs[:slots], refs[slots:]
    gain_ref, q_ref, q_gain_ref, turn_ref = refs[:4]
    sent_ref, normed_ref, rows_out_ref, rows_ref = refs[4:]
    own = slot_refs[0].shape[1]
    head_width = q_gain_ref.shape[1]
    for slot in range(slots):
        start = pl.multiple_of(partner("head", slot) * own, LANES)
        rows_ref[:, pl.ds(start, own)] = slot_refs[slot][...].astype(F32)
    rows = rows_ref[...]
    rows_out_ref[...] = rows * (1.0 / slots)
    scale = lax.rsqrt(jnp.mean(rows * rows, axis=-1, keepdims=True) + EPS)
    normed = (rows * scale * gain_ref[...]).astype(BF16)
    normed_ref[...] = normed
    queries = jnp.dot(normed, q_ref[...], preferred_element_type=F32)
    heads = [
        keyed(queries[:, start : start + head_width], q_gain_ref[...], turn_ref)
        for start in range(0, q_ref.shape[1], head_width)
    ]
    sent_ref[...] = jnp.concatenate(heads, axis=1).astype(BF16)


def fresh_body(normed_ref, gain_ref, turn_ref, weight_hbm, out_ref, weight_ref, sem):
    move = pltpu.make_async_copy(weight_hbm, weight_ref, sem)
    move.start()
    move.wait()
    projected = jnp.dot(normed_ref[...], weight_ref[...], preferred_element_type=F32)
    blocks, _, head_width = out_ref.shape
    first_block = lax.axis_index("head") * blocks
    for block in range(blocks):
        plain = projected[:, block * head_width : (block + 1) * head_width]
        is_key = (first_block + block) % 2 == 0
        turned = keyed(plain, gain_ref[...], turn_ref)
        out_ref[block] = jnp.where(is_key, turned, plain).astype(BF16)


def gate_body(normed_ref, weight_hbm, gate_ref, weight_ref, sem):
    move = pltpu.make_async_copy(weight_hbm, weight_ref, sem)
    move.start()
    move.wait()
    gate_ref[...] = jnp.dot(normed_ref[...], weight_ref[...], preferred_element_type=F32)


def split_parts(value):
    high = value.astype(BF16).astype(F32)
    middle = (value - high).astype(BF16).astype(F32)
    low = value - high - middle
    return [high, middle, low]


def attend_body(cont_count, kv_heads, slots, *refs):
    slot_refs, refs = refs[:slots], refs[slots:]
    (
        keys_ref,
        values_ref,
        tail_keys_ref,
        tail_values_ref,
        final_gain_ref,
        score_weight_ref,
        limits_ref,
        fresh_ref,
        other_ref,
    ) = refs[:9]
    out_refs = refs[9:]
    count = slot_refs[0].shape[0]
    width = keys_ref.shape[1]
    own_heads = slot_refs[0].shape[1] // width
    own_rows = own_heads * count
    all_heads = own_heads * slots
    sharing = all_heads // kv_heads
    new_count = count // cont_count
    head_place = lax.axis_index("head")
    queries = []
    for slot in range(slots):
        got = slot_refs[slot][...].astype(F32)
        queries += [got[:, i * width : (i + 1) * width] for i in range(own_heads)]
    queries = jnp.concatenate(queries, axis=0).astype(BF16)
    blocks = fresh_ref.shape[0]
    if blocks % 2:
        own, other = fresh_ref[0].astype(F32), other_ref[0].astype(F32)
        even = head_place % 2 == 0
        fresh_keys, fresh_values = jnp.where(even, own, other), jnp.where(even, other, own)
    else:
        pairs = range(0, blocks, 2)
        fresh_keys = jnp.concatenate([fresh_ref[i].astype(F32) for i in pairs], axis=0)
        fresh_values = jnp.concatenate([fresh_ref[i + 1].astype(F32) for i in pairs], axis=0)
    many = all_heads * count
    score_scale = 1.0 / math.sqrt(width)

    def part(keys, values, live):
        rows = queries[: live.shape[0]]
        scores = lax.dot_general(
            rows, keys, (((1,), (1,)), ((), ())), preferred_element_type=F32
        )
        weights = jnp.where(live, jnp.exp(scores * score_scale), 0.0).astype(BF16)
        with_ones = jnp.concatenate([values, jnp.ones(values.shape, BF16)], axis=1)
        return jnp.dot(weights, with_ones, preferred_element_type=F32)

    def places(span):
        row = lax.broadcasted_iota(jnp.int32, (many, span), 0)
        lane = lax.broadcasted_iota(jnp.int32, (many, span), 1)
        place = head_place ^ (row // own_rows)
        head = place * own_heads + (row % own_rows) // count
        return row, lane, head // sharing

    total_rows = keys_ref.shape[0]
    step = min(1024, total_rows)
    row, lane, kv_of = places(step)
    matching = lane % kv_heads == kv_of
    left = (limits_ref[0][:1, :1] - head_place * (total_rows // kv_heads)) * kv_heads
    numer = jnp.zeros((many, 2 * width), F32)
    for start in range(0, total_rows, step):
        live = matching & (lane < left - start)
        numer += part(keys_ref[start : start + step, :], values_ref[start : start + step, :], live)

    tail_rows = tail_keys_ref.shape[0] // cont_count
    row, lane, kv_of = places(tail_rows)
    matching = lane % kv_heads == kv_of
    for cont in range(cont_count):
        left = (limits_ref[1 + cont][:1, :1] - head_place * (tail_rows // kv_heads)) * kv_heads
        live = matching & (lane < left) & ((row % count) // new_count == cont)
        start = cont * tail_rows
        numer += part(
            tail_keys_ref[start : start + tail_rows, :],
            tail_values_ref[start : start + tail_rows, :],
            live,
        )

    shape = (own_rows, fresh_keys.shape[0])
    row = lax.broadcasted_iota(jnp.int32, shape, 0)
    lane = lax.broadcasted_iota(jnp.int32, shape, 1)
    live = (
        (lane // count == row // (count * sharing))
        & ((lane % count) // new_count == (row % count) // new_count)
        & (lane % new_count <= row % new_count)
    )
    own_numer = part(fresh_keys.astype(BF16), fresh_values.astype(BF16), live)

    product = final_gain_ref[...] * score_weight_ref[...]
    pieces = [
        p[:, i * LANES : (i + 1) * LANES]
        for p in split_parts(product)
        for i in range(product.shape[1] // LANES)
    ]
    filler = jnp.zeros((own_rows - len(pieces), LANES), F32)
    extra = jnp.concatenate(pieces + [filler], axis=0)
    for slot, out_ref in zip(far_first(slots), out_refs):
        mine = numer[slot * own_rows : (slot + 1) * own_rows, :]
        mine = mine if slot else mine + own_numer
        out_ref[...] = jnp.concatenate([mine, extra], axis=1).astype(BF16)


def mix_body(slots, *refs):
    got_refs = refs[:slots]
    gate_ref, rows_ref, weight_ref, out_ref = refs[slots:]
    own_rows = got_refs[0].shape[0]
    count = rows_ref.shape[0]
    width = LANES
    summed = got_refs[0][:, : 2 * width].astype(F32)
    for slot in range(1, slots):
        summed += got_refs[slot][:, : 2 * width].astype(F32)
    attention = summed[:, :width] / summed[:, width:]
    side_by_side = jnp.concatenate(
        [attention[i : i + count] for i in range(0, own_rows, count)], axis=1
    )
    gated = (side_by_side * jax.nn.sigmoid(gate_ref[...])).astype(BF16)
    mixed = jnp.dot(gated, weight_ref[...], preferred_element_type=F32)
    mixed += rows_ref[...]
    mixed = mixed.astype(BF16)
    places, copies, _, block = out_ref.shape
    for place in range(places):
        piece = mixed[:, place * block : (place + 1) * block]
        for copy in range(copies):
            out_ref[place, copy] = piece


def halves(places):
    middle = max(places // 2, 1)
    return list(range(middle, places, 2)), list(range(0, middle, 2))


def beside_width(share, count):
    return pl.cdiv(count * share + 2, LANES) * LANES


def two_parts(value):
    high = value.astype(BF16).astype(F32)
    return [high, value - high]


def padded(pieces, width):
    filled = sum(piece.shape[1] for piece in pieces)
    filler = jnp.zeros((pieces[0].shape[0], width - filled), F32)
    return jnp.concatenate(pieces + [filler], axis=1)


def expand_body(got_ref, gain_ref, gate_ref, up_ref, owners_ref, *refs):
    out_refs, group_of_ref = refs[:-1], refs[-1]
    groups, sources, count, block = got_ref.shape
    for i in range(groups):
        group_of_ref[owners_ref[i]] = i
    order = [flip ^ bit for half in halves(groups) for bit in (1, 0) for flip in half]
    pieces = []
    for slot in order:
        got = got_ref[group_of_ref[lax.axis_index("req") ^ own_flip(slot)]]
        summed = got[0].astype(F32)
        for source in range(1, sources):
            summed += got[source].astype(F32)
        pieces.append(summed)
    attended = jnp.concatenate(pieces, axis=0).astype(BF16).astype(F32)
    scaled = (attended * gain_ref[lax.axis_index("req")]).astype(BF16)
    gate = jnp.dot(scaled, gate_ref[...], preferred_element_type=F32)
    up = jnp.dot(scaled, up_ref[...], preferred_element_type=F32)
    share = block // sources
    mine = jnp.zeros((attended.shape[0], share), F32)
    for i in range(sources):
        piece = attended[:, i * share : (i + 1) * share]
        mine = jnp.where(lax.axis_index("head") == i, piece, mine)
    squares = jnp.sum(attended * attended, axis=-1, keepdims=True)
    beside = padded([mine] + two_parts(squares), beside_width(share, 1))
    wide = jnp.concatenate([gate, up, beside], axis=1)
    start = 0
    for out_ref in out_refs:
        for i in range(out_ref.shape[0]):
            out_ref[i] = wide[start : start + count].astype(out_ref.dtype)
            start += count


def combined(sums, share, shares, kept, got):
    added = kept + got
    at = sums + shares * share
    squares = added[:, at : at + 1] + added[:, at + 1 : at + 2]
    beside = [kept[:, sums:at], got[:, sums:at]] + two_parts(squares)
    beside = padded(beside, beside_width(share, 2 * shares))
    return jnp.concatenate([added[:, :sums], beside], axis=1)


def halve_body(sums, share, shares, kept_ref, got_ref, *out_refs):
    for i in range(kept_ref.shape[0]):
        piece = combined(sums, share, shares, kept_ref[i], got_ref[i].astype(F32))
        out_ref = out_refs[i % len(out_refs)]
        out_ref[i // len(out_refs)] = piece.astype(out_ref.dtype)


def reduce_body(share, sources, kept_ref, got_ref, weight_ref, out_ref, shares_ref):
    hidden_units, features = weight_ref.shape
    sums = 2 * hidden_units
    places = shares_ref.shape[0]
    kept, got = kept_ref[0], got_ref[0].astype(F32)
    total = kept + got
    for i in range(places // 2):
        lanes = slice(sums + i * share, sums + (i + 1) * share)
        shares_ref[lax.axis_index("req") ^ own_flip(i)] = kept[:, lanes]
        shares_ref[lax.axis_index("req") ^ own_flip(i + places // 2)] = got[:, lanes]
    at = sums + places // 2 * share
    squares = total[:, at : at + 1] + total[:, at + 1 : at + 2]
    scale = lax.rsqrt(squares / features + EPS)
    gate = total[:, :hidden_units] * scale
    up = total[:, hidden_units:sums] * scale
    act = (gate * jax.nn.sigmoid(gate) * up).astype(BF16)
    down = jnp.dot(act, weight_ref[...], preferred_element_type=F32)
    residual = jnp.concatenate(
        [
            jnp.where(lax.axis_index("head") == i, shares_ref[place], 0.0)
            for place in range(places)
            for i in range(sources)
        ],
        axis=1,
    )
    out_ref[...] = (down + residual).astype(BF16)


def finish_body(slots, *refs):
    got_refs, part_refs = refs[:slots], refs[slots : 2 * slots]
    new_ref, score_ref, total_ref, whole_ref, weight_ref = refs[2 * slots :]
    count, features = got_refs[0].shape
    own = new_ref.shape[1]
    pieces = own // LANES
    for slot in range(slots):
        source = partner("head", slot)
        total_ref[source] = got_refs[slot][...].astype(F32)
        extra = part_refs[slot][:, 2 * LANES :].astype(F32)
        for i in range(pieces):
            start = pl.multiple_of(source * own + i * LANES, LANES)
            weight_ref[:, pl.ds(start, LANES)] = (
                extra[i : i + 1]
                + extra[pieces + i : pieces + i + 1]
                + extra[2 * pieces + i : 2 * pieces + i + 1]
            )
    total = total_ref[0]
    for source in range(1, slots):
        total += total_ref[source]
    total = total.astype(BF16).astype(F32)
    whole_ref[...] = total
    start = pl.multiple_of(lax.axis_index("head") * own, LANES)
    new_ref[...] = whole_ref[:, pl.ds(start, own)].astype(BF16)
    weight = weight_ref[...]
    product = jnp.sum(total * weight, axis=-1, keepdims=True)
    squares = jnp.sum(total * total, axis=-1, keepdims=True)
    score = product * lax.rsqrt(squares / features + EPS)
    row = lax.broadcasted_iota(jnp.int32, (count, LANES), 0)
    lane = lax.broadcasted_iota(jnp.int32, (count, LANES), 1)
    flat = jnp.sum(jnp.where(row == lane, score, 0.0), axis=0, keepdims=True)
    score_ref[...] = flat[:, :count]


def shards(
    hidden,
    attn_gain,
    q_weight,
    gate_weight,
    key_value_weight,
    q_gain,
    k_gain,
    out_weight,
    prompt_key_cache,
    prompt_value_cache,
    tail_key_cache,
    tail_value_cache,
    mlp_gain,
    mlp_gate,
    mlp_up,
    mlp_down,
    final_gain,
    score_weight,
    prompt_lengths,
    tail_lengths,
    group_prompt,
):
    head_count = lax.axis_size("head")
    group_count = lax.axis_size("req")
    count = hidden.shape[0]
    features = attn_gain.shape[0]
    width = q_gain.shape[0]
    own_cols = q_weight.shape[1]
    own_heads = own_cols // width
    kv_heads = prompt_key_cache.shape[2]
    cont_count = tail_lengths.shape[1]
    block = features // group_count
    hidden_units = mlp_gate.shape[1]
    smem = whole(pltpu.SMEM)
    facts = (prompt_lengths, tail_lengths.T, group_prompt)

    rows = around([hidden] * head_count, "head")[1:]
    moved = (
        q_weight,
        hidden,
        attn_gain.reshape(1, features),
        q_gain.reshape(1, width),
        k_gain.reshape(1, width),
        final_gain.reshape(1, -1),
        score_weight.reshape(1, -1),
    )
    near_q, own_rows, gain, near_q_gain, near_k_gain, last_gain, last_weight, *rest = call(
        functools.partial(prepare_body, cont_count, count, len(moved)),
        [(x.shape, x.dtype) for x in moved]
        + [((2, count, width), F32), ((1 + cont_count, count, width), jnp.int32)],
        [whole(pl.ANY)] * (len(moved) + 3),
        4,
        "prepare",
        read=2 * sum(x.size for x in moved),
        scratch=[
            pltpu.SMEM(facts[0].shape, jnp.int32),
            pltpu.SMEM(facts[1].shape, jnp.int32),
            pltpu.SMEM(facts[2].shape, jnp.int32),
            pltpu.SemaphoreType.DMA((3,)),
            pltpu.SemaphoreType.DMA((len(moved),)),
        ],
    )(*[in_hbm(x) for x in moved + facts])
    turn, limits = rest
    sent, normed, rows_share = call(
        functools.partial(project_body, head_count),
        [((count, own_cols), BF16), ((count, features), BF16), ((count, features), F32)],
        [whole()] * (head_count + 4),
        4,
        "project",
        flops=2 * count * features * own_cols,
        read=2 * features * own_cols,
        scratch=[pltpu.VMEM((count, features), F32)],
    )(
        own_rows,
        *rows,
        gain,
        near_q,
        near_q_gain,
        turn,
    )
    blocks = key_value_weight.shape[1] // width
    (fresh,) = call(
        fresh_body,
        [((blocks, count, width), BF16)],
        [whole()] * 3 + [whole(pl.ANY)],
        4,
        "fresh",
        flops=2 * count * features * own_cols,
        read=2 * features * own_cols,
        scratch=[pltpu.VMEM(key_value_weight.shape, BF16), pltpu.SemaphoreType.DMA],
    )(normed, near_k_gain, turn, in_hbm(key_value_weight))
    other = swapped(fresh, "head", 1) if blocks % 2 else fresh
    got = around([sent] * head_count, "head")
    (gate,) = call(
        gate_body,
        [((count, own_cols), F32)],
        [whole(), whole(pl.ANY)],
        4,
        "gate",
        flops=2 * count * features * own_cols,
        read=2 * features * own_cols,
        scratch=[pltpu.VMEM(gate_weight.shape, BF16), pltpu.SemaphoreType.DMA],
    )(normed, in_hbm(gate_weight))
    caches = [
        x.reshape(-1, width)
        for x in (prompt_key_cache, prompt_value_cache, tail_key_cache, tail_value_cache)
    ]
    parts = call(
        functools.partial(attend_body, cont_count, kv_heads, head_count),
        [((own_heads * count, 2 * width + LANES), BF16)] * head_count,
        [whole()] * (head_count + 9),
        8,
        "attend",
        flops=1 << 29,
        read=4 * prompt_key_cache.size,
    )(
        *got,
        *[in_vmem(x) for x in caches],
        last_gain,
        last_weight,
        limits,
        fresh,
        other,
    )
    parts = around(parts, "head")
    (mixed,) = call(
        functools.partial(mix_body, head_count),
        [((group_count, head_count, count, block), BF16)],
        [whole()] * (head_count + 3),
        4,
        "mix",
        flops=2 * count * features * own_cols,
        read=2 * features * own_cols,
    )(*reversed_tail(parts), gate, rows_share, in_vmem(out_weight))
    mixed = mixed.reshape(group_count * head_count, count, block)
    mixed = lax.all_to_all(mixed, ("req", "head"), split_axis=0, concat_axis=0, tiled=True)
    mixed = mixed.reshape(group_count, head_count, count, block)
    sums = 2 * hidden_units
    share = block // head_count
    far, near = halves(group_count)
    pieces = call(
        expand_body,
        [
            ((len(half), count, sums + beside_width(share, 1)), dtype)
            for half in (far, near)
            for dtype in (BF16, F32)
        ],
        [whole()] * 4 + [smem],
        8,
        "expand",
        flops=4 * count * group_count * block * hidden_units,
        read=4 * block * hidden_units,
        scratch=[pltpu.SMEM((group_count,), jnp.int32)],
    )(
        mixed,
        mlp_gain.reshape(group_count, 1, block),
        in_vmem(mlp_gate),
        in_vmem(mlp_up),
        group_prompt,
    )
    ends = []
    for sent, kept, last in ((*pieces[:2], BF16), (*pieces[2:], F32)):
        bit = 1
        while True:
            left, shares = kept.shape[0], 2 * bit
            outs = [(left // 2, F32), (left // 2, BF16)] if left > 1 else [(1, last)]
            results = call(
                functools.partial(halve_body, sums, share, bit),
                [((m, count, sums + beside_width(share, shares)), dtype) for m, dtype in outs],
                [whole()] * 2,
                4,
                "halve",
                read=4 * sent.size,
            )(kept, crossed(sent, bit))
            if left == 1:
                ends.append(results[0])
                break
            kept, sent = results
            bit = shares
    (down,) = call(
        functools.partial(reduce_body, share, head_count),
        [((count, features), BF16)],
        [whole()] * 3,
        4,
        "reduce",
        flops=2 * count * features * hidden_units,
        read=2 * features * hidden_units,
        scratch=[pltpu.VMEM((group_count, count, share), F32)],
    )(ends[1], crossed(ends[0], group_count // 2), in_vmem(mlp_down))
    own = features // head_count
    new_hidden, score = call(
        functools.partial(finish_body, head_count),
        [((count, own), BF16), ((1, count), F32)],
        [whole()] * (2 * head_count),
        4,
        "finish",
        outs_vmem=False,
        scratch=[
            pltpu.VMEM((head_count, count, features), F32),
            pltpu.VMEM((count, features), F32),
            pltpu.VMEM((1, features), F32),
        ],
    )(*around([down] * head_count, "head"), *parts)
    return (new_hidden, score.reshape(count))


def solution(mesh):
    return jax.shard_map(
        shards,
        mesh=mesh,
        in_specs=(
            P("req", "head"),
            P(),
            P(None, "head"),
            P(None, "head"),
            P(None, "head"),
            P(),
            P(),
            P("head", None),
            P("req", "head", None, None),
            P("req", "head", None, None),
            P("req", None, "head", None, None),
            P("req", None, "head", None, None),
            P(),
            P("req", "head"),
            P("req", "head"),
            P("head", None),
            P("head"),
            P("head"),
            P(),
            P(),
            P(),
        ),
        out_specs=(P("req", "head"), P("req")),
        check_vma=False,
    )
```

```python
import functools
import math

import jax
import jax.numpy as jnp
from jax import lax
from jax.experimental import pallas as pl
from jax.experimental.pallas import tpu as pltpu
from jax.sharding import PartitionSpec as P

EPS = 1e-06
THETA = 1000000.0
LANES = 128
BF16 = jnp.bfloat16
F32 = jnp.float32


def in_vmem(x):
    return pltpu.with_memory_space_constraint(x, pltpu.VMEM)


def whole(memory_space=pltpu.VMEM):
    return pl.BlockSpec(memory_space=memory_space)


def in_hbm(x):
    return pltpu.with_memory_space_constraint(x, pltpu.HBM)


def swapped(x, axis, flip):
    return lax.ppermute(x, axis, [(i, i ^ flip) for i in range(lax.axis_size(axis))])


def far_first(count):
    return [0] + list(reversed(range(1, count)))


def reversed_tail(pieces):
    return [pieces[0]] + list(reversed(pieces[1:]))


def around(pieces, axis):
    got = [
        swapped(piece, axis, flip) if flip else piece
        for flip, piece in zip(far_first(len(pieces)), pieces)
    ]
    return reversed_tail(got)


def partner(axis, slot):
    return lax.axis_index(axis) ^ slot


def turned(flip):
    return (flip & ~3) | ((flip & 1) << 1) | ((flip >> 1) & 1)


def crossed(x, flip):
    groups, places = lax.axis_size("req"), lax.axis_size("head")
    pairs = [
        (i * places + j, (i ^ (turned(flip) if j % 2 else flip)) * places + j)
        for i in range(groups)
        for j in range(places)
    ]
    return lax.ppermute(x, ("req", "head"), pairs)


def own_flip(flip):
    return jnp.where(lax.axis_index("head") % 2 == 1, turned(flip), flip)


def call(body, outs, specs, limit_mib, name, flops=0, read=0, outs_vmem=True, scratch=()):
    shapes = [
        pltpu.VMEM(shape, dtype) if outs_vmem else jax.ShapeDtypeStruct(shape, dtype)
        for shape, dtype in outs
    ]
    return pl.pallas_call(
        body,
        out_shape=shapes,
        in_specs=specs,
        out_specs=[whole()] * len(outs),
        scratch_shapes=list(scratch),
        compiler_params=pltpu.CompilerParams(vmem_limit_bytes=limit_mib << 20),
        cost_estimate=pl.CostEstimate(flops=flops, bytes_accessed=read, transcendentals=0),
        name=name,
    )


def start_copies(sources, targets, sems):
    moves = [
        pltpu.make_async_copy(source, target, sems.at[i])
        for i, (source, target) in enumerate(zip(sources, targets))
    ]
    for move in moves:
        move.start()
    return moves


def prepare_body(cont_count, count, copies, *refs):
    sources, refs = refs[:copies], refs[copies:]
    facts_hbm, refs = refs[:3], refs[3:]
    targets, refs = refs[:copies], refs[copies:]
    turn_ref, limits_ref, prompts_ref, tails_ref, owners_ref, fact_sems, sems = refs
    facts = start_copies(facts_hbm, (prompts_ref, tails_ref, owners_ref), fact_sems)
    moves = start_copies(sources, targets, sems)
    for fact in facts:
        fact.wait()
    head_width = turn_ref.shape[2]
    new_count = count // cont_count
    prompt = owners_ref[lax.axis_index("req")]
    prompt_len = prompts_ref[prompt]
    row_of = lax.broadcasted_iota(jnp.int32, (count, head_width), 0)
    lane_of = lax.broadcasted_iota(jnp.int32, (count, head_width), 1)
    position = jnp.zeros((count, head_width), jnp.int32)
    limits_ref[0] = jnp.full((count, head_width), prompt_len, jnp.int32)
    for cont in range(cont_count):
        start = prompt_len + tails_ref[cont, prompt]
        limits_ref[1 + cont] = jnp.full((count, head_width), tails_ref[cont, prompt], jnp.int32)
        position = jnp.where(row_of // new_count == cont, start + row_of % new_count, position)
    half = head_width // 2
    frequency = jnp.exp((-math.log(THETA) * 2.0 / head_width) * (lane_of % half).astype(F32))
    angles = position.astype(F32) * frequency
    turn_ref[0] = jnp.cos(angles)
    turn_ref[1] = jnp.where(lane_of < half, -1.0, 1.0) * jnp.sin(angles)
    for move in moves:
        move.wait()


def keyed(block, gain, turn_ref):
    inverse = lax.rsqrt(jnp.mean(block * block, axis=-1, keepdims=True) + EPS)
    block = block * inverse * gain
    return block * turn_ref[0] + pltpu.roll(block, block.shape[1] // 2, 1) * turn_ref[1]


def project_body(slots, *refs):
    slot_refs, refs = refs[:slots], refs[slots:]
    gain_ref, q_ref, q_gain_ref, turn_ref = refs[:4]
    sent_ref, normed_ref, rows_out_ref, rows_ref = refs[4:]
    own = slot_refs[0].shape[1]
    head_width = q_gain_ref.shape[1]
    for slot in range(slots):
        start = pl.multiple_of(partner("head", slot) * own, LANES)
        rows_ref[:, pl.ds(start, own)] = slot_refs[slot][...].astype(F32)
    rows = rows_ref[...]
    rows_out_ref[...] = rows * (1.0 / slots)
    scale = lax.rsqrt(jnp.mean(rows * rows, axis=-1, keepdims=True) + EPS)
    normed = (rows * scale * gain_ref[...]).astype(BF16)
    normed_ref[...] = normed
    queries = jnp.dot(normed, q_ref[...], preferred_element_type=F32)
    heads = [
        keyed(queries[:, start : start + head_width], q_gain_ref[...], turn_ref)
        for start in range(0, q_ref.shape[1], head_width)
    ]
    sent_ref[...] = jnp.concatenate(heads, axis=1).astype(BF16)


def fresh_body(normed_ref, gain_ref, turn_ref, weight_ref, out_ref):
    projected = jnp.dot(normed_ref[...], weight_ref[...], preferred_element_type=F32)
    blocks, _, head_width = out_ref.shape
    first_block = lax.axis_index("head") * blocks
    for block in range(blocks):
        plain = projected[:, block * head_width : (block + 1) * head_width]
        is_key = (first_block + block) % 2 == 0
        turned = keyed(plain, gain_ref[...], turn_ref)
        out_ref[block] = jnp.where(is_key, turned, plain).astype(BF16)


def gate_body(normed_ref, weight_hbm, gate_ref, weight_ref, sem):
    move = pltpu.make_async_copy(weight_hbm, weight_ref, sem)
    move.start()
    move.wait()
    gate_ref[...] = jnp.dot(normed_ref[...], weight_ref[...], preferred_element_type=F32)


def split_parts(value):
    high = value.astype(BF16).astype(F32)
    middle = (value - high).astype(BF16).astype(F32)
    low = value - high - middle
    return [high, middle, low]


def attend_body(cont_count, kv_heads, slots, *refs):
    slot_refs, refs = refs[:slots], refs[slots:]
    (
        keys_ref,
        values_ref,
        tail_keys_ref,
        tail_values_ref,
        final_gain_ref,
        score_weight_ref,
        limits_ref,
        fresh_ref,
        other_ref,
    ) = refs[:9]
    out_refs = refs[9:]
    count = slot_refs[0].shape[0]
    width = keys_ref.shape[1]
    own_heads = slot_refs[0].shape[1] // width
    own_rows = own_heads * count
    all_heads = own_heads * slots
    sharing = all_heads // kv_heads
    new_count = count // cont_count
    head_place = lax.axis_index("head")
    queries = []
    for slot in range(slots):
        got = slot_refs[slot][...].astype(F32)
        queries += [got[:, i * width : (i + 1) * width] for i in range(own_heads)]
    queries = jnp.concatenate(queries, axis=0).astype(BF16)
    blocks = fresh_ref.shape[0]
    if blocks % 2:
        own, other = fresh_ref[0].astype(F32), other_ref[0].astype(F32)
        even = head_place % 2 == 0
        fresh_keys, fresh_values = jnp.where(even, own, other), jnp.where(even, other, own)
    else:
        pairs = range(0, blocks, 2)
        fresh_keys = jnp.concatenate([fresh_ref[i].astype(F32) for i in pairs], axis=0)
        fresh_values = jnp.concatenate([fresh_ref[i + 1].astype(F32) for i in pairs], axis=0)
    many = all_heads * count
    score_scale = math.log2(math.e) / math.sqrt(width)

    def part(keys, values, live):
        rows = queries[: live.shape[0]]
        scores = lax.dot_general(
            rows, keys, (((1,), (1,)), ((), ())), preferred_element_type=F32
        )
        weights = jnp.where(live, jnp.exp2(scores * score_scale), 0.0).astype(BF16)
        with_ones = jnp.concatenate([values, jnp.ones(values.shape, BF16)], axis=1)
        return jnp.dot(weights, with_ones, preferred_element_type=F32)

    def places(span):
        row = lax.broadcasted_iota(jnp.int32, (many, span), 0)
        lane = lax.broadcasted_iota(jnp.int32, (many, span), 1)
        place = head_place ^ (row // own_rows)
        head = place * own_heads + (row % own_rows) // count
        return row, lane, head // sharing

    total_rows = keys_ref.shape[0]
    step = min(1024, total_rows)
    row, lane, kv_of = places(step)
    matching = lane % kv_heads == kv_of
    left = (limits_ref[0][:1, :1] - head_place * (total_rows // kv_heads)) * kv_heads
    numer = jnp.zeros((many, 2 * width), F32)
    for start in range(0, total_rows, step):
        live = matching & (lane < left - start)
        numer += part(keys_ref[start : start + step, :], values_ref[start : start + step, :], live)

    tail_rows = tail_keys_ref.shape[0] // cont_count
    row, lane, kv_of = places(tail_rows)
    matching = lane % kv_heads == kv_of
    for cont in range(cont_count):
        left = (limits_ref[1 + cont][:1, :1] - head_place * (tail_rows // kv_heads)) * kv_heads
        live = matching & (lane < left) & ((row % count) // new_count == cont)
        start = cont * tail_rows
        numer += part(
            tail_keys_ref[start : start + tail_rows, :],
            tail_values_ref[start : start + tail_rows, :],
            live,
        )

    shape = (own_rows, fresh_keys.shape[0])
    row = lax.broadcasted_iota(jnp.int32, shape, 0)
    lane = lax.broadcasted_iota(jnp.int32, shape, 1)
    live = (
        (lane // count == row // (count * sharing))
        & ((lane % count) // new_count == (row % count) // new_count)
        & (lane % new_count <= row % new_count)
    )
    own_numer = part(fresh_keys.astype(BF16), fresh_values.astype(BF16), live)

    product = final_gain_ref[...] * score_weight_ref[...]
    pieces = [
        p[:, i * LANES : (i + 1) * LANES]
        for p in split_parts(product)
        for i in range(product.shape[1] // LANES)
    ]
    filler = jnp.zeros((own_rows - len(pieces), LANES), F32)
    extra = jnp.concatenate(pieces + [filler], axis=0)
    for slot, out_ref in zip(far_first(slots), out_refs):
        mine = numer[slot * own_rows : (slot + 1) * own_rows, :]
        mine = mine if slot else mine + own_numer
        out_ref[...] = jnp.concatenate([mine, extra], axis=1).astype(BF16)


def mix_body(slots, *refs):
    got_refs = refs[:slots]
    gate_ref, rows_ref, weight_ref, out_ref = refs[slots:]
    own_rows = got_refs[0].shape[0]
    count = rows_ref.shape[0]
    width = LANES
    summed = got_refs[0][:, : 2 * width].astype(F32)
    for slot in range(1, slots):
        summed += got_refs[slot][:, : 2 * width].astype(F32)
    attention = summed[:, :width] / summed[:, width:]
    side_by_side = jnp.concatenate(
        [attention[i : i + count] for i in range(0, own_rows, count)], axis=1
    )
    gated = (side_by_side * jax.nn.sigmoid(gate_ref[...])).astype(BF16)
    mixed = jnp.dot(gated, weight_ref[...], preferred_element_type=F32)
    mixed += rows_ref[...]
    mixed = mixed.astype(BF16)
    places, copies, _, block = out_ref.shape
    for place in range(places):
        piece = mixed[:, place * block : (place + 1) * block]
        for copy in range(copies):
            out_ref[place, copy] = piece


def halves(places):
    middle = max(places // 2, 1)
    return list(range(middle, places, 2)), list(range(0, middle, 2))


def widths(block, sources):
    share = block // sources
    return share, pl.cdiv(share + 2, LANES) * LANES, pl.cdiv(2 * share + 2, LANES) * LANES


def two_parts(value):
    high = value.astype(BF16).astype(F32)
    return [high, value - high]


def padded(pieces, width):
    filled = sum(piece.shape[1] for piece in pieces)
    filler = jnp.zeros((pieces[0].shape[0], width - filled), F32)
    return jnp.concatenate(pieces + [filler], axis=1)


def expand_body(got_ref, gain_ref, gate_ref, up_ref, owners_ref, *refs):
    out_refs, group_of_ref = refs[:-1], refs[-1]
    groups, sources, count, block = got_ref.shape
    for i in range(groups):
        group_of_ref[owners_ref[i]] = i
    order = [flip ^ bit for half in halves(groups) for bit in (1, 0) for flip in half]
    pieces = []
    for slot in order:
        got = got_ref[group_of_ref[lax.axis_index("req") ^ own_flip(slot)]]
        summed = got[0].astype(F32)
        for source in range(1, sources):
            summed += got[source].astype(F32)
        pieces.append(summed)
    attended = jnp.concatenate(pieces, axis=0).astype(BF16).astype(F32)
    scaled = (attended * gain_ref[lax.axis_index("req")]).astype(BF16)
    gate = jnp.dot(scaled, gate_ref[...], preferred_element_type=F32)
    up = jnp.dot(scaled, up_ref[...], preferred_element_type=F32)
    share, extra, _ = widths(block, sources)
    mine = jnp.zeros((attended.shape[0], share), F32)
    for i in range(sources):
        piece = attended[:, i * share : (i + 1) * share]
        mine = jnp.where(lax.axis_index("head") == i, piece, mine)
    squares = jnp.sum(attended * attended, axis=-1, keepdims=True)
    beside = padded([mine] + two_parts(squares), extra)
    wide = jnp.concatenate([gate, up, beside], axis=1)
    start = 0
    for out_ref in out_refs:
        for i in range(out_ref.shape[0]):
            out_ref[i] = wide[start : start + count].astype(out_ref.dtype)
            start += count


def pair_body(sums, share, got_ref, kept_ref, *out_refs):
    odd = (lax.axis_index("req") & own_flip(1)) != 0
    for i, out_ref in enumerate(out_refs):
        got = got_ref[i].astype(F32)
        kept = kept_ref[i]
        added = got + kept
        got, kept = got[:, sums : sums + share], kept[:, sums : sums + share]
        first, second = jnp.where(odd, got, kept), jnp.where(odd, kept, got)
        beside = added[:, sums:]
        squares = beside[:, share : share + 1] + beside[:, share + 1 : share + 2]
        beside = padded([first, second] + two_parts(squares), out_ref.shape[1] - sums)
        out_ref[...] = jnp.concatenate([added[:, :sums], beside], axis=1).astype(out_ref.dtype)


def reduce_body(flips, sources, share, *refs):
    got_refs = refs[: len(flips)]
    weight_ref, out_ref, shares_ref = refs[len(flips) :]
    hidden_units, features = weight_ref.shape
    sums = 2 * hidden_units
    total = got_refs[0][...].astype(F32)
    for got_ref in got_refs[1:]:
        total += got_ref[...].astype(F32)
    for flip, got_ref in zip(flips, got_refs):
        place = lax.axis_index("req") ^ own_flip(flip)
        first = place - (place & own_flip(1))
        beside = got_ref[:, sums:].astype(F32)
        shares_ref[first] = beside[:, :share]
        shares_ref[first + own_flip(1)] = beside[:, share : 2 * share]
    at = sums + 2 * share
    squares = total[:, at : at + 1] + total[:, at + 1 : at + 2]
    scale = lax.rsqrt(squares / features + EPS)
    gate = total[:, :hidden_units] * scale
    up = total[:, hidden_units:sums] * scale
    act = (gate * jax.nn.sigmoid(gate) * up).astype(BF16)
    down = jnp.dot(act, weight_ref[...], preferred_element_type=F32)
    residual = jnp.concatenate(
        [
            jnp.where(lax.axis_index("head") == i, shares_ref[place], 0.0)
            for place in range(shares_ref.shape[0])
            for i in range(sources)
        ],
        axis=1,
    )
    out_ref[...] = (down + residual).astype(BF16)


def finish_body(slots, *refs):
    got_refs, part_refs = refs[:slots], refs[slots : 2 * slots]
    new_ref, score_ref, total_ref, whole_ref, weight_ref = refs[2 * slots :]
    count, features = got_refs[0].shape
    own = new_ref.shape[1]
    pieces = own // LANES
    for slot in range(slots):
        source = partner("head", slot)
        total_ref[source] = got_refs[slot][...].astype(F32)
        extra = part_refs[slot][:, 2 * LANES :].astype(F32)
        for i in range(pieces):
            start = pl.multiple_of(source * own + i * LANES, LANES)
            weight_ref[:, pl.ds(start, LANES)] = (
                extra[i : i + 1]
                + extra[pieces + i : pieces + i + 1]
                + extra[2 * pieces + i : 2 * pieces + i + 1]
            )
    total = total_ref[0]
    for source in range(1, slots):
        total += total_ref[source]
    total = total.astype(BF16).astype(F32)
    whole_ref[...] = total
    start = pl.multiple_of(lax.axis_index("head") * own, LANES)
    new_ref[...] = whole_ref[:, pl.ds(start, own)].astype(BF16)
    weight = weight_ref[...]
    product = jnp.sum(total * weight, axis=-1, keepdims=True)
    squares = jnp.sum(total * total, axis=-1, keepdims=True)
    score = product * lax.rsqrt(squares / features + EPS)
    row = lax.broadcasted_iota(jnp.int32, (count, LANES), 0)
    lane = lax.broadcasted_iota(jnp.int32, (count, LANES), 1)
    flat = jnp.sum(jnp.where(row == lane, score, 0.0), axis=0, keepdims=True)
    score_ref[...] = flat[:, :count]


def shards(
    hidden,
    attn_gain,
    q_weight,
    gate_weight,
    key_value_weight,
    q_gain,
    k_gain,
    out_weight,
    prompt_key_cache,
    prompt_value_cache,
    tail_key_cache,
    tail_value_cache,
    mlp_gain,
    mlp_gate,
    mlp_up,
    mlp_down,
    final_gain,
    score_weight,
    prompt_lengths,
    tail_lengths,
    group_prompt,
):
    head_count = lax.axis_size("head")
    group_count = lax.axis_size("req")
    count = hidden.shape[0]
    features = attn_gain.shape[0]
    width = q_gain.shape[0]
    own_cols = q_weight.shape[1]
    own_heads = own_cols // width
    kv_heads = prompt_key_cache.shape[2]
    cont_count = tail_lengths.shape[1]
    block = features // group_count
    hidden_units = mlp_gate.shape[1]
    smem = whole(pltpu.SMEM)
    facts = (prompt_lengths, tail_lengths.T, group_prompt)

    rows = around([hidden] * head_count, "head")[1:]
    moved = (
        q_weight,
        key_value_weight,
        hidden,
        attn_gain.reshape(1, features),
        q_gain.reshape(1, width),
        k_gain.reshape(1, width),
        final_gain.reshape(1, -1),
        score_weight.reshape(1, -1),
    )
    near_q, near_kv, own_rows, gain, near_q_gain, near_k_gain, last_gain, last_weight, *rest = call(
        functools.partial(prepare_body, cont_count, count, len(moved)),
        [(x.shape, x.dtype) for x in moved]
        + [((2, count, width), F32), ((1 + cont_count, count, width), jnp.int32)],
        [whole(pl.ANY)] * (len(moved) + 3),
        4,
        "prepare",
        read=2 * sum(x.size for x in moved),
        scratch=[
            pltpu.SMEM(facts[0].shape, jnp.int32),
            pltpu.SMEM(facts[1].shape, jnp.int32),
            pltpu.SMEM(facts[2].shape, jnp.int32),
            pltpu.SemaphoreType.DMA((3,)),
            pltpu.SemaphoreType.DMA((len(moved),)),
        ],
    )(*[in_hbm(x) for x in moved + facts])
    turn, limits = rest
    sent, normed, rows_share = call(
        functools.partial(project_body, head_count),
        [((count, own_cols), BF16), ((count, features), BF16), ((count, features), F32)],
        [whole()] * (head_count + 4),
        4,
        "project",
        flops=2 * count * features * own_cols,
        read=2 * features * own_cols,
        scratch=[pltpu.VMEM((count, features), F32)],
    )(
        own_rows,
        *rows,
        gain,
        near_q,
        near_q_gain,
        turn,
    )
    blocks = key_value_weight.shape[1] // width
    (fresh,) = call(
        fresh_body,
        [((blocks, count, width), BF16)],
        [whole()] * 4,
        4,
        "fresh",
        flops=2 * count * features * own_cols,
        read=2 * features * own_cols,
    )(normed, near_k_gain, turn, near_kv)
    other = swapped(fresh, "head", 1) if blocks % 2 else fresh
    got = around([sent] * head_count, "head")
    (gate,) = call(
        gate_body,
        [((count, own_cols), F32)],
        [whole(), whole(pl.ANY)],
        4,
        "gate",
        flops=2 * count * features * own_cols,
        read=2 * features * own_cols,
        scratch=[pltpu.VMEM(gate_weight.shape, BF16), pltpu.SemaphoreType.DMA],
    )(normed, in_hbm(gate_weight))
    caches = [
        x.reshape(-1, width)
        for x in (prompt_key_cache, prompt_value_cache, tail_key_cache, tail_value_cache)
    ]
    parts = call(
        functools.partial(attend_body, cont_count, kv_heads, head_count),
        [((own_heads * count, 2 * width + LANES), BF16)] * head_count,
        [whole()] * (head_count + 9),
        8,
        "attend",
        flops=1 << 29,
        read=4 * prompt_key_cache.size,
    )(
        *got,
        *[in_vmem(x) for x in caches],
        last_gain,
        last_weight,
        limits,
        fresh,
        other,
    )
    parts = around(parts, "head")
    (mixed,) = call(
        functools.partial(mix_body, head_count),
        [((group_count, head_count, count, block), BF16)],
        [whole()] * (head_count + 3),
        4,
        "mix",
        flops=2 * count * features * own_cols,
        read=2 * features * own_cols,
    )(*reversed_tail(parts), gate, rows_share, in_vmem(out_weight))
    mixed = mixed.reshape(group_count * head_count, count, block)
    mixed = lax.all_to_all(mixed, ("req", "head"), split_axis=0, concat_axis=0, tiled=True)
    mixed = mixed.reshape(group_count, head_count, count, block)
    sums = 2 * hidden_units
    share, extra, pair_extra = widths(block, head_count)
    far, near = halves(group_count)
    pieces = call(
        expand_body,
        [
            ((len(half), count, sums + extra), dtype)
            for half in (far, near)
            for dtype in (BF16, F32)
        ],
        [whole()] * 4 + [smem],
        8,
        "expand",
        flops=4 * count * group_count * block * hidden_units,
        read=4 * block * hidden_units,
        scratch=[pltpu.SMEM((group_count,), jnp.int32)],
    )(
        mixed,
        mlp_gain.reshape(group_count, 1, block),
        in_vmem(mlp_gate),
        in_vmem(mlp_up),
        group_prompt,
    )
    summed = []
    for half, sent, kept in ((far, *pieces[:2]), (near, *pieces[2:])):
        pairs = call(
            functools.partial(pair_body, sums, share),
            [((count, sums + pair_extra), BF16)] * len(half),
            [whole()] * 2,
            4,
            "pair",
            read=4 * sent.size,
        )(crossed(sent, 1), kept)
        for flip, pair in zip(half, pairs):
            summed.append(crossed(pair, flip) if flip else pair)
    (down,) = call(
        functools.partial(reduce_body, far + near, head_count, share),
        [((count, features), BF16)],
        [whole()] * (len(summed) + 1),
        4,
        "reduce",
        flops=2 * count * features * hidden_units,
        read=2 * features * hidden_units,
        scratch=[pltpu.VMEM((group_count, count, share), F32)],
    )(*summed, in_vmem(mlp_down))
    own = features // head_count
    new_hidden, score = call(
        functools.partial(finish_body, head_count),
        [((count, own), BF16), ((1, count), F32)],
        [whole()] * (2 * head_count),
        4,
        "finish",
        outs_vmem=False,
        scratch=[
            pltpu.VMEM((head_count, count, features), F32),
            pltpu.VMEM((count, features), F32),
            pltpu.VMEM((1, features), F32),
        ],
    )(*around([down] * head_count, "head"), *parts)
    return (new_hidden, score.reshape(count))


def solution(mesh):
    return jax.shard_map(
        shards,
        mesh=mesh,
        in_specs=(
            P("req", "head"),
            P(),
            P(None, "head"),
            P(None, "head"),
            P(None, "head"),
            P(),
            P(),
            P("head", None),
            P("req", "head", None, None),
            P("req", "head", None, None),
            P("req", None, "head", None, None),
            P("req", None, "head", None, None),
            P(),
            P("req", "head"),
            P("req", "head"),
            P("head", None),
            P("head"),
            P("head"),
            P(),
            P(),
            P(),
        ),
        out_specs=(P("req", "head"), P("req")),
        check_vma=False,
    )
```

```python
import functools
import math

import jax
import jax.numpy as jnp
from jax import lax
from jax.experimental import pallas as pl
from jax.experimental.pallas import tpu as pltpu
from jax.sharding import PartitionSpec as P

EPS = 1e-06
THETA = 1000000.0
LANES = 128
BF16 = jnp.bfloat16
F32 = jnp.float32


def in_vmem(x):
    return pltpu.with_memory_space_constraint(x, pltpu.VMEM)


def whole(memory_space=pltpu.VMEM):
    return pl.BlockSpec(memory_space=memory_space)


def in_hbm(x):
    return pltpu.with_memory_space_constraint(x, pltpu.HBM)


def swapped(x, axis, flip):
    return lax.ppermute(x, axis, [(i, i ^ flip) for i in range(lax.axis_size(axis))])


def far_first(count):
    return [0] + list(reversed(range(1, count)))


def reversed_tail(pieces):
    return [pieces[0]] + list(reversed(pieces[1:]))


def around(pieces, axis):
    got = [
        swapped(piece, axis, flip) if flip else piece
        for flip, piece in zip(far_first(len(pieces)), pieces)
    ]
    return reversed_tail(got)


def partner(axis, slot):
    return lax.axis_index(axis) ^ slot


def turned(flip):
    return (flip & ~3) | ((flip & 1) << 1) | ((flip >> 1) & 1)


def crossed(x, flip):
    groups, places = lax.axis_size("req"), lax.axis_size("head")
    pairs = [
        (i * places + j, (i ^ (turned(flip) if j % 2 else flip)) * places + j)
        for i in range(groups)
        for j in range(places)
    ]
    return lax.ppermute(x, ("req", "head"), pairs)


def own_flip(flip):
    return jnp.where(lax.axis_index("head") % 2 == 1, turned(flip), flip)


def call(body, outs, specs, limit_mib, name, flops=0, read=0, outs_vmem=True, scratch=()):
    shapes = [
        pltpu.VMEM(shape, dtype) if outs_vmem else jax.ShapeDtypeStruct(shape, dtype)
        for shape, dtype in outs
    ]
    return pl.pallas_call(
        body,
        out_shape=shapes,
        in_specs=specs,
        out_specs=[whole()] * len(outs),
        scratch_shapes=list(scratch),
        compiler_params=pltpu.CompilerParams(vmem_limit_bytes=limit_mib << 20),
        cost_estimate=pl.CostEstimate(flops=flops, bytes_accessed=read, transcendentals=0),
        name=name,
    )


def start_copies(sources, targets, sems):
    moves = [
        pltpu.make_async_copy(source, target, sems.at[i])
        for i, (source, target) in enumerate(zip(sources, targets))
    ]
    for move in moves:
        move.start()
    return moves


def prepare_body(cont_count, count, copies, *refs):
    sources, refs = refs[:copies], refs[copies:]
    facts_hbm, refs = refs[:3], refs[3:]
    targets, refs = refs[:copies], refs[copies:]
    turn_ref, limits_ref, prompts_ref, tails_ref, owners_ref, fact_sems, sems = refs
    facts = start_copies(facts_hbm, (prompts_ref, tails_ref, owners_ref), fact_sems)
    moves = start_copies(sources, targets, sems)
    for fact in facts:
        fact.wait()
    head_width = turn_ref.shape[2]
    new_count = count // cont_count
    prompt = owners_ref[lax.axis_index("req")]
    prompt_len = prompts_ref[prompt]
    row_of = lax.broadcasted_iota(jnp.int32, (count, head_width), 0)
    lane_of = lax.broadcasted_iota(jnp.int32, (count, head_width), 1)
    position = jnp.zeros((count, head_width), jnp.int32)
    limits_ref[0] = jnp.full((count, head_width), prompt_len, jnp.int32)
    for cont in range(cont_count):
        start = prompt_len + tails_ref[cont, prompt]
        limits_ref[1 + cont] = jnp.full((count, head_width), tails_ref[cont, prompt], jnp.int32)
        position = jnp.where(row_of // new_count == cont, start + row_of % new_count, position)
    half = head_width // 2
    frequency = jnp.exp((-math.log(THETA) * 2.0 / head_width) * (lane_of % half).astype(F32))
    angles = position.astype(F32) * frequency
    turn_ref[0] = jnp.cos(angles)
    turn_ref[1] = jnp.where(lane_of < half, -1.0, 1.0) * jnp.sin(angles)
    for move in moves:
        move.wait()


def keyed(block, gain, turn_ref):
    inverse = lax.rsqrt(jnp.mean(block * block, axis=-1, keepdims=True) + EPS)
    block = block * inverse * gain
    return block * turn_ref[0] + pltpu.roll(block, block.shape[1] // 2, 1) * turn_ref[1]


def project_body(slots, *refs):
    slot_refs, refs = refs[:slots], refs[slots:]
    gain_ref, q_ref, q_gain_ref, turn_ref = refs[:4]
    sent_ref, normed_ref, rows_out_ref, rows_ref = refs[4:]
    own = slot_refs[0].shape[1]
    head_width = q_gain_ref.shape[1]
    for slot in range(slots):
        start = pl.multiple_of(partner("head", slot) * own, LANES)
        rows_ref[:, pl.ds(start, own)] = slot_refs[slot][...].astype(F32)
    rows = rows_ref[...]
    rows_out_ref[...] = rows * (1.0 / slots)
    scale = lax.rsqrt(jnp.mean(rows * rows, axis=-1, keepdims=True) + EPS)
    normed = (rows * scale * gain_ref[...]).astype(BF16)
    normed_ref[...] = normed
    queries = jnp.dot(normed, q_ref[...], preferred_element_type=F32)
    heads = [
        keyed(queries[:, start : start + head_width], q_gain_ref[...], turn_ref)
        for start in range(0, q_ref.shape[1], head_width)
    ]
    sent_ref[...] = jnp.concatenate(heads, axis=1).astype(BF16)


def fresh_body(normed_ref, gain_ref, turn_ref, weight_ref, out_ref):
    projected = jnp.dot(normed_ref[...], weight_ref[...], preferred_element_type=F32)
    blocks, _, head_width = out_ref.shape
    first_block = lax.axis_index("head") * blocks
    for block in range(blocks):
        plain = projected[:, block * head_width : (block + 1) * head_width]
        is_key = (first_block + block) % 2 == 0
        turned = keyed(plain, gain_ref[...], turn_ref)
        out_ref[block] = jnp.where(is_key, turned, plain).astype(BF16)


def gate_body(normed_ref, weight_hbm, gate_ref, weight_ref, sem):
    move = pltpu.make_async_copy(weight_hbm, weight_ref, sem)
    move.start()
    move.wait()
    gate_ref[...] = jnp.dot(normed_ref[...], weight_ref[...], preferred_element_type=F32)


def split_parts(value):
    high = value.astype(BF16).astype(F32)
    middle = (value - high).astype(BF16).astype(F32)
    low = value - high - middle
    return [high, middle, low]


def attend_body(cont_count, kv_heads, slots, *refs):
    slot_refs, refs = refs[:slots], refs[slots:]
    (
        keys_ref,
        values_ref,
        tail_keys_ref,
        tail_values_ref,
        final_gain_ref,
        score_weight_ref,
        limits_ref,
        fresh_ref,
        other_ref,
    ) = refs[:9]
    out_refs = refs[9:]
    count = slot_refs[0].shape[0]
    width = keys_ref.shape[1]
    own_heads = slot_refs[0].shape[1] // width
    own_rows = own_heads * count
    all_heads = own_heads * slots
    sharing = all_heads // kv_heads
    new_count = count // cont_count
    head_place = lax.axis_index("head")
    queries = []
    for slot in range(slots):
        got = slot_refs[slot][...].astype(F32)
        queries += [got[:, i * width : (i + 1) * width] for i in range(own_heads)]
    queries = jnp.concatenate(queries, axis=0).astype(BF16)
    blocks = fresh_ref.shape[0]
    if blocks % 2:
        own, other = fresh_ref[0].astype(F32), other_ref[0].astype(F32)
        even = head_place % 2 == 0
        fresh_keys, fresh_values = jnp.where(even, own, other), jnp.where(even, other, own)
    else:
        pairs = range(0, blocks, 2)
        fresh_keys = jnp.concatenate([fresh_ref[i].astype(F32) for i in pairs], axis=0)
        fresh_values = jnp.concatenate([fresh_ref[i + 1].astype(F32) for i in pairs], axis=0)
    many = all_heads * count
    score_scale = math.log2(math.e) / math.sqrt(width)

    def part(keys, values, live):
        rows = queries[: live.shape[0]]
        scores = lax.dot_general(
            rows, keys, (((1,), (1,)), ((), ())), preferred_element_type=F32
        )
        weights = jnp.where(live, jnp.exp2(scores * score_scale), 0.0).astype(BF16)
        with_ones = jnp.concatenate([values, jnp.ones(values.shape, BF16)], axis=1)
        return jnp.dot(weights, with_ones, preferred_element_type=F32)

    def places(span):
        row = lax.broadcasted_iota(jnp.int32, (many, span), 0)
        lane = lax.broadcasted_iota(jnp.int32, (many, span), 1)
        place = head_place ^ (row // own_rows)
        head = place * own_heads + (row % own_rows) // count
        return row, lane, head // sharing

    total_rows = keys_ref.shape[0]
    step = min(1024, total_rows)
    row, lane, kv_of = places(step)
    matching = lane % kv_heads == kv_of
    left = (limits_ref[0][:1, :1] - head_place * (total_rows // kv_heads)) * kv_heads
    numer = jnp.zeros((many, 2 * width), F32)
    for start in range(0, total_rows, step):
        live = matching & (lane < left - start)
        numer += part(keys_ref[start : start + step, :], values_ref[start : start + step, :], live)

    tail_rows = tail_keys_ref.shape[0] // cont_count
    row, lane, kv_of = places(tail_rows)
    matching = lane % kv_heads == kv_of
    for cont in range(cont_count):
        left = (limits_ref[1 + cont][:1, :1] - head_place * (tail_rows // kv_heads)) * kv_heads
        live = matching & (lane < left) & ((row % count) // new_count == cont)
        start = cont * tail_rows
        numer += part(
            tail_keys_ref[start : start + tail_rows, :],
            tail_values_ref[start : start + tail_rows, :],
            live,
        )

    shape = (own_rows, fresh_keys.shape[0])
    row = lax.broadcasted_iota(jnp.int32, shape, 0)
    lane = lax.broadcasted_iota(jnp.int32, shape, 1)
    live = (
        (lane // count == row // (count * sharing))
        & ((lane % count) // new_count == (row % count) // new_count)
        & (lane % new_count <= row % new_count)
    )
    own_numer = part(fresh_keys.astype(BF16), fresh_values.astype(BF16), live)

    product = final_gain_ref[...] * score_weight_ref[...]
    pieces = [
        p[:, i * LANES : (i + 1) * LANES]
        for p in split_parts(product)
        for i in range(product.shape[1] // LANES)
    ]
    filler = jnp.zeros((own_rows - len(pieces), LANES), F32)
    extra = jnp.concatenate(pieces + [filler], axis=0)
    for slot, out_ref in zip(far_first(slots), out_refs):
        mine = numer[slot * own_rows : (slot + 1) * own_rows, :]
        mine = mine if slot else mine + own_numer
        out_ref[...] = jnp.concatenate([mine, extra], axis=1).astype(BF16)


def mix_body(slots, *refs):
    got_refs = refs[:slots]
    gate_ref, rows_ref, weight_ref, out_ref = refs[slots:]
    own_rows = got_refs[0].shape[0]
    count = rows_ref.shape[0]
    width = LANES
    summed = got_refs[0][:, : 2 * width].astype(F32)
    for slot in range(1, slots):
        summed += got_refs[slot][:, : 2 * width].astype(F32)
    attention = summed[:, :width] / summed[:, width:]
    side_by_side = jnp.concatenate(
        [attention[i : i + count] for i in range(0, own_rows, count)], axis=1
    )
    gated = (side_by_side * jax.nn.sigmoid(gate_ref[...])).astype(BF16)
    mixed = jnp.dot(gated, weight_ref[...], preferred_element_type=F32)
    mixed += rows_ref[...]
    mixed = mixed.astype(BF16)
    places, copies, _, block = out_ref.shape
    for place in range(places):
        piece = mixed[:, place * block : (place + 1) * block]
        for copy in range(copies):
            out_ref[place, copy] = piece


def halves(places):
    middle = max(places // 2, 1)
    return list(reversed(range(middle, places, 2))), list(range(0, middle, 2))


def widths(block, sources):
    share = block // sources
    return share, pl.cdiv(share + 2, LANES) * LANES, pl.cdiv(2 * share + 2, LANES) * LANES


def two_parts(value):
    high = value.astype(BF16).astype(F32)
    return [high, value - high]


def padded(pieces, width):
    filled = sum(piece.shape[1] for piece in pieces)
    filler = jnp.zeros((pieces[0].shape[0], width - filled), F32)
    return jnp.concatenate(pieces + [filler], axis=1)


def expand_body(got_ref, gain_ref, gate_ref, up_ref, owners_ref, *refs):
    out_refs, group_of_ref = refs[:-1], refs[-1]
    groups, sources, count, block = got_ref.shape
    for i in range(groups):
        group_of_ref[owners_ref[i]] = i
    order = [flip ^ bit for half in halves(groups) for bit in (1, 0) for flip in half]
    pieces = []
    for slot in order:
        got = got_ref[group_of_ref[lax.axis_index("req") ^ own_flip(slot)]]
        summed = got[0].astype(F32)
        for source in range(1, sources):
            summed += got[source].astype(F32)
        pieces.append(summed)
    attended = jnp.concatenate(pieces, axis=0).astype(BF16).astype(F32)
    scaled = (attended * gain_ref[lax.axis_index("req")]).astype(BF16)
    gate = jnp.dot(scaled, gate_ref[...], preferred_element_type=F32)
    up = jnp.dot(scaled, up_ref[...], preferred_element_type=F32)
    share, extra, _ = widths(block, sources)
    mine = jnp.zeros((attended.shape[0], share), F32)
    for i in range(sources):
        piece = attended[:, i * share : (i + 1) * share]
        mine = jnp.where(lax.axis_index("head") == i, piece, mine)
    squares = jnp.sum(attended * attended, axis=-1, keepdims=True)
    beside = padded([mine] + two_parts(squares), extra)
    wide = jnp.concatenate([gate, up, beside], axis=1)
    start = 0
    for out_ref in out_refs:
        for i in range(out_ref.shape[0]):
            out_ref[i] = wide[start : start + count].astype(out_ref.dtype)
            start += count


def pair_body(sums, share, got_ref, kept_ref, *out_refs):
    odd = (lax.axis_index("req") & own_flip(1)) != 0
    for i, out_ref in enumerate(out_refs):
        got = got_ref[i].astype(F32)
        kept = kept_ref[i]
        added = got + kept
        got, kept = got[:, sums : sums + share], kept[:, sums : sums + share]
        first, second = jnp.where(odd, got, kept), jnp.where(odd, kept, got)
        beside = added[:, sums:]
        squares = beside[:, share : share + 1] + beside[:, share + 1 : share + 2]
        beside = padded([first, second] + two_parts(squares), out_ref.shape[1] - sums)
        out_ref[...] = jnp.concatenate([added[:, :sums], beside], axis=1).astype(out_ref.dtype)


def reduce_body(flips, sources, share, *refs):
    got_refs = refs[: len(flips)]
    weight_ref, out_ref, shares_ref = refs[len(flips) :]
    hidden_units, features = weight_ref.shape
    sums = 2 * hidden_units
    total = got_refs[0][...].astype(F32)
    for got_ref in got_refs[1:]:
        total += got_ref[...].astype(F32)
    for flip, got_ref in zip(flips, got_refs):
        place = lax.axis_index("req") ^ own_flip(flip)
        first = place - (place & own_flip(1))
        beside = got_ref[:, sums:].astype(F32)
        shares_ref[first] = beside[:, :share]
        shares_ref[first + own_flip(1)] = beside[:, share : 2 * share]
    at = sums + 2 * share
    squares = total[:, at : at + 1] + total[:, at + 1 : at + 2]
    scale = lax.rsqrt(squares / features + EPS)
    gate = total[:, :hidden_units] * scale
    up = total[:, hidden_units:sums] * scale
    act = (gate * jax.nn.sigmoid(gate) * up).astype(BF16)
    down = jnp.dot(act, weight_ref[...], preferred_element_type=F32)
    residual = jnp.concatenate(
        [
            jnp.where(lax.axis_index("head") == i, shares_ref[place], 0.0)
            for place in range(shares_ref.shape[0])
            for i in range(sources)
        ],
        axis=1,
    )
    out_ref[...] = (down + residual).astype(BF16)


def finish_body(slots, *refs):
    got_refs, part_refs = refs[:slots], refs[slots : 2 * slots]
    new_ref, score_ref, total_ref, whole_ref, weight_ref = refs[2 * slots :]
    count, features = got_refs[0].shape
    own = new_ref.shape[1]
    pieces = own // LANES
    for slot in range(slots):
        source = partner("head", slot)
        total_ref[source] = got_refs[slot][...].astype(F32)
        extra = part_refs[slot][:, 2 * LANES :].astype(F32)
        for i in range(pieces):
            start = pl.multiple_of(source * own + i * LANES, LANES)
            weight_ref[:, pl.ds(start, LANES)] = (
                extra[i : i + 1]
                + extra[pieces + i : pieces + i + 1]
                + extra[2 * pieces + i : 2 * pieces + i + 1]
            )
    total = total_ref[0]
    for source in range(1, slots):
        total += total_ref[source]
    total = total.astype(BF16).astype(F32)
    whole_ref[...] = total
    start = pl.multiple_of(lax.axis_index("head") * own, LANES)
    new_ref[...] = whole_ref[:, pl.ds(start, own)].astype(BF16)
    weight = weight_ref[...]
    product = jnp.sum(total * weight, axis=-1, keepdims=True)
    squares = jnp.sum(total * total, axis=-1, keepdims=True)
    score = product * lax.rsqrt(squares / features + EPS)
    row = lax.broadcasted_iota(jnp.int32, (count, LANES), 0)
    lane = lax.broadcasted_iota(jnp.int32, (count, LANES), 1)
    flat = jnp.sum(jnp.where(row == lane, score, 0.0), axis=0, keepdims=True)
    score_ref[...] = flat[:, :count]


def shards(
    hidden,
    attn_gain,
    q_weight,
    gate_weight,
    key_value_weight,
    q_gain,
    k_gain,
    out_weight,
    prompt_key_cache,
    prompt_value_cache,
    tail_key_cache,
    tail_value_cache,
    mlp_gain,
    mlp_gate,
    mlp_up,
    mlp_down,
    final_gain,
    score_weight,
    prompt_lengths,
    tail_lengths,
    group_prompt,
):
    head_count = lax.axis_size("head")
    group_count = lax.axis_size("req")
    count = hidden.shape[0]
    features = attn_gain.shape[0]
    width = q_gain.shape[0]
    own_cols = q_weight.shape[1]
    own_heads = own_cols // width
    kv_heads = prompt_key_cache.shape[2]
    cont_count = tail_lengths.shape[1]
    block = features // group_count
    hidden_units = mlp_gate.shape[1]
    smem = whole(pltpu.SMEM)
    facts = (prompt_lengths, tail_lengths.T, group_prompt)

    rows = around([hidden] * head_count, "head")[1:]
    moved = (
        q_weight,
        key_value_weight,
        hidden,
        attn_gain.reshape(1, features),
        q_gain.reshape(1, width),
        k_gain.reshape(1, width),
        final_gain.reshape(1, -1),
        score_weight.reshape(1, -1),
    )
    near_q, near_kv, own_rows, gain, near_q_gain, near_k_gain, last_gain, last_weight, *rest = call(
        functools.partial(prepare_body, cont_count, count, len(moved)),
        [(x.shape, x.dtype) for x in moved]
        + [((2, count, width), F32), ((1 + cont_count, count, width), jnp.int32)],
        [whole(pl.ANY)] * (len(moved) + 3),
        4,
        "prepare",
        read=2 * sum(x.size for x in moved),
        scratch=[
            pltpu.SMEM(facts[0].shape, jnp.int32),
            pltpu.SMEM(facts[1].shape, jnp.int32),
            pltpu.SMEM(facts[2].shape, jnp.int32),
            pltpu.SemaphoreType.DMA((3,)),
            pltpu.SemaphoreType.DMA((len(moved),)),
        ],
    )(*[in_hbm(x) for x in moved + facts])
    turn, limits = rest
    sent, normed, rows_share = call(
        functools.partial(project_body, head_count),
        [((count, own_cols), BF16), ((count, features), BF16), ((count, features), F32)],
        [whole()] * (head_count + 4),
        4,
        "project",
        flops=2 * count * features * own_cols,
        read=2 * features * own_cols,
        scratch=[pltpu.VMEM((count, features), F32)],
    )(
        own_rows,
        *rows,
        gain,
        near_q,
        near_q_gain,
        turn,
    )
    blocks = key_value_weight.shape[1] // width
    (fresh,) = call(
        fresh_body,
        [((blocks, count, width), BF16)],
        [whole()] * 4,
        4,
        "fresh",
        flops=2 * count * features * own_cols,
        read=2 * features * own_cols,
    )(normed, near_k_gain, turn, near_kv)
    other = swapped(fresh, "head", 1) if blocks % 2 else fresh
    got = around([sent] * head_count, "head")
    (gate,) = call(
        gate_body,
        [((count, own_cols), F32)],
        [whole(), whole(pl.ANY)],
        4,
        "gate",
        flops=2 * count * features * own_cols,
        read=2 * features * own_cols,
        scratch=[pltpu.VMEM(gate_weight.shape, BF16), pltpu.SemaphoreType.DMA],
    )(normed, in_hbm(gate_weight))
    caches = [
        x.reshape(-1, width)
        for x in (prompt_key_cache, prompt_value_cache, tail_key_cache, tail_value_cache)
    ]
    parts = call(
        functools.partial(attend_body, cont_count, kv_heads, head_count),
        [((own_heads * count, 2 * width + LANES), BF16)] * head_count,
        [whole()] * (head_count + 9),
        8,
        "attend",
        flops=1 << 29,
        read=4 * prompt_key_cache.size,
    )(
        *got,
        *[in_vmem(x) for x in caches],
        last_gain,
        last_weight,
        limits,
        fresh,
        other,
    )
    parts = around(parts, "head")
    (mixed,) = call(
        functools.partial(mix_body, head_count),
        [((group_count, head_count, count, block), BF16)],
        [whole()] * (head_count + 3),
        4,
        "mix",
        flops=2 * count * features * own_cols,
        read=2 * features * own_cols,
    )(*reversed_tail(parts), gate, rows_share, in_vmem(out_weight))
    mixed = mixed.reshape(group_count * head_count, count, block)
    mixed = lax.all_to_all(mixed, ("req", "head"), split_axis=0, concat_axis=0, tiled=True)
    mixed = mixed.reshape(group_count, head_count, count, block)
    sums = 2 * hidden_units
    share, extra, pair_extra = widths(block, head_count)
    far, near = halves(group_count)
    pieces = call(
        expand_body,
        [
            ((len(half), count, sums + extra), dtype)
            for half in (far, near)
            for dtype in (BF16, F32)
        ],
        [whole()] * 4 + [smem],
        8,
        "expand",
        flops=4 * count * group_count * block * hidden_units,
        read=4 * block * hidden_units,
        scratch=[pltpu.SMEM((group_count,), jnp.int32)],
    )(
        mixed,
        mlp_gain.reshape(group_count, 1, block),
        in_vmem(mlp_gate),
        in_vmem(mlp_up),
        group_prompt,
    )
    summed = []
    for half, sent, kept in ((far, *pieces[:2]), (near, *pieces[2:])):
        pairs = call(
            functools.partial(pair_body, sums, share),
            [((count, sums + pair_extra), BF16)] * len(half),
            [whole()] * 2,
            4,
            "pair",
            read=4 * sent.size,
        )(crossed(sent, 1), kept)
        for flip, pair in zip(half, pairs):
            summed.append(crossed(pair, flip) if flip else pair)
    (down,) = call(
        functools.partial(reduce_body, far + near, head_count, share),
        [((count, features), BF16)],
        [whole()] * (len(summed) + 1),
        4,
        "reduce",
        flops=2 * count * features * hidden_units,
        read=2 * features * hidden_units,
        scratch=[pltpu.VMEM((group_count, count, share), F32)],
    )(*summed, in_vmem(mlp_down))
    own = features // head_count
    new_hidden, score = call(
        functools.partial(finish_body, head_count),
        [((count, own), BF16), ((1, count), F32)],
        [whole()] * (2 * head_count),
        4,
        "finish",
        outs_vmem=False,
        scratch=[
            pltpu.VMEM((head_count, count, features), F32),
            pltpu.VMEM((count, features), F32),
            pltpu.VMEM((1, features), F32),
        ],
    )(*around([down] * head_count, "head"), *parts)
    return (new_hidden, score.reshape(count))


def solution(mesh):
    return jax.shard_map(
        shards,
        mesh=mesh,
        in_specs=(
            P("req", "head"),
            P(),
            P(None, "head"),
            P(None, "head"),
            P(None, "head"),
            P(),
            P(),
            P("head", None),
            P("req", "head", None, None),
            P("req", "head", None, None),
            P("req", None, "head", None, None),
            P("req", None, "head", None, None),
            P(),
            P("req", "head"),
            P("req", "head"),
            P("head", None),
            P("head"),
            P("head"),
            P(),
            P(),
            P(),
        ),
        out_specs=(P("req", "head"), P("req")),
        check_vma=False,
    )
```
